32 devices in a mesh: dp: 8 (over z, x), seq: 4 (over y, core).
Axes of the slice: x: 2, y: 2, z: 4, core: 2. Of those that a mesh axis runs over, the one named last changes fastest.
Arguments:
- hidden: bfloat16 [8, 512, 5120], P('dp', 'seq'), may hold values from -6 to 6
- queries: bfloat16 [8, 512, 2560], P('dp', 'seq'), may hold values from -9 to 9
- keys: bfloat16 [8, 512, 512], P('dp', 'seq'), may hold values from -9 to 9
- value_weight: bfloat16 [5120, 512], P('dp'), may hold values from -0.078125 to 0.078125
- doc_ids: int32 [8, 512], P('dp', 'seq'), may hold values from 0 to 3, never falling along the last dimension, each value on 1 to 256 neighbouring positions
- cotangent: bfloat16 [8, 512, 2560], P('dp', 'seq'), may hold values from -6 to 6
Outputs:
- attn_out: bfloat16 [8, 512, 2560], P('dp', 'seq')
- grad_queries: bfloat16 [8, 512, 2560], P('dp', 'seq')
- grad_keys: bfloat16 [8, 512, 512], P('dp', 'seq')
- grad_hidden: bfloat16 [8, 512, 5120], P('dp', 'seq')
- grad_weight: float32 [5120, 512], P('dp')
The draws below stay inside these ranges and needn't reach their ends.
Inputs may be any that keep to these rules, and one draw needn't show every extreme that they name: `doc_ids`: document numbers never fall along a span; one document has exactly 256 tokens, none more.
All inputs are finite; a program needn't handle non-finite values.
Results may differ from the reference program's by a relative error of at most 0.025.
Values may be sent and summed in bfloat16 or wider, within the bound.
No kernel may reach another device: no remote copies, remote signals or barrier semaphores. Data moves between devices by JAX's collectives and lax.ppermute only.
A program may use at most 128 MiB of HBM per device.

```python
import math
import jax
import jax.numpy as jnp
import numpy as np
from jax import lax

D = 5120
QUERY_HEADS = 20
KEY_VALUE_HEADS = 4
HEAD_SIZE = 128
TOKENS_PER_SLOT = 128
QUERY_PER_KV = 5
KW = 512
QW = 2560
SPAN_TOKENS = 512
SPAN_COUNT = 8
N_SEQ = 4


def shift_back(source, shifted_by):
    padding = jnp.zeros_like(source[:, :shifted_by])
    return jnp.concatenate((source[:, shifted_by:], padding), axis=1)


def planted_pair(key):
    base_key = jax.random.fold_in(key, 5171)
    flow_list = jax.random.split(base_key, 7)
    query_layout = (SPAN_COUNT, SPAN_TOKENS, KEY_VALUE_HEADS, QUERY_PER_KV, HEAD_SIZE)
    key_layout = (SPAN_COUNT, SPAN_TOKENS, KEY_VALUE_HEADS, HEAD_SIZE)
    query_base = 1.5 * jnp.clip(jax.random.normal(flow_list[0], query_layout, jnp.float32), -6.0, 6.0)
    key_base = 1.5 * jnp.clip(jax.random.normal(flow_list[1], key_layout, jnp.float32), -6.0, 6.0)
    stride = max(SPAN_TOKENS // 4, 2)
    block_list = SPAN_TOKENS // stride
    offsets = jax.random.randint(flow_list[2], (SPAN_COUNT, block_list), 1, stride)
    picked_rows = jax.random.randint(flow_list[3], (SPAN_COUNT, block_list), 0, KEY_VALUE_HEADS)
    position = jnp.arange(SPAN_TOKENS, dtype=jnp.int32)
    block_lookup = jnp.minimum(position // stride, block_list - 1)
    flagged_rows = (position[None, :] % stride == offsets[:, block_lookup]) & (position[None, :] // stride < block_list) & (position[None, :] > TOKENS_PER_SLOT)
    head_marker = flagged_rows[:, :, None] & (picked_rows[:, block_lookup][:, :, None] == jnp.arange(KEY_VALUE_HEADS, dtype=jnp.int32)[None, None, :])
    sign_table = jax.random.rademacher(flow_list[4], key_layout, jnp.float32)
    signal_strength = jax.random.uniform(flow_list[5], (SPAN_COUNT, SPAN_TOKENS, KEY_VALUE_HEADS, QUERY_PER_KV, 1), jnp.float32, 0.4, 1.0)
    score_margin = jax.random.uniform(flow_list[6], (SPAN_COUNT, SPAN_TOKENS, KEY_VALUE_HEADS, 1), jnp.float32, 2.5, 3.0)
    magnitude = math.sqrt(300.0) * HEAD_SIZE ** (-0.25)
    queries = jnp.where(head_marker[..., None, None], signal_strength * magnitude * sign_table[:, :, :, None, :], query_base)
    main_mark = shift_back(head_marker, TOKENS_PER_SLOT)
    second_mark = shift_back(head_marker, TOKENS_PER_SLOT + 1)
    main_keys = magnitude * shift_back(sign_table, TOKENS_PER_SLOT)
    second_keys = magnitude * (1.0 - shift_back(score_margin, TOKENS_PER_SLOT + 1) / 300.0) * shift_back(sign_table, TOKENS_PER_SLOT + 1)
    keys = jnp.where(main_mark[..., None], main_keys, jnp.where(second_mark[..., None], second_keys, key_base))
    return (queries.reshape(SPAN_COUNT, SPAN_TOKENS, QUERY_HEADS * HEAD_SIZE), keys.reshape(SPAN_COUNT, SPAN_TOKENS, KEY_VALUE_HEADS * HEAD_SIZE))


def draw_queries(key, part):
    return planted_pair(key)[0].astype(jnp.bfloat16)


def draw_keys(key, part):
    return planted_pair(key)[1].astype(jnp.bfloat16)


def with_spikes(values, rng, source, target, blocks, factor):
    owner, partner = [(jnp.arange(values.shape[axis_at]) // (values.shape[axis_at] // blocks)).reshape([-1 if axis == axis_at else 1 for axis in range(values.ndim)]) for axis_at in (source, target)]
    chosen = jax.random.permutation(rng, blocks)[partner]
    strong = (owner == chosen) | (owner == (partner + blocks // 2) % blocks)
    return jnp.where(strong, factor * values, values)


def steps_of(stream_key, shape, cuts, smallest, top_value):
    def one(dim, shards_of):
        steps = jax.random.uniform(jax.random.fold_in(jax.random.fold_in(stream_key, 6), dim), (shards_of,), jnp.float32, smallest / len(cuts), top_value / len(cuts))
        return jnp.repeat(jnp.exp(steps), shape[dim] // shards_of).reshape((-1,) + (1,) * (len(shape) - dim - 1))

    gain = one(*cuts[0])
    for cut in cuts[1:]:
        gain = gain * one(*cut)
    return gain


def length_profile(count, total, limit, lean):
    weights = [(1 << 20) // math.isqrt(standing ** lean) + 1 for standing in range(2, count + 1)]
    surplus, given = total - limit - (count - 1), [1] * (count - 1)
    while surplus > 0:
        movable = [i for i in range(count - 1) if given[i] < limit]
        pool, remaining = sum([weights[i] for i in movable]), surplus
        for i in movable:
            addition = min(limit - given[i], max(1, remaining * weights[i] // pool), surplus)
            given[i] = given[i] + addition
            surplus = surplus - addition
    return np.array([limit] + given)


def uneven(own_key, count, total, most, skew):
    if count == 2:
        one = jax.random.randint(own_key, (), max(1, total - most), min(most, total - 1) + 1)
        return jnp.stack([one, total - one])
    sizes = jnp.asarray(length_profile(count, total, most, skew), jnp.int32)
    couples = (count - 1) // 2
    giver, taker = sizes[1:1 + 2 * couples:2], sizes[2:2 + 2 * couples:2]
    room = jnp.minimum(giver - 1, most - taker)
    moved = jax.random.randint(jax.random.fold_in(own_key, 1), (couples,), 0, 1 << 20) % (room + 1)
    sizes = sizes.at[1:1 + 2 * couples:2].set(giver - moved).at[2:2 + 2 * couples:2].set(taker + moved)
    return sizes[jax.random.permutation(jax.random.fold_in(own_key, 2), count)]


def noise(key, shape, scale, reach, cuts=(), kind=jnp.bfloat16):
    values = jax.random.normal(key, shape, jnp.float32) * scale
    if len(cuts) > 0:
        values = steps_of(key, shape, cuts, -0.22, 0.18) * values
    return jnp.clip(values, min=-reach, max=reach).astype(kind)


def heavy_noise(own_key, extent, scale, bound, pieces, heavy, held_as=jnp.bfloat16):
    values = scale * jax.random.normal(own_key, extent, jnp.float32)
    if pieces:
        values = values * steps_of(own_key, extent, pieces, -0.22, 0.18)
    return jnp.clip(with_spikes(values, jax.random.fold_in(own_key, 3), *heavy), -bound, bound).astype(held_as)


def setup_inputs(seed: int = 0) -> dict:
    key_list = jax.random.split(jax.random.key(seed), 7)
    hidden = heavy_noise(key_list[0], (SPAN_COUNT, SPAN_TOKENS, D), 1.0, 6.0, ((0, 8), (1, 4)), (0, 2, 8, 2.0))
    queries = draw_queries(jax.random.fold_in(key_list[6], 71), 0)
    keys = draw_keys(jax.random.fold_in(key_list[6], 71), 0)
    value_weight = noise(key_list[3], (D, KW), D ** -0.5, 0.078125, ((0, 8),))
    doc_ids = jax.vmap(lambda own: jnp.searchsorted(jnp.cumsum(uneven(own, 4, SPAN_TOKENS, SPAN_TOKENS // 2, 2)), jnp.arange(SPAN_TOKENS), side="right"))(jax.random.split(key_list[4], SPAN_COUNT)).reshape((SPAN_COUNT, SPAN_TOKENS)).astype(jnp.int32)
    cotangent = noise(key_list[5], (SPAN_COUNT, SPAN_TOKENS, QW), 1.0, 6.0, ((0, 8), (1, 4)))
    return {"hidden": hidden, "queries": queries, "keys": keys, "value_weight": value_weight, "doc_ids": doc_ids, "cotangent": cotangent}


def attend_span(operands):
    query_gathered, key_gathered, value_gathered, doc, gradient_total = operands
    scale = HEAD_SIZE ** -0.5

    def key_slices(key_tile):
        start_offset = (key_tile * TOKENS_PER_SLOT).astype(jnp.int32)
        key_head_rows = lax.dynamic_slice_in_dim(key_gathered, start_offset, TOKENS_PER_SLOT, 0).reshape(TOKENS_PER_SLOT, KEY_VALUE_HEADS, HEAD_SIZE).astype(jnp.float32)
        value_head_rows = lax.dynamic_slice_in_dim(value_gathered, start_offset, TOKENS_PER_SLOT, 0).reshape(TOKENS_PER_SLOT, KEY_VALUE_HEADS, HEAD_SIZE).astype(jnp.float32)
        key_doc = lax.dynamic_slice_in_dim(doc, start_offset, TOKENS_PER_SLOT, 0)
        key_pos = start_offset + jnp.arange(TOKENS_PER_SLOT, dtype=jnp.int32)
        return start_offset, key_head_rows, value_head_rows, key_doc, key_pos

    def query_step(carry, query_block):
        key_gradient_sum, value_gradient_sum = carry
        query_offset = (query_block * TOKENS_PER_SLOT).astype(jnp.int32)
        query_head_rows = lax.dynamic_slice_in_dim(query_gathered, query_offset, TOKENS_PER_SLOT, 0).reshape(TOKENS_PER_SLOT, KEY_VALUE_HEADS, QUERY_PER_KV, HEAD_SIZE).astype(jnp.float32)
        gradient_heads = lax.dynamic_slice_in_dim(gradient_total, query_offset, TOKENS_PER_SLOT, 0).reshape(TOKENS_PER_SLOT, KEY_VALUE_HEADS, QUERY_PER_KV, HEAD_SIZE).astype(jnp.float32)
        query_doc = lax.dynamic_slice_in_dim(doc, query_offset, TOKENS_PER_SLOT, 0)
        query_pos = query_offset + jnp.arange(TOKENS_PER_SLOT, dtype=jnp.int32)

        def masked_scores(key_head_rows, key_doc, key_pos):
            scores = jnp.einsum('qhgd,khd->hgqk', query_head_rows, key_head_rows) * scale
            allow = (key_pos[None, :] <= query_pos[:, None]) & (key_doc[None, :] == query_doc[:, None])
            return jnp.where(allow, scores, -1e30), allow

        def forward_step(state, key_tile):
            peak, total, accum = state
            start_offset, key_head_rows, value_head_rows, key_doc, key_pos = key_slices(key_tile)
            masked, allow = masked_scores(key_head_rows, key_doc, key_pos)
            new_peak = jnp.maximum(peak, jnp.max(masked, axis=-1))
            expd = jnp.where(allow, jnp.exp(masked - new_peak[..., None]), 0.0)
            factor = jnp.exp(peak - new_peak)
            weights = lax.optimization_barrier(expd.astype(jnp.bfloat16)).astype(jnp.float32)
            total = total * factor + jnp.sum(expd, axis=-1)
            accum = accum * factor[..., None] + jnp.einsum('hgqk,khd->hgqd', weights, value_head_rows)
            return (new_peak, total, accum), None

        head_layout = (KEY_VALUE_HEADS, QUERY_PER_KV, TOKENS_PER_SLOT)
        start_state = (jnp.full(head_layout, -1e30, jnp.float32), jnp.zeros(head_layout, jnp.float32),
                       jnp.zeros((KEY_VALUE_HEADS, QUERY_PER_KV, TOKENS_PER_SLOT, HEAD_SIZE), jnp.float32))
        (peak, total, accum), unused = lax.scan(forward_step, start_state, jnp.arange(N_SEQ, dtype=jnp.int32))
        out_heads = (accum / total[..., None]).astype(jnp.bfloat16).transpose(2, 0, 1, 3)
        delta = jnp.sum(gradient_heads * out_heads.astype(jnp.float32), axis=-1).transpose(1, 2, 0)

        def backward_step(state, key_tile):
            grad_query, key_total, value_total = state
            start_offset, key_head_rows, value_head_rows, key_doc, key_pos = key_slices(key_tile)
            masked, allow = masked_scores(key_head_rows, key_doc, key_pos)
            probs = jnp.where(allow, jnp.exp(masked - peak[..., None]), 0.0) / total[..., None]
            probs_b = lax.optimization_barrier(probs.astype(jnp.bfloat16)).astype(jnp.float32)
            dprob = jnp.einsum('qhgd,khd->hgqk', gradient_heads, value_head_rows)
            dscore = lax.optimization_barrier((probs * (dprob - delta[..., None])).astype(jnp.bfloat16)).astype(jnp.float32)
            grad_query = grad_query + jnp.einsum('hgqk,khd->qhgd', dscore, key_head_rows)
            key_part = lax.optimization_barrier((jnp.einsum('hgqk,qhgd->khd', dscore, query_head_rows) * scale).astype(jnp.bfloat16)).astype(jnp.float32)
            value_part = lax.optimization_barrier(jnp.einsum('hgqk,qhgd->khd', probs_b, gradient_heads).astype(jnp.bfloat16)).astype(jnp.float32)
            key_total = lax.dynamic_update_slice_in_dim(key_total, lax.dynamic_slice_in_dim(key_total, start_offset, TOKENS_PER_SLOT, 0) + key_part, start_offset, 0)
            value_total = lax.dynamic_update_slice_in_dim(value_total, lax.dynamic_slice_in_dim(value_total, start_offset, TOKENS_PER_SLOT, 0) + value_part, start_offset, 0)
            return (grad_query, key_total, value_total), None

        reverse_state = (jnp.zeros((TOKENS_PER_SLOT, KEY_VALUE_HEADS, QUERY_PER_KV, HEAD_SIZE), jnp.float32), key_gradient_sum, value_gradient_sum)
        (grad_query, key_gradient_sum, value_gradient_sum), unused = lax.scan(backward_step, reverse_state, jnp.arange(N_SEQ, dtype=jnp.int32))
        grad_rows = (grad_query * scale).astype(jnp.bfloat16)
        return (key_gradient_sum, value_gradient_sum), (out_heads.reshape(TOKENS_PER_SLOT, QW), grad_rows.reshape(TOKENS_PER_SLOT, QW))

    zero_filled = jnp.zeros((SPAN_TOKENS, KEY_VALUE_HEADS, HEAD_SIZE), jnp.float32)
    (key_gradient_sum, value_gradient_sum), (outs, grads) = lax.scan(query_step, (zero_filled, zero_filled), jnp.arange(N_SEQ, dtype=jnp.int32))
    return (outs.reshape(SPAN_TOKENS, QW), grads.reshape(SPAN_TOKENS, QW),
            key_gradient_sum.reshape(SPAN_TOKENS, KW).astype(jnp.bfloat16), value_gradient_sum.reshape(SPAN_TOKENS, KW).astype(jnp.bfloat16))


def reference(hidden, queries, keys, value_weight, doc_ids, cotangent):
    flat = hidden.reshape(SPAN_COUNT * SPAN_TOKENS, D)
    values = jnp.dot(flat, value_weight, preferred_element_type=jnp.float32).astype(jnp.bfloat16).reshape(SPAN_COUNT, SPAN_TOKENS, KW)
    attn_out, grad_queries, grad_keys, grad_values = lax.map(attend_span, (queries, keys, values, doc_ids, cotangent))
    grad_flat = grad_values.reshape(SPAN_COUNT * SPAN_TOKENS, KW)
    grad_hidden = jnp.dot(grad_flat, value_weight.T, preferred_element_type=jnp.float32).astype(jnp.bfloat16).reshape(SPAN_COUNT, SPAN_TOKENS, D)
    grad_weight = jnp.dot(flat.T, grad_flat, preferred_element_type=jnp.float32)
    return attn_out, grad_queries, grad_keys, grad_hidden, grad_weight
```

```python
import functools

import jax
import jax.numpy as jnp
from jax import lax
from jax.experimental import pallas as pl
from jax.experimental.pallas import tpu as pltpu
from jax.sharding import PartitionSpec as P

QUERY_HEADS = 20
KEY_VALUE_HEADS = 4
HEAD_SIZE = 128
QUERY_PER_KV = 5

BF = jnp.bfloat16
F32 = jnp.float32
VM = pl.BlockSpec(memory_space=pltpu.VMEM)
ANY = pl.BlockSpec(memory_space=pl.ANY)


def body(hidden, queries, keys, value_weight, doc_ids, cotangent):
    tokens = hidden[0]
    row_count = tokens.shape[0]
    width = value_weight.shape[1]
    scale = HEAD_SIZE ** (-0.5)
    shard_list = lax.axis_size("seq")
    my_index = lax.axis_index("seq")
    full_weight = lax.all_gather(value_weight, "dp", axis=0, tiled=True)
    values_sum = jnp.dot(tokens, full_weight, preferred_element_type=jnp.float32)
    values = values_sum.astype(jnp.bfloat16)
    every_key, every_value, all_docs = (
        lax.all_gather(keys[0], "seq", axis=0, tiled=True),
        lax.all_gather(values, "seq", axis=0, tiled=True),
        lax.all_gather(doc_ids[0], "seq", axis=0, tiled=True),
    )
    query_head_rows = queries[0].reshape(row_count, KEY_VALUE_HEADS, QUERY_PER_KV, HEAD_SIZE)
    gradient_heads = cotangent[0].reshape(row_count, KEY_VALUE_HEADS, QUERY_PER_KV, HEAD_SIZE)
    query_docs = doc_ids[0]
    query_pos = my_index * row_count + jnp.arange(row_count, dtype=jnp.int32)
    local_pos = jnp.arange(row_count, dtype=jnp.int32)

    def block_scores(shard):
        start_offset = shard * row_count
        key_tile = lax.dynamic_slice_in_dim(every_key, start_offset, row_count, 0).reshape(
            row_count, KEY_VALUE_HEADS, HEAD_SIZE
        )
        value_tile = lax.dynamic_slice_in_dim(every_value, start_offset, row_count, 0).reshape(
            row_count, KEY_VALUE_HEADS, HEAD_SIZE
        )
        doc_block = lax.dynamic_slice_in_dim(all_docs, start_offset, row_count, 0)
        scores = (
            jnp.einsum(
                "qhgd,khd->hgqk", query_head_rows, key_tile, preferred_element_type=jnp.float32
            )
            * scale
        )
        allow = ((start_offset + local_pos)[None, :] <= query_pos[:, None]) & (
            doc_block[None, :] == query_docs[:, None]
        )
        return (jnp.where(allow, scores, -1e30), allow, key_tile, value_tile)

    def forward_step(shard, carry):
        peak, total, out_acc = carry
        masked, allow, key_tile, value_tile = block_scores(shard)
        new_peak = jnp.maximum(peak, jnp.max(masked, axis=-1))
        expd = jnp.where(allow, jnp.exp(masked - new_peak[..., None]), 0.0)
        factor = jnp.exp(peak - new_peak)
        total = total * factor + jnp.sum(expd, axis=-1)
        out_acc = out_acc * factor[..., None] + jnp.einsum(
            "hgqk,khd->hgqd",
            expd.astype(jnp.bfloat16),
            value_tile,
            preferred_element_type=jnp.float32,
        )
        return (new_peak, total, out_acc)

    head_layout = (KEY_VALUE_HEADS, QUERY_PER_KV, row_count)
    start_state = (
        jnp.full(head_layout, -1e30, jnp.float32),
        jnp.zeros(head_layout, jnp.float32),
        jnp.zeros((KEY_VALUE_HEADS, QUERY_PER_KV, row_count, HEAD_SIZE), jnp.float32),
    )
    peak, total, out_acc = lax.fori_loop(0, shard_list, forward_step, start_state)
    attn_b = (out_acc / total[..., None]).astype(jnp.bfloat16).transpose(2, 0, 1, 3)
    delta = jnp.sum(
        gradient_heads.astype(jnp.float32) * attn_b.astype(jnp.float32), axis=-1
    ).transpose(1, 2, 0)

    def gradient_update(shard, carry):
        dq_acc, grad_buf = carry
        masked, allow, key_tile, value_tile = block_scores(shard)
        probs = jnp.where(allow, jnp.exp(masked - peak[..., None]), 0.0) / total[..., None]
        probs_b = probs.astype(jnp.bfloat16)
        dprob = jnp.einsum(
            "qhgd,khd->hgqk", gradient_heads, value_tile, preferred_element_type=jnp.float32
        )
        dscore = (probs * (dprob - delta[..., None])).astype(jnp.bfloat16)
        dq_acc = dq_acc + jnp.einsum(
            "hgqk,khd->qhgd", dscore, key_tile, preferred_element_type=jnp.float32
        )
        dk_block = (
            jnp.einsum(
                "hgqk,qhgd->khd", dscore, query_head_rows, preferred_element_type=jnp.float32
            )
            * scale
        ).astype(jnp.bfloat16)
        dv_block = jnp.einsum(
            "hgqk,qhgd->khd", probs_b, gradient_heads, preferred_element_type=jnp.float32
        ).astype(jnp.bfloat16)
        paired = jnp.concatenate(
            (dk_block.reshape(row_count, width), dv_block.reshape(row_count, width)), axis=1
        )
        grad_buf = lax.dynamic_update_slice_in_dim(grad_buf, paired, shard * row_count, 0)
        return (dq_acc, grad_buf)

    blank_buffer = jnp.zeros((row_count * shard_list, 2 * width), jnp.bfloat16)
    dq_acc, grad_buf = lax.fori_loop(
        0,
        shard_list,
        gradient_update,
        (
            jnp.zeros((row_count, KEY_VALUE_HEADS, QUERY_PER_KV, HEAD_SIZE), jnp.float32),
            blank_buffer,
        ),
    )
    grad_queries = (dq_acc * scale).astype(jnp.bfloat16).reshape(row_count, QUERY_HEADS * HEAD_SIZE)
    summed = lax.psum_scatter(
        grad_buf.astype(jnp.float32).astype(jnp.bfloat16), "seq", scatter_dimension=0, tiled=True
    ).astype(jnp.float32)
    grad_keys = summed[:, :width].astype(jnp.bfloat16)
    grad_values = summed[:, width:].astype(jnp.bfloat16)
    grad_hidden = jnp.einsum(
        "kc,dc->kd", grad_values, full_weight, preferred_element_type=jnp.float32
    ).astype(jnp.bfloat16)
    partial_rows = lax.psum_scatter(
        jnp.einsum("kd,kc->dc", tokens, grad_values, preferred_element_type=jnp.float32).astype(
            jnp.bfloat16
        ),
        "dp",
        scatter_dimension=0,
        tiled=True,
    )
    grad_weight = lax.psum(partial_rows, "seq").astype(jnp.float32)
    return (
        attn_b.reshape(row_count, QUERY_HEADS * HEAD_SIZE)[None],
        grad_queries[None],
        grad_keys[None],
        grad_hidden[None],
        grad_weight,
    )


N_DP = 8
ROWS = 128
SHARD = 640
HALF = SHARD // 2
WINDOW = 384
PAD = WINDOW - HALF
WIDE = N_DP * WINDOW
CORE_KV = 256
CORE_Q = 1280


def params():
    return pltpu.CompilerParams(vmem_limit_bytes=50 * 1024 * 1024)


def cost(flops, nbytes):
    return pl.CostEstimate(flops=int(flops), bytes_accessed=int(nbytes), transcendentals=0)


def sds(shape, dtype=BF):
    return jax.ShapeDtypeStruct(shape, dtype)


def swap(x, axis, k):
    size = lax.axis_size(axis)
    return lax.ppermute(x, axis, [(i, i ^ k) for i in range(size)])


def weight_part_kernel(w_ref, o_ref, sem):
    s = lax.axis_index("seq")
    y, c = s // 2, s % 2
    copy = pltpu.make_async_copy(
        w_ref.at[pl.ds(pl.multiple_of(y * HALF, HALF), HALF), pl.ds(pl.multiple_of(c * CORE_KV, CORE_KV), CORE_KV)],
        o_ref,
        sem,
    )
    copy.start()
    copy.wait()


def weight_part(w):
    return pl.pallas_call(
        weight_part_kernel,
        out_shape=sds((HALF, CORE_KV)),
        in_specs=[ANY],
        out_specs=ANY,
        scratch_shapes=[pltpu.SemaphoreType.DMA],
        compiler_params=params(),
        cost_estimate=cost(0, 2 * HALF * CORE_KV * 2),
    )(w)


def hidden_parts_kernel(h_ref, keep_ref, send_ref, sems):
    s = lax.axis_index("seq")
    r = lax.axis_index("dp")
    y = s // 2
    copies = []
    for which, (out, part) in enumerate(((send_ref, 1 - y), (keep_ref, y))):
        for j in range(N_DP):
            start = pl.multiple_of((r ^ j) * SHARD + part * (SHARD - WINDOW), 128)
            copies.append(
                pltpu.make_async_copy(
                    h_ref.at[:, pl.ds(start, WINDOW)],
                    out.at[:, pl.ds(j * WINDOW, WINDOW)],
                    sems.at[which * N_DP + j],
                )
            )
    for copy in copies:
        copy.start()
    for copy in copies:
        copy.wait()


def hidden_parts(h):
    return pl.pallas_call(
        hidden_parts_kernel,
        out_shape=(sds((ROWS, WIDE)), sds((ROWS, WIDE))),
        in_specs=[ANY],
        out_specs=(ANY, ANY),
        scratch_shapes=[pltpu.SemaphoreType.DMA((2 * N_DP,))],
        compiler_params=params(),
        cost_estimate=cost(0, 4 * ROWS * WIDE * 2),
    )(h)


def values_kernel(h0, h1, h2, h3, w0, w1, w2, w3, w4, w5, w6, w7, vp_ref, wpad_ref):
    y = lax.axis_index("seq") // 2
    for j, w in enumerate((w0, w1, w2, w3, w4, w5, w6, w7)):
        wpad_ref[pl.ds(pl.multiple_of(j * WINDOW + y * PAD, PAD), HALF), :] = w[...]
        wpad_ref[pl.ds(pl.multiple_of(j * WINDOW + (1 - y) * HALF, PAD), PAD), :] = jnp.zeros((PAD, CORE_KV), BF)
    for t, h in enumerate((h0, h1, h2, h3)):
        vp_ref[t * ROWS : (t + 1) * ROWS, :] = jnp.dot(
            h[...], wpad_ref[...], preferred_element_type=F32
        ).astype(BF)


def partial_values(hs, ws):
    return pl.pallas_call(
        values_kernel,
        out_shape=(sds((4 * ROWS, CORE_KV)), sds((WIDE, CORE_KV))),
        in_specs=[VM] * 12,
        out_specs=(VM, VM),
        compiler_params=params(),
        cost_estimate=cost(2 * 512 * WIDE * 256, 6e6),
    )(*hs, *ws)


def dot_tt(a, b):
    return lax.dot_general(a, b, (((0,), (0,)), ((), ())), preferred_element_type=F32)


def dot_nt(a, b):
    return lax.dot_general(a, b, (((1,), (1,)), ((), ())), preferred_element_type=F32)


def attention_kernel(
    q0, q1, g0, g1, k0, k1, k2, k3, vp, rv,
    o0, o1, dq0, dq1, dv_ref, dk_ref, dks_ref, bias,
):
    s = lax.axis_index("seq")
    c = s % 2
    factor = HEAD_SIZE ** (-0.5)
    log2e = 1.4426950408889634
    ks = (k0, k1, k2, k3)
    rows = [k[ROWS : ROWS + 16, 0:ROWS][0:1, :].astype(F32) for k in ks]
    for t in range(4):
        key_doc = jnp.transpose(jnp.broadcast_to(rows[t], (ROWS, ROWS)))
        key_pos = (s ^ t) * ROWS + lax.broadcasted_iota(jnp.int32, (ROWS, ROWS), 0)
        for u in range(2):
            query_pos = (s ^ u) * ROWS + lax.broadcasted_iota(jnp.int32, (ROWS, ROWS), 1)
            allow = (key_pos <= query_pos) & (key_doc == jnp.broadcast_to(rows[u], (ROWS, ROWS)))
            bias[t * ROWS : (t + 1) * ROWS, u * ROWS : (u + 1) * ROWS] = jnp.where(allow, 0.0, -1e30)
    for kvh in range(2):
        cols = pl.ds(pl.multiple_of(c * CORE_KV + kvh * HEAD_SIZE, HEAD_SIZE), HEAD_SIZE)
        mine = slice(kvh * HEAD_SIZE, (kvh + 1) * HEAD_SIZE)
        key = jnp.concatenate([k[0:ROWS, cols] for k in ks], axis=0)
        far = rv[:, mine].astype(F32)
        far = jnp.concatenate([far[2 * ROWS :], far[: 2 * ROWS]], axis=0)
        value = (vp[:, mine].astype(F32) + far).astype(BF)
        dk = jnp.zeros((4 * ROWS, HEAD_SIZE), F32)
        dv = jnp.zeros((4 * ROWS, HEAD_SIZE), F32)
        for g in range(QUERY_PER_KV):
            head = kvh * QUERY_PER_KV + g
            qcols = pl.ds(pl.multiple_of(c * CORE_Q + head * HEAD_SIZE, HEAD_SIZE), HEAD_SIZE)
            ocols = slice(head * HEAD_SIZE, (head + 1) * HEAD_SIZE)
            query = jnp.concatenate([q0[:, qcols], q1[:, qcols]], axis=0)
            cot = jnp.concatenate([g0[:, qcols], g1[:, qcols]], axis=0)
            st = dot_nt(key, query) * (factor * log2e) + bias[...]
            peak = jnp.max(st, axis=0, keepdims=True)
            e = jnp.exp2(st - peak)
            inv = 1.0 / jnp.sum(e, axis=0, keepdims=True)
            out_t = dot_tt(value, e.astype(BF)) * inv
            out = jnp.transpose(out_t).astype(BF)
            o0[:, ocols] = out[:ROWS]
            o1[:, ocols] = out[ROWS:]
            probs = e * inv
            dprob = dot_nt(value, cot)
            term = probs * dprob
            delta = jnp.sum(term, axis=0, keepdims=True)
            ds = (term - probs * delta).astype(BF)
            dq = jnp.transpose(dot_tt(key, ds) * factor).astype(BF)
            dq0[:, ocols] = dq[:ROWS]
            dq1[:, ocols] = dq[ROWS:]
            dk = dk + jnp.dot(ds, query, preferred_element_type=F32)
            dv = dv + jnp.dot(probs.astype(BF), cot, preferred_element_type=F32)
        dk = (dk * factor).astype(BF)
        dk_ref[:, mine] = dk[: 2 * ROWS]
        dks_ref[:, mine] = dk[2 * ROWS :]
        dv_ref[:, mine] = dv.astype(BF)


def attention(q, qs, g, gs, ks, vp, rv):
    return pl.pallas_call(
        attention_kernel,
        out_shape=(sds((ROWS, CORE_Q)),) * 4
        + (sds((4 * ROWS, CORE_KV)), sds((2 * ROWS, CORE_KV)), sds((2 * ROWS, CORE_KV))),
        in_specs=[VM] * 10,
        out_specs=(VM,) * 7,
        scratch_shapes=[pltpu.VMEM((4 * ROWS, 2 * ROWS), F32)],
        compiler_params=params(),
        cost_estimate=cost(2 * 6 * 10 * 256 * 512 * 128 * 4, 6e6),
    )(q, qs, g, gs, *ks, vp, rv)


def weight_grad_kernel(dv, rdv, h0, h1, h2, h3, own_a, own_b, send_a, send_b, gv_keep, gv_send, gv):
    for t in range(4):
        a = dv[t * ROWS : (t + 1) * ROWS, :].astype(F32)
        b = rdv[(t ^ 2) * ROWS : ((t ^ 2) + 1) * ROWS, :].astype(F32)
        total = (a + b).astype(BF)
        gv[t * ROWS : (t + 1) * ROWS, :] = total
        half = (t // 2) * ROWS
        if t % 2 == 0:
            gv_keep[half : half + ROWS, :] = total
        else:
            gv_send[half : half + ROWS, :] = total
    y = lax.axis_index("seq") // 2
    for j, (out, place) in (
        (5, (send_a, 0)), (7, (send_a, 1)), (4, (own_a, 0)), (6, (own_a, 1)),
        (1, (send_b, 0)), (3, (send_b, 1)), (0, (own_b, 0)), (2, (own_b, 1)),
    ):
        acc = jnp.zeros((WINDOW, CORE_KV), F32)
        for t, h in enumerate((h0, h1, h2, h3)):
            acc = acc + dot_tt(h[:, j * WINDOW : (j + 1) * WINDOW], gv[t * ROWS : (t + 1) * ROWS, :])
        part = jnp.where(y == 0, acc[:HALF], acc[PAD:])
        out[place * HALF : (place + 1) * HALF, :] = part.astype(BF)


def weight_grad(dv, rdv, hs):
    return pl.pallas_call(
        weight_grad_kernel,
        out_shape=(sds((2 * HALF, CORE_KV)),) * 4 + (sds((2 * ROWS, CORE_KV)),) * 2,
        in_specs=[VM] * 6,
        out_specs=(VM,) * 6,
        scratch_shapes=[pltpu.VMEM((4 * ROWS, CORE_KV), BF)],
        compiler_params=params(),
        cost_estimate=cost(2 * 512 * WIDE * 256, 6e6),
    )(dv, rdv, *hs)


def hidden_grad_kernel(gv, gvs, wp, wps, gh0, gh2):
    full = dot_nt(gv[...], wp[...]) + dot_nt(gvs[...], wps[...])
    full = full.astype(BF)
    gh0[...] = full[:ROWS]
    gh2[...] = full[ROWS:]


def hidden_grad(gv, gvs, wp, wps):
    return pl.pallas_call(
        hidden_grad_kernel,
        out_shape=(sds((ROWS, WIDE)),) * 2,
        in_specs=[VM] * 4,
        out_specs=(VM,) * 2,
        compiler_params=params(),
        cost_estimate=cost(2 * 256 * WIDE * 512, 6e6),
    )(gv, gvs, wp, wps)


def hidden_join_kernel(own_ref, far_ref, o_ref):
    y = lax.axis_index("seq") // 2
    r = lax.axis_index("dp")
    for j in range(N_DP):
        own = own_ref[:, j * WINDOW : (j + 1) * WINDOW]
        far = far_ref[:, j * WINDOW : (j + 1) * WINDOW]
        low = jnp.where(y == 0, own, far)
        high = jnp.where(y == 0, far, own)
        base = pl.multiple_of((r ^ j) * SHARD, 128)
        o_ref[:, pl.ds(base, 256)] = low[:, :256]
        o_ref[:, pl.ds(pl.multiple_of(base + 256, 128), 128)] = low[:, 256:] + high[:, :128]
        o_ref[:, pl.ds(pl.multiple_of(base + 384, 128), 256)] = high[:, 128:]


def hidden_join(own, far):
    return pl.pallas_call(
        hidden_join_kernel,
        out_shape=sds((ROWS, N_DP * SHARD)),
        in_specs=[VM] * 2,
        out_specs=VM,
        compiler_params=params(),
        cost_estimate=cost(0, 3e6),
    )(own, far)


def add_pair_kernel(a, b, o0, o1):
    total = (a[...].astype(F32) + b[...].astype(F32)).astype(BF)
    o0[...] = total[:HALF]
    o1[...] = total[HALF:]


def add_pair(a, b):
    return pl.pallas_call(
        add_pair_kernel,
        out_shape=(sds((HALF, CORE_KV)),) * 2,
        in_specs=[VM] * 2,
        out_specs=(VM,) * 2,
        compiler_params=params(),
        cost_estimate=cost(0, 1e6),
    )(a, b)


def add_four_kernel(a, b, c, d, o):
    o[...] = (
        (a[...].astype(F32) + b[...].astype(F32)) + (c[...].astype(F32) + d[...].astype(F32))
    ).astype(BF)


def add_four(a, b, c, d):
    return pl.pallas_call(
        add_four_kernel,
        out_shape=sds((HALF, CORE_KV)),
        in_specs=[VM] * 4,
        out_specs=VM,
        compiler_params=params(),
        cost_estimate=cost(0, 1e6),
    )(a, b, c, d)


def weight_join_kernel(p0, p1, p2, p3, o_ref):
    s = lax.axis_index("seq")
    for t, p in enumerate((p0, p1, p2, p3)):
        owner = s ^ t
        o_ref[
            pl.ds(pl.multiple_of((owner // 2) * HALF, HALF), HALF),
            pl.ds(pl.multiple_of((owner % 2) * CORE_KV, CORE_KV), CORE_KV),
        ] = p[...].astype(F32)


def weight_join(ps):
    return pl.pallas_call(
        weight_join_kernel,
        out_shape=sds((SHARD, 2 * CORE_KV), F32),
        in_specs=[VM] * 4,
        out_specs=VM,
        compiler_params=params(),
        cost_estimate=cost(0, 2e6),
    )(*ps)


def heads_join_kernel(a0, a1, b0, b1, c0, c1, oa, ob, oc):
    c = lax.axis_index("seq") % 2
    for near, far, out in ((a0, a1, oa), (b0, b1, ob), (c0, c1, oc)):
        width = near.shape[1]
        out[:, pl.ds(pl.multiple_of(c * width, 128), width)] = near[...]
        out[:, pl.ds(pl.multiple_of((1 - c) * width, 128), width)] = far[...]


def heads_join(*parts):
    return pl.pallas_call(
        heads_join_kernel,
        out_shape=tuple(sds((ROWS, 2 * p.shape[1])) for p in parts[::2]),
        in_specs=[VM] * 6,
        out_specs=(VM,) * 3,
        compiler_params=params(),
        cost_estimate=cost(0, 4e6),
    )(*parts)


def paired_body(hidden, queries, keys, value_weight, doc_ids, cotangent):
    h, q, g = hidden[0], queries[0], cotangent[0]
    w0 = weight_part(value_weight)
    w2, w4, w6 = swap(w0, "dp", 2), swap(w0, "dp", 4), swap(w0, "dp", 6)
    w1 = swap(w0, "dp", 1)
    w3 = swap(w2, "dp", 1)
    w5, w7 = swap(w4, "dp", 1), swap(w6, "dp", 1)
    h0, h_send = hidden_parts(h)
    h2 = swap(h_send, "seq", 2)
    h1 = swap(h0, "seq", 1)
    h3 = swap(h2, "seq", 1)
    doc_row = jnp.pad(doc_ids.astype(BF), ((0, 15), (0, keys.shape[2] - ROWS)))
    k0 = jnp.concatenate([keys[0], doc_row], axis=0)
    k2 = swap(k0, "seq", 2)
    k1, k3 = swap(k0, "seq", 1), swap(k2, "seq", 1)
    qs, gs = swap(q, "seq", 1), swap(g, "seq", 1)

    vp, wpad = partial_values((h0, h1, h2, h3), (w0, w1, w2, w3, w4, w5, w6, w7))
    rv = swap(vp, "seq", 2)
    wpad_s = swap(wpad, "seq", 1)
    o0, o1, dq0, dq1, dv, dk0, dk_send = attention(q, qs, g, gs, (k0, k1, k2, k3), vp, rv)
    rdv = swap(dv, "seq", 2)
    own_a, own_b, send_a, send_b, gv, gv_send = weight_grad(dv, rdv, (h0, h1, h2, h3))
    far_a = swap(send_a, "dp", 1)
    far_b = swap(send_b, "dp", 1)
    gvs = swap(gv_send, "seq", 1)
    gh0, gh2 = hidden_grad(gv, gvs, wpad, wpad_s)
    s4, s6 = add_pair(own_a, far_a)
    t6, t4 = swap(s6, "dp", 6), swap(s4, "dp", 4)
    s0, s2 = add_pair(own_b, far_b)
    t2 = swap(s2, "dp", 2)
    gh_far = swap(gh2, "seq", 2)
    dk_far = swap(dk_send, "seq", 2)
    dk_a, dk_b = add_dk(dk0, dk_far)
    oc, dqc, dkc = swap(o1, "seq", 1), swap(dq1, "seq", 1), swap(dk_b, "seq", 1)
    attn_out, grad_queries, grad_keys = heads_join(o0, oc, dq0, dqc, dk_a, dkc)
    grad_hidden = hidden_join(gh0, gh_far)
    p0 = add_four(s0, t2, t4, t6)
    p2 = swap(p0, "seq", 2)
    p1, p3 = swap(p0, "seq", 1), swap(p2, "seq", 1)
    grad_weight = weight_join((p0, p1, p2, p3))
    return attn_out[None], grad_queries[None], grad_keys[None], grad_hidden[None], grad_weight


def add_dk_kernel(a, b, o0, o1):
    total = (a[...].astype(F32) + b[...].astype(F32)).astype(BF)
    o0[...] = total[:ROWS]
    o1[...] = total[ROWS:]


def add_dk(a, b):
    return pl.pallas_call(
        add_dk_kernel,
        out_shape=(sds((ROWS, CORE_KV)),) * 2,
        in_specs=[VM] * 2,
        out_specs=(VM,) * 2,
        compiler_params=params(),
        cost_estimate=cost(0, 1e6),
    )(a, b)


def solution(mesh):
    in_specs = (
        P("dp", "seq", None),
        P("dp", "seq", None),
        P("dp", "seq", None),
        P("dp", None),
        P("dp", "seq"),
        P("dp", "seq", None),
    )
    out_specs = (
        P("dp", "seq", None),
        P("dp", "seq", None),
        P("dp", "seq", None),
        P("dp", "seq", None),
        P("dp", None),
    )
    paired = mesh.shape["dp"] == N_DP and mesh.shape["seq"] == 4
    return jax.shard_map(
        paired_body if paired else body, mesh=mesh, in_specs=in_specs, out_specs=out_specs, check_vma=False
    )
```

```python
import functools

import jax
import jax.numpy as jnp
from jax import lax
from jax.experimental import pallas as pl
from jax.experimental.pallas import tpu as pltpu
from jax.sharding import PartitionSpec as P

QUERY_HEADS = 20
KEY_VALUE_HEADS = 4
HEAD_SIZE = 128
QUERY_PER_KV = 5

BF = jnp.bfloat16
F32 = jnp.float32
VM = pl.BlockSpec(memory_space=pltpu.VMEM)
ANY = pl.BlockSpec(memory_space=pl.ANY)


def body(hidden, queries, keys, value_weight, doc_ids, cotangent):
    tokens = hidden[0]
    row_count = tokens.shape[0]
    width = value_weight.shape[1]
    scale = HEAD_SIZE ** (-0.5)
    shard_list = lax.axis_size("seq")
    my_index = lax.axis_index("seq")
    full_weight = lax.all_gather(value_weight, "dp", axis=0, tiled=True)
    values_sum = jnp.dot(tokens, full_weight, preferred_element_type=jnp.float32)
    values = values_sum.astype(jnp.bfloat16)
    every_key, every_value, all_docs = (
        lax.all_gather(keys[0], "seq", axis=0, tiled=True),
        lax.all_gather(values, "seq", axis=0, tiled=True),
        lax.all_gather(doc_ids[0], "seq", axis=0, tiled=True),
    )
    query_head_rows = queries[0].reshape(row_count, KEY_VALUE_HEADS, QUERY_PER_KV, HEAD_SIZE)
    gradient_heads = cotangent[0].reshape(row_count, KEY_VALUE_HEADS, QUERY_PER_KV, HEAD_SIZE)
    query_docs = doc_ids[0]
    query_pos = my_index * row_count + jnp.arange(row_count, dtype=jnp.int32)
    local_pos = jnp.arange(row_count, dtype=jnp.int32)

    def block_scores(shard):
        start_offset = shard * row_count
        key_tile = lax.dynamic_slice_in_dim(every_key, start_offset, row_count, 0).reshape(
            row_count, KEY_VALUE_HEADS, HEAD_SIZE
        )
        value_tile = lax.dynamic_slice_in_dim(every_value, start_offset, row_count, 0).reshape(
            row_count, KEY_VALUE_HEADS, HEAD_SIZE
        )
        doc_block = lax.dynamic_slice_in_dim(all_docs, start_offset, row_count, 0)
        scores = (
            jnp.einsum(
                "qhgd,khd->hgqk", query_head_rows, key_tile, preferred_element_type=jnp.float32
            )
            * scale
        )
        allow = ((start_offset + local_pos)[None, :] <= query_pos[:, None]) & (
            doc_block[None, :] == query_docs[:, None]
        )
        return (jnp.where(allow, scores, -1e30), allow, key_tile, value_tile)

    def forward_step(shard, carry):
        peak, total, out_acc = carry
        masked, allow, key_tile, value_tile = block_scores(shard)
        new_peak = jnp.maximum(peak, jnp.max(masked, axis=-1))
        expd = jnp.where(allow, jnp.exp(masked - new_peak[..., None]), 0.0)
        factor = jnp.exp(peak - new_peak)
        total = total * factor + jnp.sum(expd, axis=-1)
        out_acc = out_acc * factor[..., None] + jnp.einsum(
            "hgqk,khd->hgqd",
            expd.astype(jnp.bfloat16),
            value_tile,
            preferred_element_type=jnp.float32,
        )
        return (new_peak, total, out_acc)

    head_layout = (KEY_VALUE_HEADS, QUERY_PER_KV, row_count)
    start_state = (
        jnp.full(head_layout, -1e30, jnp.float32),
        jnp.zeros(head_layout, jnp.float32),
        jnp.zeros((KEY_VALUE_HEADS, QUERY_PER_KV, row_count, HEAD_SIZE), jnp.float32),
    )
    peak, total, out_acc = lax.fori_loop(0, shard_list, forward_step, start_state)
    attn_b = (out_acc / total[..., None]).astype(jnp.bfloat16).transpose(2, 0, 1, 3)
    delta = jnp.sum(
        gradient_heads.astype(jnp.float32) * attn_b.astype(jnp.float32), axis=-1
    ).transpose(1, 2, 0)

    def gradient_update(shard, carry):
        dq_acc, grad_buf = carry
        masked, allow, key_tile, value_tile = block_scores(shard)
        probs = jnp.where(allow, jnp.exp(masked - peak[..., None]), 0.0) / total[..., None]
        probs_b = probs.astype(jnp.bfloat16)
        dprob = jnp.einsum(
            "qhgd,khd->hgqk", gradient_heads, value_tile, preferred_element_type=jnp.float32
        )
        dscore = (probs * (dprob - delta[..., None])).astype(jnp.bfloat16)
        dq_acc = dq_acc + jnp.einsum(
            "hgqk,khd->qhgd", dscore, key_tile, preferred_element_type=jnp.float32
        )
        dk_block = (
            jnp.einsum(
                "hgqk,qhgd->khd", dscore, query_head_rows, preferred_element_type=jnp.float32
            )
            * scale
        ).astype(jnp.bfloat16)
        dv_block = jnp.einsum(
            "hgqk,qhgd->khd", probs_b, gradient_heads, preferred_element_type=jnp.float32
        ).astype(jnp.bfloat16)
        paired = jnp.concatenate(
            (dk_block.reshape(row_count, width), dv_block.reshape(row_count, width)), axis=1
        )
        grad_buf = lax.dynamic_update_slice_in_dim(grad_buf, paired, shard * row_count, 0)
        return (dq_acc, grad_buf)

    blank_buffer = jnp.zeros((row_count * shard_list, 2 * width), jnp.bfloat16)
    dq_acc, grad_buf = lax.fori_loop(
        0,
        shard_list,
        gradient_update,
        (
            jnp.zeros((row_count, KEY_VALUE_HEADS, QUERY_PER_KV, HEAD_SIZE), jnp.float32),
            blank_buffer,
        ),
    )
    grad_queries = (dq_acc * scale).astype(jnp.bfloat16).reshape(row_count, QUERY_HEADS * HEAD_SIZE)
    summed = lax.psum_scatter(
        grad_buf.astype(jnp.float32).astype(jnp.bfloat16), "seq", scatter_dimension=0, tiled=True
    ).astype(jnp.float32)
    grad_keys = summed[:, :width].astype(jnp.bfloat16)
    grad_values = summed[:, width:].astype(jnp.bfloat16)
    grad_hidden = jnp.einsum(
        "kc,dc->kd", grad_values, full_weight, preferred_element_type=jnp.float32
    ).astype(jnp.bfloat16)
    partial_rows = lax.psum_scatter(
        jnp.einsum("kd,kc->dc", tokens, grad_values, preferred_element_type=jnp.float32).astype(
            jnp.bfloat16
        ),
        "dp",
        scatter_dimension=0,
        tiled=True,
    )
    grad_weight = lax.psum(partial_rows, "seq").astype(jnp.float32)
    return (
        attn_b.reshape(row_count, QUERY_HEADS * HEAD_SIZE)[None],
        grad_queries[None],
        grad_keys[None],
        grad_hidden[None],
        grad_weight,
    )


N_DP = 8
ROWS = 128
SHARD = 640
HALF = SHARD // 2
CHUNK = 128
WIDE = N_DP * HALF
CORE_KV = 256
CORE_Q = 1280
KEY_AT = WIDE
DOC_AT = KEY_AT + 512
QUERY_AT = DOC_AT + ROWS
COT_AT = QUERY_AT + CORE_Q
PACK = COT_AT + CORE_Q


def params(mib=32):
    return pltpu.CompilerParams(vmem_limit_bytes=mib * 1024 * 1024)


def cost(flops, nbytes):
    return pl.CostEstimate(flops=int(flops), bytes_accessed=int(nbytes), transcendentals=0)


def sds(shape, dtype=BF):
    return jax.ShapeDtypeStruct(shape, dtype)


def swap(x, axis, k):
    size = lax.axis_size(axis)
    return lax.ppermute(x, axis, [(i, i ^ k) for i in range(size)])


def after(x, *others):
    return lax.optimization_barrier((x, *others))[0]


def dot_tt(a, b):
    return lax.dot_general(a, b, (((0,), (0,)), ((), ())), preferred_element_type=F32)


def dot_nt(a, b):
    return lax.dot_general(a, b, (((1,), (1,)), ((), ())), preferred_element_type=F32)


def turn(x):
    return pltpu.roll(x.astype(F32), CHUNK // 2, 1).astype(x.dtype)


def first_half():
    return lax.broadcasted_iota(jnp.int32, (ROWS, CHUNK), 1) < CHUNK // 2


def pack_kernel(h, k, doc, w, q, g, send, keep, w0):
    s = lax.axis_index("seq")
    r = lax.axis_index("dp")
    y, c = s // 2, s % 2
    cols = pl.ds(pl.multiple_of(c * CORE_KV, CORE_KV), CORE_KV)
    w0[0:256, :] = w[pl.ds(pl.multiple_of(y * 384, 128), 256), cols]
    w0[256:HALF, :] = w[pl.ds(pl.multiple_of(256 + y * 64, 64), 64), cols]
    low = first_half()
    for out, part in ((send, 1 - y), (keep, y)):
        for p in range(N_DP // 2):
            mids = []
            for i in range(2):
                base = (r ^ (2 * p + i)) * SHARD
                start = pl.multiple_of(base + part * 384, 128)
                out[:, p * SHARD + i * 256 : p * SHARD + (i + 1) * 256] = h[:, pl.ds(start, 256)]
                mid = h[:, pl.ds(pl.multiple_of(base + 256, 128), CHUNK)]
                mids.append(jnp.where(part == i, mid, turn(mid)))
            out[:, p * SHARD + 512 : (p + 1) * SHARD] = jnp.where(low, mids[0], mids[1])
        out[:, KEY_AT:DOC_AT] = k[...]
        out[:, DOC_AT:QUERY_AT] = jnp.broadcast_to(doc[...].astype(F32), (ROWS, ROWS)).astype(BF)
    other = pl.ds(pl.multiple_of((1 - c) * CORE_Q, CORE_Q), CORE_Q)
    keep[:, QUERY_AT:COT_AT] = q[:, other]
    keep[:, COT_AT:PACK] = g[:, other]


def pack(h, k, doc, w, q, g):
    return pl.pallas_call(
        pack_kernel,
        out_shape=(sds((ROWS, QUERY_AT)), sds((ROWS, PACK)), sds((HALF, CORE_KV))),
        in_specs=[VM] * 6,
        out_specs=(VM,) * 3,
        compiler_params=params(60),
        cost_estimate=cost(0, 3e6),
    )(h, k, doc, w, q, g)


def values_kernel(h0, h1, h2, w0, w1, w2, w3, w4, w5, w6, w7, vp_ref, wp_ref):
    ws = (w0, w1, w2, w3, w4, w5, w6, w7)
    for p in range(N_DP // 2):
        a, b = ws[2 * p], ws[2 * p + 1]
        base = p * SHARD
        wp_ref[base : base + 256, :] = a[0:256, :]
        wp_ref[base + 256 : base + 512, :] = b[0:256, :]
        wp_ref[base + 512 : base + 576, :] = a[256:HALF, :]
        wp_ref[base + 576 : base + 640, :] = b[256:HALF, :]
    for t, h in enumerate((h0, h1, h2)):
        vp_ref[t * ROWS : (t + 1) * ROWS, :] = jnp.dot(
            h[:, 0:WIDE], wp_ref[...], preferred_element_type=F32
        ).astype(BF)


def partial_values(hs, ws):
    return pl.pallas_call(
        values_kernel,
        out_shape=(sds((3 * ROWS, CORE_KV)), sds((WIDE, CORE_KV))),
        in_specs=[VM] * 11,
        out_specs=(VM, VM),
        compiler_params=params(),
        cost_estimate=cost(2 * 384 * WIDE * 256, 6e6),
    )(*hs, *ws)


def last_values_kernel(vp, h3, wp, o_ref):
    o_ref[0 : 3 * ROWS, :] = vp[...]
    o_ref[3 * ROWS :, :] = jnp.dot(h3[:, 0:WIDE], wp[...], preferred_element_type=F32).astype(BF)


def last_values(vp, h3, wp):
    return pl.pallas_call(
        last_values_kernel,
        out_shape=sds((4 * ROWS, CORE_KV)),
        in_specs=[VM] * 3,
        out_specs=VM,
        compiler_params=params(),
        cost_estimate=cost(2 * 128 * WIDE * 256, 2e6),
    )(vp, h3, wp)


def scores_kernel(q0, p0, p1, p2, p3, e_ref, inv_ref, bias):
    s = lax.axis_index("seq")
    c = s % 2
    factor = HEAD_SIZE ** (-0.5)
    log2e = 1.4426950408889634
    ps = (p0, p1, p2, p3)
    rows = [p[0:16, DOC_AT:QUERY_AT][0:1, :].astype(F32) for p in ps]
    for t in range(4):
        key_doc = jnp.transpose(jnp.broadcast_to(rows[t], (ROWS, ROWS)))
        key_pos = (s ^ t) * ROWS + lax.broadcasted_iota(jnp.int32, (ROWS, ROWS), 0)
        for u in range(2):
            query_pos = (s ^ u) * ROWS + lax.broadcasted_iota(jnp.int32, (ROWS, ROWS), 1)
            allow = (key_pos <= query_pos) & (key_doc == jnp.broadcast_to(rows[u], (ROWS, ROWS)))
            bias[t * ROWS : (t + 1) * ROWS, u * ROWS : (u + 1) * ROWS] = jnp.where(allow, 0.0, -1e30)
    for kvh in range(2):
        cols = pl.ds(pl.multiple_of(KEY_AT + c * CORE_KV + kvh * HEAD_SIZE, HEAD_SIZE), HEAD_SIZE)
        key = jnp.concatenate([p[:, cols] for p in ps], axis=0)
        for i in range(QUERY_PER_KV):
            head = kvh * QUERY_PER_KV + i
            qcols = pl.ds(pl.multiple_of(c * CORE_Q + head * HEAD_SIZE, HEAD_SIZE), HEAD_SIZE)
            far = p1[:, QUERY_AT + head * HEAD_SIZE : QUERY_AT + (head + 1) * HEAD_SIZE]
            query = jnp.concatenate([q0[:, qcols], far], axis=0)
            st = dot_nt(key, query) * (factor * log2e) + bias[...]
            e = jnp.exp2(st - jnp.max(st, axis=0, keepdims=True))
            inv_ref[head * 8 : head * 8 + 8, :] = jnp.broadcast_to(
                1.0 / jnp.sum(e, axis=0, keepdims=True), (8, 2 * ROWS)
            )
            e_ref[head] = e.astype(BF)


def scores(q, ps):
    return pl.pallas_call(
        scores_kernel,
        out_shape=(sds((10, 4 * ROWS, 2 * ROWS)), sds((80, 2 * ROWS), F32)),
        in_specs=[VM] * 5,
        out_specs=(VM,) * 2,
        scratch_shapes=[pltpu.VMEM((4 * ROWS, 2 * ROWS), F32)],
        compiler_params=params(),
        cost_estimate=cost(2 * 10 * 256 * 512 * 128 * 8, 6e6),
    )(q, *ps)


def attention_kernel(
    e_ref, inv_ref, q0, g0, p0, p1, p2, p3, vp, rv,
    o0, dq0, dk0, dk2, swap_ref, dv_ref,
):
    c = lax.axis_index("seq") % 2
    factor = HEAD_SIZE ** (-0.5)
    ps = (p0, p1, p2, p3)
    for kvh in range(2):
        cols = pl.ds(pl.multiple_of(KEY_AT + c * CORE_KV + kvh * HEAD_SIZE, HEAD_SIZE), HEAD_SIZE)
        mine = slice(kvh * HEAD_SIZE, (kvh + 1) * HEAD_SIZE)
        key = jnp.concatenate([p[:, cols] for p in ps], axis=0)
        far = rv[:, mine].astype(F32)
        far = jnp.concatenate([far[2 * ROWS :], far[: 2 * ROWS]], axis=0)
        value = (vp[:, mine].astype(F32) + far).astype(BF)
        dk = jnp.zeros((4 * ROWS, HEAD_SIZE), F32)
        dv = jnp.zeros((4 * ROWS, HEAD_SIZE), F32)
        for i in range(QUERY_PER_KV):
            head = kvh * QUERY_PER_KV + i
            qcols = pl.ds(pl.multiple_of(c * CORE_Q + head * HEAD_SIZE, HEAD_SIZE), HEAD_SIZE)
            low, high = head * HEAD_SIZE, (head + 1) * HEAD_SIZE
            query = jnp.concatenate([q0[:, qcols], p1[:, QUERY_AT + low : QUERY_AT + high]], axis=0)
            cot = jnp.concatenate([g0[:, qcols], p1[:, COT_AT + low : COT_AT + high]], axis=0)
            e = e_ref[head]
            inv = inv_ref[head * 8 : head * 8 + 8, :][0:1, :]
            out = jnp.transpose(dot_tt(value, e) * inv).astype(BF)
            o0[:, low:high] = out[:ROWS]
            swap_ref[:, low:high] = out[ROWS:]
            probs = e.astype(F32) * inv
            term = probs * dot_nt(value, cot)
            delta = jnp.sum(term, axis=0, keepdims=True)
            ds = (term - probs * delta).astype(BF)
            dq = jnp.transpose(dot_tt(key, ds) * factor).astype(BF)
            dq0[:, low:high] = dq[:ROWS]
            swap_ref[:, CORE_Q + low : CORE_Q + high] = dq[ROWS:]
            dk = dk + jnp.dot(ds, query, preferred_element_type=F32)
            dv = dv + jnp.dot(probs.astype(BF), cot, preferred_element_type=F32)
        dk = (dk * factor).astype(BF)
        dk0[:, mine] = dk[:ROWS]
        dk2[:, mine] = dk[2 * ROWS : 3 * ROWS]
        at = 2 * CORE_Q + kvh * HEAD_SIZE
        swap_ref[:, at : at + HEAD_SIZE] = dk[ROWS : 2 * ROWS]
        swap_ref[:, at + CORE_KV : at + CORE_KV + HEAD_SIZE] = dk[3 * ROWS :]
        dv_ref[:, mine] = dv.astype(BF)


def attention(e, inv, q, g, ps, vp, rv):
    return pl.pallas_call(
        attention_kernel,
        out_shape=(sds((ROWS, CORE_Q)),) * 2
        + (sds((ROWS, CORE_KV)),) * 2
        + (sds((ROWS, 2 * CORE_Q + 2 * CORE_KV)), sds((4 * ROWS, CORE_KV))),
        in_specs=[VM] * 10,
        out_specs=(VM,) * 6,
        compiler_params=params(),
        cost_estimate=cost(2 * 5 * 10 * 256 * 512 * 128 * 4, 6e6),
    )(e, inv, q, g, *ps, vp, rv)


def weight_grad_pair(p, hs, gv, even, odd):
    for (out, at), start in ((even, 0), (odd, 256)):
        acc = jnp.zeros((256, CORE_KV), F32)
        for t, h in enumerate(hs):
            first = p * SHARD + start
            acc = acc + dot_tt(h[:, first : first + 256], gv[t * ROWS : (t + 1) * ROWS, :])
        out[at : at + 256, :] = acc.astype(BF)
    acc = jnp.zeros((CHUNK, CORE_KV), F32)
    for t, h in enumerate(hs):
        acc = acc + dot_tt(h[:, p * SHARD + 512 : (p + 1) * SHARD], gv[t * ROWS : (t + 1) * ROWS, :])
    acc = acc.astype(BF)
    for (out, at), half in ((even, acc[:64]), (odd, acc[64:])):
        out[at + 256 : at + HALF, :] = half


def weight_grad_far_kernel(dv, rdv, h0, h1, h2, h3, send, own, gv, gv_keep, gv_send):
    for t in range(4):
        a = dv[t * ROWS : (t + 1) * ROWS, :].astype(F32)
        b = rdv[(t ^ 2) * ROWS : ((t ^ 2) + 1) * ROWS, :].astype(F32)
        total = (a + b).astype(BF)
        gv[t * ROWS : (t + 1) * ROWS, :] = total
        half = (t // 2) * ROWS
        if t % 2 == 0:
            gv_keep[half : half + ROWS, :] = total
        else:
            gv_send[half : half + ROWS, :] = total
    for place, p in enumerate((2, 3)):
        weight_grad_pair(p, (h0, h1, h2, h3), gv, (own, place * HALF), (send, place * HALF))


def weight_grad_far(dv, rdv, hs):
    return pl.pallas_call(
        weight_grad_far_kernel,
        out_shape=(sds((2 * HALF, CORE_KV)),) * 2 + (sds((4 * ROWS, CORE_KV)),) + (sds((2 * ROWS, CORE_KV)),) * 2,
        in_specs=[VM] * 6,
        out_specs=(VM,) * 5,
        compiler_params=params(),
        cost_estimate=cost(512 * WIDE * 256, 4e6),
    )(dv, rdv, *hs)


def weight_grad_near_kernel(gv, h0, h1, h2, h3, send, own):
    for p, out in ((1, send), (0, own)):
        weight_grad_pair(p, (h0, h1, h2, h3), gv, (out, 0), (out, HALF))


def weight_grad_near(gv, hs):
    return pl.pallas_call(
        weight_grad_near_kernel,
        out_shape=(sds((2 * HALF, CORE_KV)),) * 2,
        in_specs=[VM] * 5,
        out_specs=(VM,) * 2,
        compiler_params=params(),
        cost_estimate=cost(512 * WIDE * 256, 4e6),
    )(gv, *hs)


def hidden_grad_kernel(gv, gvs, wp, wps, dk2, swapped, gh0, send_a, send_b):
    full = dot_nt(gv[...], wp[...]) + dot_nt(gvs[...], wps[...])
    full = full.astype(BF)
    gh0[...] = full[:ROWS]
    far = full[ROWS:]
    send_a[...] = far[:, : WIDE // 2]
    send_b[:, : WIDE // 2] = far[:, WIDE // 2 :]
    c = lax.axis_index("seq") % 2
    at = WIDE // 2
    send_b[:, pl.ds(pl.multiple_of(at + c * CORE_KV, CORE_KV), CORE_KV)] = dk2[...]
    send_b[:, pl.ds(pl.multiple_of(at + (1 - c) * CORE_KV, CORE_KV), CORE_KV)] = swapped[
        :, 2 * CORE_Q + CORE_KV :
    ]


def hidden_grad(gv, gvs, wp, wps, dk2, swapped):
    return pl.pallas_call(
        hidden_grad_kernel,
        out_shape=(sds((ROWS, WIDE)), sds((ROWS, WIDE // 2)), sds((ROWS, WIDE // 2 + 2 * CORE_KV))),
        in_specs=[VM] * 6,
        out_specs=(VM,) * 3,
        compiler_params=params(),
        cost_estimate=cost(2 * 256 * WIDE * 512, 6e6),
    )(gv, gvs, wp, wps, dk2, swapped)


def hidden_join_kernel(own_ref, far_a, far_b, dk0, swapped, o_ref, dk_ref, far_ref):
    far_ref[:, 0 : WIDE // 2] = far_a[...]
    far_ref[:, WIDE // 2 :] = far_b[:, : WIDE // 2]
    s = lax.axis_index("seq")
    y, c = s // 2, s % 2
    r = lax.axis_index("dp")
    low = first_half()
    for p in range(N_DP // 2):
        for i in range(2):
            base = (r ^ (2 * p + i)) * SHARD
            src = slice(p * SHARD + i * 256, p * SHARD + (i + 1) * 256)
            o_ref[:, pl.ds(pl.multiple_of(base + y * 384, 128), 256)] = own_ref[:, src]
            o_ref[:, pl.ds(pl.multiple_of(base + (1 - y) * 384, 128), 256)] = far_ref[:, src]
        own = own_ref[:, p * SHARD + 512 : (p + 1) * SHARD]
        far = far_ref[:, p * SHARD + 512 : (p + 1) * SHARD]
        part0 = jnp.where(y == 0, own, far)
        part1 = jnp.where(y == 0, far, own)
        at0 = pl.multiple_of((r ^ (2 * p)) * SHARD + 256, 128)
        at1 = pl.multiple_of((r ^ (2 * p + 1)) * SHARD + 256, 128)
        o_ref[:, pl.ds(at0, CHUNK)] = jnp.where(low, part0, turn(part1))
        o_ref[:, pl.ds(at1, CHUNK)] = jnp.where(low, turn(part0), part1)
    for place, near in ((c, dk0[...]), (1 - c, swapped[:, 2 * CORE_Q : 2 * CORE_Q + CORE_KV])):
        far = far_b[:, pl.ds(pl.multiple_of(WIDE // 2 + place * CORE_KV, CORE_KV), CORE_KV)]
        dk_ref[:, pl.ds(pl.multiple_of(place * CORE_KV, CORE_KV), CORE_KV)] = (
            near.astype(F32) + far.astype(F32)
        ).astype(BF)


def hidden_join(own, fars, dk0, swapped):
    return pl.pallas_call(
        hidden_join_kernel,
        out_shape=(sds((ROWS, N_DP * SHARD)), sds((ROWS, 2 * CORE_KV))),
        in_specs=[VM] * 5,
        out_specs=(VM, VM),
        scratch_shapes=[pltpu.VMEM((ROWS, WIDE), BF)],
        compiler_params=params(),
        cost_estimate=cost(0, 3e6),
    )(own, *fars, dk0, swapped)


def heads_join_kernel(o0, dq0, swapped, o_ref, dq_ref):
    c = lax.axis_index("seq") % 2
    near = pl.ds(pl.multiple_of(c * CORE_Q, CORE_Q), CORE_Q)
    far = pl.ds(pl.multiple_of((1 - c) * CORE_Q, CORE_Q), CORE_Q)
    o_ref[:, near] = o0[...]
    o_ref[:, far] = swapped[:, 0:CORE_Q]
    dq_ref[:, near] = dq0[...]
    dq_ref[:, far] = swapped[:, CORE_Q : 2 * CORE_Q]


def heads_join(o0, dq0, swapped):
    return pl.pallas_call(
        heads_join_kernel,
        out_shape=(sds((ROWS, 2 * CORE_Q)),) * 2,
        in_specs=[VM] * 3,
        out_specs=(VM,) * 2,
        compiler_params=params(),
        cost_estimate=cost(0, 4e6),
    )(o0, dq0, swapped)


def add_pair_kernel(a, b, o0, o1):
    total = (a[...].astype(F32) + b[...].astype(F32)).astype(BF)
    o0[...] = total[:HALF]
    o1[...] = total[HALF:]


def add_pair(a, b):
    return pl.pallas_call(
        add_pair_kernel,
        out_shape=(sds((HALF, CORE_KV)),) * 2,
        in_specs=[VM] * 2,
        out_specs=(VM,) * 2,
        compiler_params=params(),
        cost_estimate=cost(0, 1e6),
    )(a, b)


def add_two_kernel(a, b, o):
    o[...] = a[...].astype(F32) + b[...].astype(F32)


def add_two(a, b):
    return pl.pallas_call(
        add_two_kernel,
        out_shape=sds((HALF, CORE_KV), F32),
        in_specs=[VM] * 2,
        out_specs=VM,
        compiler_params=params(),
        cost_estimate=cost(0, 1e6),
    )(a, b)


def add_three_kernel(a, b, c, o):
    o[...] = (a[...] + (b[...].astype(F32) + c[...].astype(F32))).astype(BF)


def add_three(a, b, c):
    return pl.pallas_call(
        add_three_kernel,
        out_shape=sds((HALF, CORE_KV)),
        in_specs=[VM] * 3,
        out_specs=VM,
        compiler_params=params(),
        cost_estimate=cost(0, 1e6),
    )(a, b, c)


def weight_join_kernel(p0, p1, p2, p3, o_ref):
    s = lax.axis_index("seq")
    for t, p in enumerate((p0, p1, p2, p3)):
        y, c = (s ^ t) // 2, (s ^ t) % 2
        cols = pl.ds(pl.multiple_of(c * CORE_KV, CORE_KV), CORE_KV)
        o_ref[pl.ds(pl.multiple_of(y * 384, 128), 256), cols] = p[0:256, :].astype(F32)
        o_ref[pl.ds(pl.multiple_of(256 + y * 64, 64), 64), cols] = p[256:HALF, :].astype(F32)


def weight_join(ps):
    return pl.pallas_call(
        weight_join_kernel,
        out_shape=sds((SHARD, 2 * CORE_KV), F32),
        in_specs=[VM] * 4,
        out_specs=VM,
        compiler_params=params(),
        cost_estimate=cost(0, 2e6),
    )(*ps)


def paired_body(hidden, queries, keys, value_weight, doc_ids, cotangent):
    q, g = queries[0], cotangent[0]
    send, p0, w0 = pack(hidden[0], keys[0], doc_ids, value_weight, q, g)
    p2 = swap(send, "seq", 2)
    w6, w4, w2 = swap(w0, "dp", 6), swap(w0, "dp", 4), swap(w0, "dp", 2)
    w1 = swap(w0, "dp", 1)
    w3 = swap(w1, "dp", 2)
    p1 = swap(p0, "seq", 1)
    w7, w5 = swap(w6, "dp", 1), swap(after(w4, w2), "dp", 1)
    p3 = swap(after(p2, w1, w3, w5, w7), "seq", 1)
    ps = (p0, p1, p2, p3)
    vp3, wp = partial_values((p0, p1, p2), (w0, w1, w2, w3, w4, w5, w6, w7))
    vp = last_values(vp3, p3, wp)
    rv = swap(vp, "seq", 2)
    e, inv = scores(after(q, vp), ps)
    wps = swap(wp, "seq", 1)
    o0, dq0, dk0, dk2, swap_out, dv = attention(e, inv, q, g, ps, vp, rv)
    rdv = swap(dv, "seq", 2)
    send_a, own_a, gv, gv_keep, gv_send = weight_grad_far(dv, rdv, ps)
    send_b, own_b = weight_grad_near(gv, ps)
    far_a = swap(send_a, "dp", 1)
    far_b = swap(send_b, "dp", 2)
    gvs = swap(after(gv_send, send_b), "seq", 1)
    swapped = swap(swap_out, "seq", 1)
    gh0, gh_a, gh_b = hidden_grad(gv_keep, gvs, wp, wps, dk2, swapped)
    s4, s6 = add_pair(own_a, far_a)
    t6, t4 = swap(s6, "dp", 6), swap(s4, "dp", 4)
    t46 = add_two(t4, t6)
    s0, s1 = add_pair(own_b, far_b)
    t1 = swap(s1, "dp", 1)
    gh_far = swap(gh_a, "seq", 2), swap(gh_b, "seq", 2)
    attn_out, grad_queries = heads_join(o0, dq0, swapped)
    d0 = add_three(t46, s0, t1)
    d2 = swap(d0, "seq", 2)
    d1 = swap(d0, "seq", 1)
    grad_hidden, grad_keys = hidden_join(gh0, gh_far, dk0, swapped)
    d2, grad_hidden, grad_keys, attn_out, grad_queries = lax.optimization_barrier(
        (d2, grad_hidden, grad_keys, attn_out, grad_queries)
    )
    d3 = swap(d2, "seq", 1)
    grad_weight = weight_join((d0, d1, d2, d3))
    return attn_out[None], grad_queries[None], grad_keys[None], grad_hidden[None], grad_weight


def solution(mesh):
    in_specs = (
        P("dp", "seq", None),
        P("dp", "seq", None),
        P("dp", "seq", None),
        P("dp", None),
        P("dp", "seq"),
        P("dp", "seq", None),
    )
    out_specs = (
        P("dp", "seq", None),
        P("dp", "seq", None),
        P("dp", "seq", None),
        P("dp", "seq", None),
        P("dp", None),
    )
    paired = mesh.shape["dp"] == N_DP and mesh.shape["seq"] == 4
    return jax.shard_map(
        paired_body if paired else body, mesh=mesh, in_specs=in_specs, out_specs=out_specs, check_vma=False
    )
```

```python
import functools

import jax
import jax.numpy as jnp
from jax import lax
from jax.experimental import pallas as pl
from jax.experimental.pallas import tpu as pltpu
from jax.sharding import PartitionSpec as P

QUERY_HEADS = 20
KEY_VALUE_HEADS = 4
HEAD_SIZE = 128
QUERY_PER_KV = 5

BF = jnp.bfloat16
F32 = jnp.float32
VM = pl.BlockSpec(memory_space=pltpu.VMEM)
ANY = pl.BlockSpec(memory_space=pl.ANY)


def body(hidden, queries, keys, value_weight, doc_ids, cotangent):
    tokens = hidden[0]
    row_count = tokens.shape[0]
    width = value_weight.shape[1]
    scale = HEAD_SIZE ** (-0.5)
    shard_list = lax.axis_size("seq")
    my_index = lax.axis_index("seq")
    full_weight = lax.all_gather(value_weight, "dp", axis=0, tiled=True)
    values_sum = jnp.dot(tokens, full_weight, preferred_element_type=jnp.float32)
    values = values_sum.astype(jnp.bfloat16)
    every_key, every_value, all_docs = (
        lax.all_gather(keys[0], "seq", axis=0, tiled=True),
        lax.all_gather(values, "seq", axis=0, tiled=True),
        lax.all_gather(doc_ids[0], "seq", axis=0, tiled=True),
    )
    query_head_rows = queries[0].reshape(row_count, KEY_VALUE_HEADS, QUERY_PER_KV, HEAD_SIZE)
    gradient_heads = cotangent[0].reshape(row_count, KEY_VALUE_HEADS, QUERY_PER_KV, HEAD_SIZE)
    query_docs = doc_ids[0]
    query_pos = my_index * row_count + jnp.arange(row_count, dtype=jnp.int32)
    local_pos = jnp.arange(row_count, dtype=jnp.int32)

    def block_scores(shard):
        start_offset = shard * row_count
        key_tile = lax.dynamic_slice_in_dim(every_key, start_offset, row_count, 0).reshape(
            row_count, KEY_VALUE_HEADS, HEAD_SIZE
        )
        value_tile = lax.dynamic_slice_in_dim(every_value, start_offset, row_count, 0).reshape(
            row_count, KEY_VALUE_HEADS, HEAD_SIZE
        )
        doc_block = lax.dynamic_slice_in_dim(all_docs, start_offset, row_count, 0)
        scores = (
            jnp.einsum(
                "qhgd,khd->hgqk", query_head_rows, key_tile, preferred_element_type=jnp.float32
            )
            * scale
        )
        allow = ((start_offset + local_pos)[None, :] <= query_pos[:, None]) & (
            doc_block[None, :] == query_docs[:, None]
        )
        return (jnp.where(allow, scores, -1e30), allow, key_tile, value_tile)

    def forward_step(shard, carry):
        peak, total, out_acc = carry
        masked, allow, key_tile, value_tile = block_scores(shard)
        new_peak = jnp.maximum(peak, jnp.max(masked, axis=-1))
        expd = jnp.where(allow, jnp.exp(masked - new_peak[..., None]), 0.0)
        factor = jnp.exp(peak - new_peak)
        total = total * factor + jnp.sum(expd, axis=-1)
        out_acc = out_acc * factor[..., None] + jnp.einsum(
            "hgqk,khd->hgqd",
            expd.astype(jnp.bfloat16),
            value_tile,
            preferred_element_type=jnp.float32,
        )
        return (new_peak, total, out_acc)

    head_layout = (KEY_VALUE_HEADS, QUERY_PER_KV, row_count)
    start_state = (
        jnp.full(head_layout, -1e30, jnp.float32),
        jnp.zeros(head_layout, jnp.float32),
        jnp.zeros((KEY_VALUE_HEADS, QUERY_PER_KV, row_count, HEAD_SIZE), jnp.float32),
    )
    peak, total, out_acc = lax.fori_loop(0, shard_list, forward_step, start_state)
    attn_b = (out_acc / total[..., None]).astype(jnp.bfloat16).transpose(2, 0, 1, 3)
    delta = jnp.sum(
        gradient_heads.astype(jnp.float32) * attn_b.astype(jnp.float32), axis=-1
    ).transpose(1, 2, 0)

    def gradient_update(shard, carry):
        dq_acc, grad_buf = carry
        masked, allow, key_tile, value_tile = block_scores(shard)
        probs = jnp.where(allow, jnp.exp(masked - peak[..., None]), 0.0) / total[..., None]
        probs_b = probs.astype(jnp.bfloat16)
        dprob = jnp.einsum(
            "qhgd,khd->hgqk", gradient_heads, value_tile, preferred_element_type=jnp.float32
        )
        dscore = (probs * (dprob - delta[..., None])).astype(jnp.bfloat16)
        dq_acc = dq_acc + jnp.einsum(
            "hgqk,khd->qhgd", dscore, key_tile, preferred_element_type=jnp.float32
        )
        dk_block = (
            jnp.einsum(
                "hgqk,qhgd->khd", dscore, query_head_rows, preferred_element_type=jnp.float32
            )
            * scale
        ).astype(jnp.bfloat16)
        dv_block = jnp.einsum(
            "hgqk,qhgd->khd", probs_b, gradient_heads, preferred_element_type=jnp.float32
        ).astype(jnp.bfloat16)
        paired = jnp.concatenate(
            (dk_block.reshape(row_count, width), dv_block.reshape(row_count, width)), axis=1
        )
        grad_buf = lax.dynamic_update_slice_in_dim(grad_buf, paired, shard * row_count, 0)
        return (dq_acc, grad_buf)

    blank_buffer = jnp.zeros((row_count * shard_list, 2 * width), jnp.bfloat16)
    dq_acc, grad_buf = lax.fori_loop(
        0,
        shard_list,
        gradient_update,
        (
            jnp.zeros((row_count, KEY_VALUE_HEADS, QUERY_PER_KV, HEAD_SIZE), jnp.float32),
            blank_buffer,
        ),
    )
    grad_queries = (dq_acc * scale).astype(jnp.bfloat16).reshape(row_count, QUERY_HEADS * HEAD_SIZE)
    summed = lax.psum_scatter(
        grad_buf.astype(jnp.float32).astype(jnp.bfloat16), "seq", scatter_dimension=0, tiled=True
    ).astype(jnp.float32)
    grad_keys = summed[:, :width].astype(jnp.bfloat16)
    grad_values = summed[:, width:].astype(jnp.bfloat16)
    grad_hidden = jnp.einsum(
        "kc,dc->kd", grad_values, full_weight, preferred_element_type=jnp.float32
    ).astype(jnp.bfloat16)
    partial_rows = lax.psum_scatter(
        jnp.einsum("kd,kc->dc", tokens, grad_values, preferred_element_type=jnp.float32).astype(
            jnp.bfloat16
        ),
        "dp",
        scatter_dimension=0,
        tiled=True,
    )
    grad_weight = lax.psum(partial_rows, "seq").astype(jnp.float32)
    return (
        attn_b.reshape(row_count, QUERY_HEADS * HEAD_SIZE)[None],
        grad_queries[None],
        grad_keys[None],
        grad_hidden[None],
        grad_weight,
    )


N_DP = 8
ROWS = 128
SHARD = 640
HALF = SHARD // 2
CHUNK = 128
WIDE = N_DP * HALF
CORE_KV = 256
SPARE = 16
CUT = 768
CORE_Q = 1280
KEY_AT = WIDE
DOC_AT = KEY_AT + 512
QUERY_AT = DOC_AT + ROWS
COT_AT = QUERY_AT + CORE_Q
PACK = COT_AT + CORE_Q


def params(mib=32):
    return pltpu.CompilerParams(vmem_limit_bytes=mib * 1024 * 1024)


def cost(flops, nbytes):
    return pl.CostEstimate(flops=int(flops), bytes_accessed=int(nbytes), transcendentals=0)


def sds(shape, dtype=BF):
    return jax.ShapeDtypeStruct(shape, dtype)


def swap(x, axis, k):
    size = lax.axis_size(axis)
    return lax.ppermute(x, axis, [(i, i ^ k) for i in range(size)])


def after(x, *others):
    return lax.optimization_barrier((x, *others))[0]


def dot_tt(a, b):
    return lax.dot_general(a, b, (((0,), (0,)), ((), ())), preferred_element_type=F32)


def dot_nt(a, b):
    return lax.dot_general(a, b, (((1,), (1,)), ((), ())), preferred_element_type=F32)


def turn(x):
    return pltpu.roll(x.astype(F32), CHUNK // 2, 1).astype(x.dtype)


def first_half():
    return lax.broadcasted_iota(jnp.int32, (ROWS, CHUNK), 1) < CHUNK // 2


def pack_kernel(h, k, doc, w, q, g, send, keep, w0):
    s = lax.axis_index("seq")
    r = lax.axis_index("dp")
    y, c = s // 2, s % 2
    cols = pl.ds(pl.multiple_of(c * CORE_KV, CORE_KV), CORE_KV)
    w0[0:256, :] = w[pl.ds(pl.multiple_of(y * 384, 128), 256), cols]
    w0[256:HALF, :] = w[pl.ds(pl.multiple_of(256 + y * 64, 64), 64), cols]
    low = first_half()
    for out, part in ((send, 1 - y), (keep, y)):
        for p in range(N_DP // 2):
            mids = []
            for i in range(2):
                base = (r ^ (2 * p + i)) * SHARD
                start = pl.multiple_of(base + part * 384, 128)
                out[:, p * SHARD + i * 256 : p * SHARD + (i + 1) * 256] = h[:, pl.ds(start, 256)]
                mid = h[:, pl.ds(pl.multiple_of(base + 256, 128), CHUNK)]
                mids.append(jnp.where(part == i, mid, turn(mid)))
            out[:, p * SHARD + 512 : (p + 1) * SHARD] = jnp.where(low, mids[0], mids[1])
        out[:, KEY_AT:DOC_AT] = k[...]
        out[:, DOC_AT:QUERY_AT] = jnp.broadcast_to(doc[...].astype(F32), (ROWS, ROWS)).astype(BF)
    other = pl.ds(pl.multiple_of((1 - c) * CORE_Q, CORE_Q), CORE_Q)
    keep[:, QUERY_AT:COT_AT] = q[:, other]
    keep[:, COT_AT:PACK] = g[:, other]


def pack(h, k, doc, w, q, g):
    return pl.pallas_call(
        pack_kernel,
        out_shape=(sds((ROWS, QUERY_AT)), sds((ROWS, PACK)), sds((HALF, CORE_KV))),
        in_specs=[VM] * 6,
        out_specs=(VM,) * 3,
        compiler_params=params(60),
        cost_estimate=cost(0, 3e6),
    )(h, k, doc, w, q, g)


def relay_kernel(p, w, own, ow):
    own[...] = p[:, 0:QUERY_AT]
    ow[...] = w[...]


def relay(p, w):
    return pl.pallas_call(
        relay_kernel,
        out_shape=(sds((ROWS, QUERY_AT)), sds((HALF, CORE_KV))),
        in_specs=[VM] * 2,
        out_specs=(VM,) * 2,
        compiler_params=params(),
        cost_estimate=cost(0, 4e6),
    )(p, w)


def values_kernel(h0, h1, h2, w0, w1, w2, w3, w4, w5, w6, w7, vp_ref, wp_ref):
    ws = (w0, w1, w2, w3, w4, w5, w6, w7)
    for p in range(N_DP // 2):
        a, b = ws[2 * p], ws[2 * p + 1]
        base = p * SHARD
        wp_ref[base : base + 256, :] = a[0:256, :]
        wp_ref[base + 256 : base + 512, :] = b[0:256, :]
        wp_ref[base + 512 : base + 576, :] = a[256:HALF, :]
        wp_ref[base + 576 : base + 640, :] = b[256:HALF, :]
    for t, h in enumerate((h0, h1, h2)):
        vp_ref[t * ROWS : (t + 1) * ROWS, :] = jnp.dot(
            h[:, 0:WIDE], wp_ref[...], preferred_element_type=F32
        ).astype(BF)


def partial_values(hs, ws):
    return pl.pallas_call(
        values_kernel,
        out_shape=(sds((3 * ROWS, CORE_KV)), sds((WIDE, CORE_KV))),
        in_specs=[VM] * 11,
        out_specs=(VM, VM),
        compiler_params=params(),
        cost_estimate=cost(2 * 384 * WIDE * 256, 6e6),
    )(*hs, *ws)


def last_values_kernel(vp, h3, wp, o0, o1):
    last = jnp.dot(h3[:, 0:WIDE], wp[...], preferred_element_type=F32).astype(BF)
    for i, o in enumerate((o0, o1)):
        cols = slice(i * HEAD_SIZE, (i + 1) * HEAD_SIZE)
        o[0 : 3 * ROWS, :] = vp[:, cols]
        o[3 * ROWS :, :] = last[:, cols]


def last_values(vp, h3, wp):
    return pl.pallas_call(
        last_values_kernel,
        out_shape=(sds((4 * ROWS, HEAD_SIZE)),) * 2,
        in_specs=[VM] * 3,
        out_specs=(VM,) * 2,
        compiler_params=params(),
        cost_estimate=cost(2 * 128 * WIDE * 256, 2e6),
    )(vp, h3, wp)


def scores_kernel(q0, p0, p1, p2, p3, e_ref, inv_ref, bias):
    s = lax.axis_index("seq")
    c = s % 2
    factor = HEAD_SIZE ** (-0.5)
    log2e = 1.4426950408889634
    ps = (p0, p1, p2, p3)
    rows = [p[0:16, DOC_AT:QUERY_AT][0:1, :].astype(F32) for p in ps]
    for t in range(4):
        key_doc = jnp.transpose(jnp.broadcast_to(rows[t], (ROWS, ROWS)))
        key_pos = (s ^ t) * ROWS + lax.broadcasted_iota(jnp.int32, (ROWS, ROWS), 0)
        for u in range(2):
            query_pos = (s ^ u) * ROWS + lax.broadcasted_iota(jnp.int32, (ROWS, ROWS), 1)
            allow = (key_pos <= query_pos) & (key_doc == jnp.broadcast_to(rows[u], (ROWS, ROWS)))
            bias[t * ROWS : (t + 1) * ROWS, u * ROWS : (u + 1) * ROWS] = jnp.where(allow, 0.0, -1e30)
    for kvh in range(2):
        cols = pl.ds(pl.multiple_of(KEY_AT + c * CORE_KV + kvh * HEAD_SIZE, HEAD_SIZE), HEAD_SIZE)
        key = jnp.concatenate([p[:, cols] for p in ps], axis=0)
        for i in range(QUERY_PER_KV):
            head = kvh * QUERY_PER_KV + i
            qcols = pl.ds(pl.multiple_of(c * CORE_Q + head * HEAD_SIZE, HEAD_SIZE), HEAD_SIZE)
            far = p1[:, QUERY_AT + head * HEAD_SIZE : QUERY_AT + (head + 1) * HEAD_SIZE]
            query = jnp.concatenate([q0[:, qcols], far], axis=0)
            st = dot_nt(key, query) * (factor * log2e) + bias[...]
            e = jnp.exp2(st - jnp.max(st, axis=0, keepdims=True))
            inv_ref[head * 8 : head * 8 + 8, :] = jnp.broadcast_to(
                1.0 / jnp.sum(e, axis=0, keepdims=True), (8, 2 * ROWS)
            )
            e_ref[head] = e.astype(BF)


def scores(q, ps):
    return pl.pallas_call(
        scores_kernel,
        out_shape=(sds((10, 4 * ROWS, 2 * ROWS)), sds((80, 2 * ROWS), F32)),
        in_specs=[VM] * 5,
        out_specs=(VM,) * 2,
        scratch_shapes=[pltpu.VMEM((4 * ROWS, 2 * ROWS), F32)],
        compiler_params=params(),
        cost_estimate=cost(2 * 10 * 256 * 512 * 128 * 8, 6e6),
    )(q, *ps)


def attend_head(kvh, e_ref, inv_ref, q0, g0, ps, vp, rv):
    c = lax.axis_index("seq") % 2
    factor = HEAD_SIZE ** (-0.5)
    p1 = ps[1]
    cols = pl.ds(pl.multiple_of(KEY_AT + c * CORE_KV + kvh * HEAD_SIZE, HEAD_SIZE), HEAD_SIZE)
    key = jnp.concatenate([p[:, cols] for p in ps], axis=0)
    far = rv[...].astype(F32)
    far = jnp.concatenate([far[2 * ROWS :], far[: 2 * ROWS]], axis=0)
    value = (vp[...].astype(F32) + far).astype(BF)
    dk = jnp.zeros((4 * ROWS, HEAD_SIZE), F32)
    dv = jnp.zeros((4 * ROWS, HEAD_SIZE), F32)
    outs = []
    for i in range(QUERY_PER_KV):
        head = kvh * QUERY_PER_KV + i
        qcols = pl.ds(pl.multiple_of(c * CORE_Q + head * HEAD_SIZE, HEAD_SIZE), HEAD_SIZE)
        low, high = head * HEAD_SIZE, (head + 1) * HEAD_SIZE
        query = jnp.concatenate([q0[:, qcols], p1[:, QUERY_AT + low : QUERY_AT + high]], axis=0)
        cot = jnp.concatenate([g0[:, qcols], p1[:, COT_AT + low : COT_AT + high]], axis=0)
        e = e_ref[head]
        inv = inv_ref[head * 8 : head * 8 + 8, :][0:1, :]
        out = jnp.transpose(dot_tt(value, e) * inv).astype(BF)
        probs = e.astype(F32) * inv
        term = probs * dot_nt(value, cot)
        delta = jnp.sum(term, axis=0, keepdims=True)
        ds = (term - probs * delta).astype(BF)
        dq = jnp.transpose(dot_tt(key, ds) * factor).astype(BF)
        outs.append((out, dq))
        dk = dk + jnp.dot(ds, query, preferred_element_type=F32)
        dv = dv + jnp.dot(probs.astype(BF), cot, preferred_element_type=F32)
    return outs, (dk * factor).astype(BF), dv.astype(BF)


def attention_first_kernel(e_ref, inv_ref, q0, g0, p0, p1, p2, p3, vp, rv, out, dk_ref, dv_ref):
    outs, dk, dv = attend_head(0, e_ref, inv_ref, q0, g0, (p0, p1, p2, p3), vp, rv)
    for i, (o, dq) in enumerate(outs):
        cols = slice(i * HEAD_SIZE, (i + 1) * HEAD_SIZE)
        out[0 : 2 * ROWS, cols] = o
        out[2 * ROWS :, cols] = dq
    dk_ref[...] = dk
    dv_ref[0 : 4 * ROWS, :] = dv
    dv_ref[4 * ROWS :, :] = jnp.zeros((SPARE, HEAD_SIZE), BF)


def attention_second_kernel(
    e_ref, inv_ref, q0, g0, p0, p1, p2, p3, vp, rv, first, first_dk,
    o0, dq0, dk0, dk2, swap_ref, dv_ref,
):
    outs, dk, dv = attend_head(1, e_ref, inv_ref, q0, g0, (p0, p1, p2, p3), vp, rv)
    half = QUERY_PER_KV * HEAD_SIZE
    o0[:, 0:half] = first[0:ROWS, :]
    swap_ref[:, 0:half] = first[ROWS : 2 * ROWS, :]
    dq0[:, 0:half] = first[2 * ROWS : 3 * ROWS, :]
    swap_ref[:, CORE_Q : CORE_Q + half] = first[3 * ROWS :, :]
    for i, (o, dq) in enumerate(outs):
        low, high = half + i * HEAD_SIZE, half + (i + 1) * HEAD_SIZE
        o0[:, low:high] = o[:ROWS]
        swap_ref[:, low:high] = o[ROWS:]
        dq0[:, low:high] = dq[:ROWS]
        swap_ref[:, CORE_Q + low : CORE_Q + high] = dq[ROWS:]
    for kvh, d in enumerate((first_dk[...], dk)):
        mine = slice(kvh * HEAD_SIZE, (kvh + 1) * HEAD_SIZE)
        dk0[:, mine] = d[:ROWS]
        dk2[:, mine] = d[2 * ROWS : 3 * ROWS]
        at = 2 * CORE_Q + kvh * HEAD_SIZE
        swap_ref[:, at : at + HEAD_SIZE] = d[ROWS : 2 * ROWS]
        swap_ref[:, at + CORE_KV : at + CORE_KV + HEAD_SIZE] = d[3 * ROWS :]
    dv_ref[...] = dv


def attention_first(*args):
    return pl.pallas_call(
        attention_first_kernel,
        out_shape=(
            sds((4 * ROWS, QUERY_PER_KV * HEAD_SIZE)), sds((4 * ROWS, HEAD_SIZE)),
            sds((4 * ROWS + SPARE, HEAD_SIZE)),
        ),
        in_specs=[VM] * 10,
        out_specs=(VM,) * 3,
        compiler_params=params(),
        cost_estimate=cost(5 * 10 * 256 * 512 * 128 * 4, 3e6),
    )(*args)


def attention_second(*args):
    return pl.pallas_call(
        attention_second_kernel,
        out_shape=(sds((ROWS, CORE_Q)),) * 2
        + (sds((ROWS, CORE_KV)),) * 2
        + (sds((ROWS, 2 * CORE_Q + 2 * CORE_KV)), sds((4 * ROWS, HEAD_SIZE))),
        in_specs=[VM] * 12,
        out_specs=(VM,) * 6,
        compiler_params=params(),
        cost_estimate=cost(5 * 10 * 256 * 512 * 128 * 4, 3e6),
    )(*args)


def weight_grad_pair(p, hs, gv, even, odd):
    for (out, at), start in ((even, 0), (odd, 256)):
        acc = jnp.zeros((256, CORE_KV), F32)
        for t, h in enumerate(hs):
            first = p * SHARD + start
            acc = acc + dot_tt(h[:, first : first + 256], gv[t * ROWS : (t + 1) * ROWS, :])
        out[at : at + 256, :] = acc.astype(BF)
    acc = jnp.zeros((CHUNK, CORE_KV), F32)
    for t, h in enumerate(hs):
        acc = acc + dot_tt(h[:, p * SHARD + 512 : (p + 1) * SHARD], gv[t * ROWS : (t + 1) * ROWS, :])
    acc = acc.astype(BF)
    for (out, at), half in ((even, acc[:64]), (odd, acc[64:])):
        out[at + 256 : at + HALF, :] = half


def value_grad_kernel(dv0, dv1, rdv0, rdv1, gv, gv_keep, gv_send):
    for t in range(4):
        parts = []
        for dv, rdv in ((dv0, rdv0), (dv1, rdv1)):
            a = dv[t * ROWS : (t + 1) * ROWS, :].astype(F32)
            b = rdv[(t ^ 2) * ROWS : ((t ^ 2) + 1) * ROWS, :].astype(F32)
            parts.append(a + b)
        total = jnp.concatenate(parts, axis=1).astype(BF)
        gv[t * ROWS : (t + 1) * ROWS, :] = total
        half = (t // 2) * ROWS
        if t % 2 == 0:
            gv_keep[half : half + ROWS, :] = total
        else:
            gv_send[half : half + ROWS, :] = total


def value_grad(dvs, rdvs):
    return pl.pallas_call(
        value_grad_kernel,
        out_shape=(sds((4 * ROWS, CORE_KV)),) + (sds((2 * ROWS, CORE_KV)),) * 2,
        in_specs=[VM] * 4,
        out_specs=(VM,) * 3,
        compiler_params=params(),
        cost_estimate=cost(0, 1e6),
    )(*dvs, *rdvs)


def weight_grad_far_kernel(gv, h0, h1, h2, h3, send, own):
    for place, p in enumerate((2, 3)):
        weight_grad_pair(p, (h0, h1, h2, h3), gv, (own, place * HALF), (send, place * HALF))


def weight_grad_far(gv, hs):
    return pl.pallas_call(
        weight_grad_far_kernel,
        out_shape=(sds((2 * HALF, CORE_KV)),) * 2,
        in_specs=[VM] * 5,
        out_specs=(VM,) * 2,
        compiler_params=params(),
        cost_estimate=cost(512 * WIDE * 256, 4e6),
    )(gv, *hs)


def weight_grad_near_kernel(gv, h0, h1, h2, h3, send, own):
    for p, out in ((1, send), (0, own)):
        weight_grad_pair(p, (h0, h1, h2, h3), gv, (out, 0), (out, HALF))


def weight_grad_near(gv, hs):
    return pl.pallas_call(
        weight_grad_near_kernel,
        out_shape=(sds((2 * HALF, CORE_KV)),) * 2,
        in_specs=[VM] * 5,
        out_specs=(VM,) * 2,
        compiler_params=params(),
        cost_estimate=cost(512 * WIDE * 256, 4e6),
    )(gv, *hs)


def hidden_grad_kernel(gv, gvs, wp, wps, dk2, swapped, gh0, send_a, send_b):
    full = dot_nt(gv[...], wp[...]) + dot_nt(gvs[...], wps[...])
    full = full.astype(BF)
    gh0[...] = full[:ROWS]
    far = full[ROWS:]
    send_a[...] = far[:, : CUT]
    send_b[:, : WIDE - CUT] = far[:, CUT :]
    c = lax.axis_index("seq") % 2
    at = WIDE - CUT
    send_b[:, pl.ds(pl.multiple_of(at + c * CORE_KV, CORE_KV), CORE_KV)] = dk2[...]
    send_b[:, pl.ds(pl.multiple_of(at + (1 - c) * CORE_KV, CORE_KV), CORE_KV)] = swapped[
        :, 2 * CORE_Q + CORE_KV :
    ]


def hidden_grad(gv, gvs, wp, wps, dk2, swapped):
    return pl.pallas_call(
        hidden_grad_kernel,
        out_shape=(sds((ROWS, WIDE)), sds((ROWS, CUT)), sds((ROWS, WIDE - CUT + 2 * CORE_KV))),
        in_specs=[VM] * 6,
        out_specs=(VM,) * 3,
        compiler_params=params(),
        cost_estimate=cost(2 * 256 * WIDE * 512, 6e6),
    )(gv, gvs, wp, wps, dk2, swapped)


def hidden_join_kernel(own_ref, far_a, far_b, dk0, swapped, o_ref, dk_ref, far_ref):
    far_ref[:, 0:CUT] = far_a[...]
    far_ref[:, CUT:] = far_b[:, : WIDE - CUT]
    s = lax.axis_index("seq")
    y, c = s // 2, s % 2
    r = lax.axis_index("dp")
    low = first_half()
    for p in range(N_DP // 2):
        for i in range(2):
            base = (r ^ (2 * p + i)) * SHARD
            src = slice(p * SHARD + i * 256, p * SHARD + (i + 1) * 256)
            o_ref[:, pl.ds(pl.multiple_of(base + y * 384, 128), 256)] = own_ref[:, src]
            o_ref[:, pl.ds(pl.multiple_of(base + (1 - y) * 384, 128), 256)] = far_ref[:, src]
        own = own_ref[:, p * SHARD + 512 : (p + 1) * SHARD]
        far = far_ref[:, p * SHARD + 512 : (p + 1) * SHARD]
        part0 = jnp.where(y == 0, own, far)
        part1 = jnp.where(y == 0, far, own)
        at0 = pl.multiple_of((r ^ (2 * p)) * SHARD + 256, 128)
        at1 = pl.multiple_of((r ^ (2 * p + 1)) * SHARD + 256, 128)
        o_ref[:, pl.ds(at0, CHUNK)] = jnp.where(low, part0, turn(part1))
        o_ref[:, pl.ds(at1, CHUNK)] = jnp.where(low, turn(part0), part1)
    for place, near in ((c, dk0[...]), (1 - c, swapped[:, 2 * CORE_Q : 2 * CORE_Q + CORE_KV])):
        far = far_b[:, pl.ds(pl.multiple_of(WIDE - CUT + place * CORE_KV, CORE_KV), CORE_KV)]
        dk_ref[:, pl.ds(pl.multiple_of(place * CORE_KV, CORE_KV), CORE_KV)] = (
            near.astype(F32) + far.astype(F32)
        ).astype(BF)


def hidden_join(own, fars, dk0, swapped):
    return pl.pallas_call(
        hidden_join_kernel,
        out_shape=(sds((ROWS, N_DP * SHARD)), sds((ROWS, 2 * CORE_KV))),
        in_specs=[VM] * 5,
        out_specs=(VM, VM),
        scratch_shapes=[pltpu.VMEM((ROWS, WIDE), BF)],
        compiler_params=params(),
        cost_estimate=cost(0, 3e6),
    )(own, *fars, dk0, swapped)


def heads_join_kernel(o0, dq0, swapped, o_ref, dq_ref):
    c = lax.axis_index("seq") % 2
    near = pl.ds(pl.multiple_of(c * CORE_Q, CORE_Q), CORE_Q)
    far = pl.ds(pl.multiple_of((1 - c) * CORE_Q, CORE_Q), CORE_Q)
    o_ref[:, near] = o0[...]
    o_ref[:, far] = swapped[:, 0:CORE_Q]
    dq_ref[:, near] = dq0[...]
    dq_ref[:, far] = swapped[:, CORE_Q : 2 * CORE_Q]


def heads_join(o0, dq0, swapped):
    return pl.pallas_call(
        heads_join_kernel,
        out_shape=(sds((ROWS, 2 * CORE_Q)),) * 2,
        in_specs=[VM] * 3,
        out_specs=(VM,) * 2,
        compiler_params=params(),
        cost_estimate=cost(0, 4e6),
    )(o0, dq0, swapped)


def add_pair_kernel(a, b, o0, o1):
    total = (a[...].astype(F32) + b[...].astype(F32)).astype(BF)
    o0[...] = total[:HALF]
    o1[...] = total[HALF:]


def add_pair(a, b):
    return pl.pallas_call(
        add_pair_kernel,
        out_shape=(sds((HALF, CORE_KV)),) * 2,
        in_specs=[VM] * 2,
        out_specs=(VM,) * 2,
        compiler_params=params(),
        cost_estimate=cost(0, 1e6),
    )(a, b)


def add_two_kernel(a, b, o):
    o[...] = a[...].astype(F32) + b[...].astype(F32)


def add_two(a, b):
    return pl.pallas_call(
        add_two_kernel,
        out_shape=sds((HALF, CORE_KV), F32),
        in_specs=[VM] * 2,
        out_specs=VM,
        compiler_params=params(),
        cost_estimate=cost(0, 1e6),
    )(a, b)


def add_three_kernel(a, b, c, o):
    o[...] = (a[...] + (b[...].astype(F32) + c[...].astype(F32))).astype(BF)


def add_three(a, b, c):
    return pl.pallas_call(
        add_three_kernel,
        out_shape=sds((HALF, CORE_KV)),
        in_specs=[VM] * 3,
        out_specs=VM,
        compiler_params=params(),
        cost_estimate=cost(0, 1e6),
    )(a, b, c)


def weight_join_kernel(p0, p1, p2, p3, o_ref):
    s = lax.axis_index("seq")
    for t, p in enumerate((p0, p1, p2, p3)):
        y, c = (s ^ t) // 2, (s ^ t) % 2
        cols = pl.ds(pl.multiple_of(c * CORE_KV, CORE_KV), CORE_KV)
        o_ref[pl.ds(pl.multiple_of(y * 384, 128), 256), cols] = p[0:256, :].astype(F32)
        o_ref[pl.ds(pl.multiple_of(256 + y * 64, 64), 64), cols] = p[256:HALF, :].astype(F32)


def weight_join(ps):
    return pl.pallas_call(
        weight_join_kernel,
        out_shape=sds((SHARD, 2 * CORE_KV), F32),
        in_specs=[VM] * 4,
        out_specs=VM,
        compiler_params=params(),
        cost_estimate=cost(0, 2e6),
    )(*ps)


def paired_body(hidden, queries, keys, value_weight, doc_ids, cotangent):
    q, g = queries[0], cotangent[0]
    send, p0, w0 = pack(hidden[0], keys[0], doc_ids, value_weight, q, g)
    p2 = swap(send, "seq", 2)
    w6, w4 = swap(w0, "dp", 6), swap(w0, "dp", 4)
    p1 = swap(p0, "seq", 1)
    later = after(w0, p1)
    w1, w2 = swap(later, "dp", 1), swap(later, "dp", 2)
    w3 = swap(w1, "dp", 2)
    own, w0 = relay(after(p0, p1), w0)
    w7, w5 = swap(after(w6, own), "dp", 1), swap(after(w4, w2), "dp", 1)
    p3 = swap(after(p2, w1, w3, w5, w7), "seq", 1)
    ps = (own, p1, p2, p3)
    vp3, wp = partial_values((own, p1, p2), (w0, w1, w2, w3, w4, w5, w6, w7))
    vp0, vp1 = last_values(vp3, p3, wp)
    rv0, rv1 = swap(vp0, "seq", 2), swap(vp1, "seq", 2)
    e, inv = scores(after(q, vp0), ps)
    wps = swap(wp, "seq", 1)
    first, first_dk, dv0 = attention_first(e, inv, q, g, *ps, vp0, rv0)
    rdv0 = swap(dv0, "seq", 2)
    o0, dq0, dk0, dk2, swap_out, dv1 = attention_second(e, inv, q, g, *ps, vp1, rv1, first, first_dk)
    rdv1 = swap(dv1, "seq", 2)
    gv, gv_keep, gv_send = value_grad((dv0, dv1), (rdv0, rdv1))
    send_a, own_a = weight_grad_far(gv, ps)
    send_b, own_b = weight_grad_near(gv, ps)
    far_a = swap(send_a, "dp", 1)
    far_b = swap(send_b, "dp", 2)
    gvs = swap(gv_send, "seq", 1)
    swapped = swap(after(swap_out, gv), "seq", 1)
    gh0, gh_a, gh_b = hidden_grad(gv_keep, gvs, wp, wps, dk2, swapped)
    s4, s6 = add_pair(own_a, far_a)
    t6, t4 = swap(s6, "dp", 6), swap(s4, "dp", 4)
    t46 = add_two(t4, t6)
    s0, s1 = add_pair(own_b, far_b)
    gh_far = swap(gh_a, "seq", 2), swap(gh_b, "seq", 2)
    attn_out, grad_queries = heads_join(o0, dq0, swapped)
    s1, attn_out, grad_queries = lax.optimization_barrier((s1, attn_out, grad_queries))
    t1 = swap(s1, "dp", 1)
    d0 = add_three(t46, s0, t1)
    d2 = swap(d0, "seq", 2)
    d1 = swap(d0, "seq", 1)
    grad_hidden, grad_keys = hidden_join(gh0, gh_far, dk0, swapped)
    d2, grad_hidden, grad_keys = lax.optimization_barrier((d2, grad_hidden, grad_keys))
    d3 = swap(d2, "seq", 1)
    grad_weight = weight_join((d0, d1, d2, d3))
    return attn_out[None], grad_queries[None], grad_keys[None], grad_hidden[None], grad_weight


def solution(mesh):
    in_specs = (
        P("dp", "seq", None),
        P("dp", "seq", None),
        P("dp", "seq", None),
        P("dp", None),
        P("dp", "seq"),
        P("dp", "seq", None),
    )
    out_specs = (
        P("dp", "seq", None),
        P("dp", "seq", None),
        P("dp", "seq", None),
        P("dp", "seq", None),
        P("dp", None),
    )
    paired = mesh.shape["dp"] == N_DP and mesh.shape["seq"] == 4
    return jax.shard_map(
        paired_body if paired else body, mesh=mesh, in_specs=in_specs, out_specs=out_specs, check_vma=False
    )
```

```python
import functools

import jax
import jax.numpy as jnp
from jax import lax
from jax.experimental import pallas as pl
from jax.experimental.pallas import tpu as pltpu
from jax.sharding import PartitionSpec as P

QUERY_HEADS = 20
KEY_VALUE_HEADS = 4
HEAD_SIZE = 128
QUERY_PER_KV = 5

BF = jnp.bfloat16
F32 = jnp.float32
VM = pl.BlockSpec(memory_space=pltpu.VMEM)
ANY = pl.BlockSpec(memory_space=pl.ANY)


def body(hidden, queries, keys, value_weight, doc_ids, cotangent):
    tokens = hidden[0]
    row_count = tokens.shape[0]
    width = value_weight.shape[1]
    scale = HEAD_SIZE ** (-0.5)
    shard_list = lax.axis_size("seq")
    my_index = lax.axis_index("seq")
    full_weight = lax.all_gather(value_weight, "dp", axis=0, tiled=True)
    values_sum = jnp.dot(tokens, full_weight, preferred_element_type=jnp.float32)
    values = values_sum.astype(jnp.bfloat16)
    every_key, every_value, all_docs = (
        lax.all_gather(keys[0], "seq", axis=0, tiled=True),
        lax.all_gather(values, "seq", axis=0, tiled=True),
        lax.all_gather(doc_ids[0], "seq", axis=0, tiled=True),
    )
    query_head_rows = queries[0].reshape(row_count, KEY_VALUE_HEADS, QUERY_PER_KV, HEAD_SIZE)
    gradient_heads = cotangent[0].reshape(row_count, KEY_VALUE_HEADS, QUERY_PER_KV, HEAD_SIZE)
    query_docs = doc_ids[0]
    query_pos = my_index * row_count + jnp.arange(row_count, dtype=jnp.int32)
    local_pos = jnp.arange(row_count, dtype=jnp.int32)

    def block_scores(shard):
        start_offset = shard * row_count
        key_tile = lax.dynamic_slice_in_dim(every_key, start_offset, row_count, 0).reshape(
            row_count, KEY_VALUE_HEADS, HEAD_SIZE
        )
        value_tile = lax.dynamic_slice_in_dim(every_value, start_offset, row_count, 0).reshape(
            row_count, KEY_VALUE_HEADS, HEAD_SIZE
        )
        doc_block = lax.dynamic_slice_in_dim(all_docs, start_offset, row_count, 0)
        scores = (
            jnp.einsum(
                "qhgd,khd->hgqk", query_head_rows, key_tile, preferred_element_type=jnp.float32
            )
            * scale
        )
        allow = ((start_offset + local_pos)[None, :] <= query_pos[:, None]) & (
            doc_block[None, :] == query_docs[:, None]
        )
        return (jnp.where(allow, scores, -1e30), allow, key_tile, value_tile)

    def forward_step(shard, carry):
        peak, total, out_acc = carry
        masked, allow, key_tile, value_tile = block_scores(shard)
        new_peak = jnp.maximum(peak, jnp.max(masked, axis=-1))
        expd = jnp.where(allow, jnp.exp(masked - new_peak[..., None]), 0.0)
        factor = jnp.exp(peak - new_peak)
        total = total * factor + jnp.sum(expd, axis=-1)
        out_acc = out_acc * factor[..., None] + jnp.einsum(
            "hgqk,khd->hgqd",
            expd.astype(jnp.bfloat16),
            value_tile,
            preferred_element_type=jnp.float32,
        )
        return (new_peak, total, out_acc)

    head_layout = (KEY_VALUE_HEADS, QUERY_PER_KV, row_count)
    start_state = (
        jnp.full(head_layout, -1e30, jnp.float32),
        jnp.zeros(head_layout, jnp.float32),
        jnp.zeros((KEY_VALUE_HEADS, QUERY_PER_KV, row_count, HEAD_SIZE), jnp.float32),
    )
    peak, total, out_acc = lax.fori_loop(0, shard_list, forward_step, start_state)
    attn_b = (out_acc / total[..., None]).astype(jnp.bfloat16).transpose(2, 0, 1, 3)
    delta = jnp.sum(
        gradient_heads.astype(jnp.float32) * attn_b.astype(jnp.float32), axis=-1
    ).transpose(1, 2, 0)

    def gradient_update(shard, carry):
        dq_acc, grad_buf = carry
        masked, allow, key_tile, value_tile = block_scores(shard)
        probs = jnp.where(allow, jnp.exp(masked - peak[..., None]), 0.0) / total[..., None]
        probs_b = probs.astype(jnp.bfloat16)
        dprob = jnp.einsum(
            "qhgd,khd->hgqk", gradient_heads, value_tile, preferred_element_type=jnp.float32
        )
        dscore = (probs * (dprob - delta[..., None])).astype(jnp.bfloat16)
        dq_acc = dq_acc + jnp.einsum(
            "hgqk,khd->qhgd", dscore, key_tile, preferred_element_type=jnp.float32
        )
        dk_block = (
            jnp.einsum(
                "hgqk,qhgd->khd", dscore, query_head_rows, preferred_element_type=jnp.float32
            )
            * scale
        ).astype(jnp.bfloat16)
        dv_block = jnp.einsum(
            "hgqk,qhgd->khd", probs_b, gradient_heads, preferred_element_type=jnp.float32
        ).astype(jnp.bfloat16)
        paired = jnp.concatenate(
            (dk_block.reshape(row_count, width), dv_block.reshape(row_count, width)), axis=1
        )
        grad_buf = lax.dynamic_update_slice_in_dim(grad_buf, paired, shard * row_count, 0)
        return (dq_acc, grad_buf)

    blank_buffer = jnp.zeros((row_count * shard_list, 2 * width), jnp.bfloat16)
    dq_acc, grad_buf = lax.fori_loop(
        0,
        shard_list,
        gradient_update,
        (
            jnp.zeros((row_count, KEY_VALUE_HEADS, QUERY_PER_KV, HEAD_SIZE), jnp.float32),
            blank_buffer,
        ),
    )
    grad_queries = (dq_acc * scale).astype(jnp.bfloat16).reshape(row_count, QUERY_HEADS * HEAD_SIZE)
    summed = lax.psum_scatter(
        grad_buf.astype(jnp.float32).astype(jnp.bfloat16), "seq", scatter_dimension=0, tiled=True
    ).astype(jnp.float32)
    grad_keys = summed[:, :width].astype(jnp.bfloat16)
    grad_values = summed[:, width:].astype(jnp.bfloat16)
    grad_hidden = jnp.einsum(
        "kc,dc->kd", grad_values, full_weight, preferred_element_type=jnp.float32
    ).astype(jnp.bfloat16)
    partial_rows = lax.psum_scatter(
        jnp.einsum("kd,kc->dc", tokens, grad_values, preferred_element_type=jnp.float32).astype(
            jnp.bfloat16
        ),
        "dp",
        scatter_dimension=0,
        tiled=True,
    )
    grad_weight = lax.psum(partial_rows, "seq").astype(jnp.float32)
    return (
        attn_b.reshape(row_count, QUERY_HEADS * HEAD_SIZE)[None],
        grad_queries[None],
        grad_keys[None],
        grad_hidden[None],
        grad_weight,
    )


N_DP = 8
ROWS = 128
SHARD = 640
HALF = SHARD // 2
CHUNK = 128
WIDE = N_DP * HALF
CORE_KV = 256
SPARE = 16
CUT = 1536
CORE_Q = 1280
KEY_AT = WIDE
DOC_AT = KEY_AT + 512
QUERY_AT = DOC_AT + ROWS
COT_AT = QUERY_AT + CORE_Q
PACK = COT_AT + CORE_Q


def params(mib=32):
    return pltpu.CompilerParams(vmem_limit_bytes=mib * 1024 * 1024)


def cost(flops, nbytes):
    return pl.CostEstimate(flops=int(flops), bytes_accessed=int(nbytes), transcendentals=0)


def sds(shape, dtype=BF):
    return jax.ShapeDtypeStruct(shape, dtype)


def swap(x, axis, k):
    size = lax.axis_size(axis)
    return lax.ppermute(x, axis, [(i, i ^ k) for i in range(size)])


def after(x, *others):
    return lax.optimization_barrier((x, *others))[0]


def dot_tt(a, b):
    return lax.dot_general(a, b, (((0,), (0,)), ((), ())), preferred_element_type=F32)


def dot_nt(a, b):
    return lax.dot_general(a, b, (((1,), (1,)), ((), ())), preferred_element_type=F32)


def turn(x):
    return pltpu.roll(x.astype(F32), CHUNK // 2, 1).astype(x.dtype)


def first_half():
    return lax.broadcasted_iota(jnp.int32, (ROWS, CHUNK), 1) < CHUNK // 2


def pack_kernel(h, k, doc, w, q, g, send, keep, w0, h_in, k_in, doc_in, w_in, send_out, keep_out, sems):
    s = lax.axis_index("seq")
    r = lax.axis_index("dp")
    y, c = s // 2, s % 2
    cols = pl.ds(pl.multiple_of(c * CORE_KV, CORE_KV), CORE_KV)
    other = pl.ds(pl.multiple_of((1 - c) * CORE_Q, CORE_Q), CORE_Q)

    def copy(i, src, dst):
        made = pltpu.make_async_copy(src, dst, sems.at[i])
        made.start()
        return made

    w_copies = (
        copy(0, w.at[pl.ds(pl.multiple_of(y * 384, 128), 256), cols], w_in.at[pl.ds(0, 256)]),
        copy(1, w.at[pl.ds(pl.multiple_of(256 + y * 64, 64), 64), cols], w_in.at[pl.ds(256, 64)]),
    )
    blocks = [
        copy(10 + j, h.at[:, pl.ds(pl.multiple_of((r ^ j) * SHARD, 128), SHARD)], h_in.at[:, pl.ds(j * SHARD, SHARD)])
        for j in range(N_DP)
    ]
    small = copy(3, k, k_in), copy(4, doc, doc_in)
    heads = (
        copy(5, q.at[:, other], keep_out.at[:, pl.ds(QUERY_AT, CORE_Q)]),
        copy(6, g.at[:, other], keep_out.at[:, pl.ds(COT_AT, CORE_Q)]),
    )
    for made in w_copies:
        made.wait()
    outs = [copy(7, w_in, w0)]
    low = first_half()
    for p in range(N_DP // 2):
        blocks[2 * p].wait()
        blocks[2 * p + 1].wait()
        for which, (out, dst, part) in enumerate(((send_out, send, 1 - y), (keep_out, keep, y))):
            mids = []
            for i in range(2):
                base = (2 * p + i) * SHARD
                start = pl.multiple_of(base + part * 384, 128)
                out[:, p * SHARD + i * 256 : p * SHARD + (i + 1) * 256] = h_in[:, pl.ds(start, 256)]
                mid = h_in[:, base + 256 : base + 384]
                mids.append(jnp.where(part == i, mid, turn(mid)))
            out[:, p * SHARD + 512 : (p + 1) * SHARD] = jnp.where(low, mids[0], mids[1])
            span = pl.ds(p * SHARD, SHARD)
            outs.append(copy(18 + 4 * which + p, out.at[:, span], dst.at[:, span]))
    for made in small:
        made.wait()
    for out in (send_out, keep_out):
        out[:, KEY_AT:DOC_AT] = k_in[...]
        out[:, DOC_AT:QUERY_AT] = jnp.broadcast_to(doc_in[...].astype(F32), (ROWS, ROWS)).astype(BF)
    rest = pl.ds(KEY_AT, QUERY_AT - KEY_AT)
    outs.append(copy(8, send_out.at[:, rest], send.at[:, rest]))
    for made in heads:
        made.wait()
    rest = pl.ds(KEY_AT, PACK - KEY_AT)
    outs.append(copy(9, keep_out.at[:, rest], keep.at[:, rest]))
    for made in outs:
        made.wait()


def pack(h, k, doc, w, q, g):
    return pl.pallas_call(
        pack_kernel,
        out_shape=(sds((ROWS, QUERY_AT)), sds((ROWS, PACK)), sds((HALF, CORE_KV))),
        in_specs=[ANY] * 6,
        out_specs=(ANY,) * 3,
        scratch_shapes=[
            pltpu.VMEM((ROWS, N_DP * SHARD), BF),
            pltpu.VMEM((ROWS, 2 * CORE_KV), BF),
            pltpu.VMEM((1, ROWS), jnp.int32),
            pltpu.VMEM((HALF, CORE_KV), BF),
            pltpu.VMEM((ROWS, QUERY_AT), BF),
            pltpu.VMEM((ROWS, PACK), BF),
            pltpu.SemaphoreType.DMA((26,)),
        ],
        compiler_params=params(62),
        cost_estimate=cost(0, 3e6),
    )(h, k, doc, w, q, g)


def relay_kernel(p, w, own, ow):
    own[...] = p[:, 0:QUERY_AT]
    ow[...] = w[...]


def relay(p, w):
    return pl.pallas_call(
        relay_kernel,
        out_shape=(sds((ROWS, QUERY_AT)), sds((HALF, CORE_KV))),
        in_specs=[VM] * 2,
        out_specs=(VM,) * 2,
        compiler_params=params(),
        cost_estimate=cost(0, 4e6),
    )(p, w)


def values_kernel(h0, h1, h2, w0, w1, w2, w3, w4, w5, w6, w7, vp_ref, wp_ref):
    ws = (w0, w1, w2, w3, w4, w5, w6, w7)
    for p in range(N_DP // 2):
        a, b = ws[2 * p], ws[2 * p + 1]
        base = p * SHARD
        wp_ref[base : base + 256, :] = a[0:256, :]
        wp_ref[base + 256 : base + 512, :] = b[0:256, :]
        wp_ref[base + 512 : base + 576, :] = a[256:HALF, :]
        wp_ref[base + 576 : base + 640, :] = b[256:HALF, :]
    for t, h in enumerate((h0, h1, h2)):
        vp_ref[t * ROWS : (t + 1) * ROWS, :] = jnp.dot(
            h[:, 0:WIDE], wp_ref[...], preferred_element_type=F32
        ).astype(BF)


def partial_values(hs, ws):
    return pl.pallas_call(
        values_kernel,
        out_shape=(sds((3 * ROWS, CORE_KV)), sds((WIDE, CORE_KV))),
        in_specs=[VM] * 11,
        out_specs=(VM, VM),
        compiler_params=params(),
        cost_estimate=cost(2 * 384 * WIDE * 256, 6e6),
    )(*hs, *ws)


def last_values_kernel(vp, h3, wp, o0, o1):
    last = jnp.dot(h3[:, 0:WIDE], wp[...], preferred_element_type=F32).astype(BF)
    for i, o in enumerate((o0, o1)):
        cols = slice(i * HEAD_SIZE, (i + 1) * HEAD_SIZE)
        o[0 : 3 * ROWS, :] = vp[:, cols]
        o[3 * ROWS :, :] = last[:, cols]


def last_values(vp, h3, wp):
    return pl.pallas_call(
        last_values_kernel,
        out_shape=(sds((4 * ROWS, HEAD_SIZE)),) * 2,
        in_specs=[VM] * 3,
        out_specs=(VM,) * 2,
        compiler_params=params(),
        cost_estimate=cost(2 * 128 * WIDE * 256, 2e6),
    )(vp, h3, wp)


def scores_kernel(q0, p0, p1, p2, p3, e_ref, inv_ref, bias):
    s = lax.axis_index("seq")
    c = s % 2
    factor = HEAD_SIZE ** (-0.5)
    log2e = 1.4426950408889634
    ps = (p0, p1, p2, p3)
    rows = [p[0:16, DOC_AT:QUERY_AT][0:1, :].astype(F32) for p in ps]
    for t in range(4):
        key_doc = jnp.transpose(jnp.broadcast_to(rows[t], (ROWS, ROWS)))
        key_pos = (s ^ t) * ROWS + lax.broadcasted_iota(jnp.int32, (ROWS, ROWS), 0)
        for u in range(2):
            query_pos = (s ^ u) * ROWS + lax.broadcasted_iota(jnp.int32, (ROWS, ROWS), 1)
            allow = (key_pos <= query_pos) & (key_doc == jnp.broadcast_to(rows[u], (ROWS, ROWS)))
            bias[t * ROWS : (t + 1) * ROWS, u * ROWS : (u + 1) * ROWS] = jnp.where(allow, 0.0, -1e30)
    for kvh in range(2):
        cols = pl.ds(pl.multiple_of(KEY_AT + c * CORE_KV + kvh * HEAD_SIZE, HEAD_SIZE), HEAD_SIZE)
        key = jnp.concatenate([p[:, cols] for p in ps], axis=0)
        for i in range(QUERY_PER_KV):
            head = kvh * QUERY_PER_KV + i
            qcols = pl.ds(pl.multiple_of(c * CORE_Q + head * HEAD_SIZE, HEAD_SIZE), HEAD_SIZE)
            far = p1[:, QUERY_AT + head * HEAD_SIZE : QUERY_AT + (head + 1) * HEAD_SIZE]
            query = jnp.concatenate([q0[:, qcols], far], axis=0)
            st = dot_nt(key, query) * (factor * log2e) + bias[...]
            e = jnp.exp2(st - jnp.max(st, axis=0, keepdims=True))
            inv_ref[head * 8 : head * 8 + 8, :] = jnp.broadcast_to(
                1.0 / jnp.sum(e, axis=0, keepdims=True), (8, 2 * ROWS)
            )
            e_ref[head] = e.astype(BF)


def scores(q, ps):
    return pl.pallas_call(
        scores_kernel,
        out_shape=(sds((10, 4 * ROWS, 2 * ROWS)), sds((80, 2 * ROWS), F32)),
        in_specs=[VM] * 5,
        out_specs=(VM,) * 2,
        scratch_shapes=[pltpu.VMEM((4 * ROWS, 2 * ROWS), F32)],
        compiler_params=params(),
        cost_estimate=cost(2 * 10 * 256 * 512 * 128 * 8, 6e6),
    )(q, *ps)


def attend_head(kvh, e_ref, inv_ref, q0, g0, ps, vp, rv):
    c = lax.axis_index("seq") % 2
    factor = HEAD_SIZE ** (-0.5)
    p1 = ps[1]
    cols = pl.ds(pl.multiple_of(KEY_AT + c * CORE_KV + kvh * HEAD_SIZE, HEAD_SIZE), HEAD_SIZE)
    key = jnp.concatenate([p[:, cols] for p in ps], axis=0)
    far = rv[...].astype(F32)
    far = jnp.concatenate([far[2 * ROWS :], far[: 2 * ROWS]], axis=0)
    value = (vp[...].astype(F32) + far).astype(BF)
    dk = jnp.zeros((4 * ROWS, HEAD_SIZE), F32)
    dv = jnp.zeros((4 * ROWS, HEAD_SIZE), F32)
    outs = []
    for i in range(QUERY_PER_KV):
        head = kvh * QUERY_PER_KV + i
        qcols = pl.ds(pl.multiple_of(c * CORE_Q + head * HEAD_SIZE, HEAD_SIZE), HEAD_SIZE)
        low, high = head * HEAD_SIZE, (head + 1) * HEAD_SIZE
        query = jnp.concatenate([q0[:, qcols], p1[:, QUERY_AT + low : QUERY_AT + high]], axis=0)
        cot = jnp.concatenate([g0[:, qcols], p1[:, COT_AT + low : COT_AT + high]], axis=0)
        e = e_ref[head]
        inv = inv_ref[head * 8 : head * 8 + 8, :][0:1, :]
        out = jnp.transpose(dot_tt(value, e) * inv).astype(BF)
        probs = e.astype(F32) * inv
        term = probs * dot_nt(value, cot)
        delta = jnp.sum(term, axis=0, keepdims=True)
        ds = (term - probs * delta).astype(BF)
        dq = jnp.transpose(dot_tt(key, ds) * factor).astype(BF)
        outs.append((out, dq))
        dk = dk + jnp.dot(ds, query, preferred_element_type=F32)
        dv = dv + jnp.dot(probs.astype(BF), cot, preferred_element_type=F32)
    return outs, (dk * factor).astype(BF), dv.astype(BF)


def attention_first_kernel(e_ref, inv_ref, q0, g0, p0, p1, p2, p3, vp, rv, out, dk_ref, dv_ref):
    outs, dk, dv = attend_head(0, e_ref, inv_ref, q0, g0, (p0, p1, p2, p3), vp, rv)
    for i, (o, dq) in enumerate(outs):
        cols = slice(i * HEAD_SIZE, (i + 1) * HEAD_SIZE)
        out[0 : 2 * ROWS, cols] = o
        out[2 * ROWS :, cols] = dq
    dk_ref[...] = dk
    dv_ref[0 : 4 * ROWS, :] = dv
    dv_ref[4 * ROWS :, :] = jnp.zeros((SPARE, HEAD_SIZE), BF)


def attention_second_kernel(
    e_ref, inv_ref, q0, g0, p0, p1, p2, p3, vp, rv, first, first_dk,
    o0, dq0, dk0, dk2, swap_ref, dv_ref,
):
    outs, dk, dv = attend_head(1, e_ref, inv_ref, q0, g0, (p0, p1, p2, p3), vp, rv)
    half = QUERY_PER_KV * HEAD_SIZE
    o0[:, 0:half] = first[0:ROWS, :]
    swap_ref[:, 0:half] = first[ROWS : 2 * ROWS, :]
    dq0[:, 0:half] = first[2 * ROWS : 3 * ROWS, :]
    swap_ref[:, CORE_Q : CORE_Q + half] = first[3 * ROWS :, :]
    for i, (o, dq) in enumerate(outs):
        low, high = half + i * HEAD_SIZE, half + (i + 1) * HEAD_SIZE
        o0[:, low:high] = o[:ROWS]
        swap_ref[:, low:high] = o[ROWS:]
        dq0[:, low:high] = dq[:ROWS]
        swap_ref[:, CORE_Q + low : CORE_Q + high] = dq[ROWS:]
    for kvh, d in enumerate((first_dk[...], dk)):
        mine = slice(kvh * HEAD_SIZE, (kvh + 1) * HEAD_SIZE)
        dk0[:, mine] = d[:ROWS]
        dk2[:, mine] = d[2 * ROWS : 3 * ROWS]
        at = 2 * CORE_Q + kvh * HEAD_SIZE
        swap_ref[:, at : at + HEAD_SIZE] = d[ROWS : 2 * ROWS]
        swap_ref[:, at + CORE_KV : at + CORE_KV + HEAD_SIZE] = d[3 * ROWS :]
    dv_ref[...] = dv


def attention_first(*args):
    return pl.pallas_call(
        attention_first_kernel,
        out_shape=(
            sds((4 * ROWS, QUERY_PER_KV * HEAD_SIZE)), sds((4 * ROWS, HEAD_SIZE)),
            sds((4 * ROWS + SPARE, HEAD_SIZE)),
        ),
        in_specs=[VM] * 10,
        out_specs=(VM,) * 3,
        compiler_params=params(),
        cost_estimate=cost(5 * 10 * 256 * 512 * 128 * 4, 3e6),
    )(*args)


def attention_second(*args):
    return pl.pallas_call(
        attention_second_kernel,
        out_shape=(sds((ROWS, CORE_Q)),) * 2
        + (sds((ROWS, CORE_KV)),) * 2
        + (sds((ROWS, 2 * CORE_Q + 2 * CORE_KV)), sds((4 * ROWS, HEAD_SIZE))),
        in_specs=[VM] * 12,
        out_specs=(VM,) * 6,
        compiler_params=params(),
        cost_estimate=cost(5 * 10 * 256 * 512 * 128 * 4, 3e6),
    )(*args)


def weight_grad_pair(p, hs, gv, *outs):
    acc = jnp.zeros((CHUNK, CORE_KV), F32)
    for t, h in enumerate(hs):
        acc = acc + dot_tt(h[:, p * SHARD + 512 : (p + 1) * SHARD], gv[t * ROWS : (t + 1) * ROWS, :])
    middle = acc.astype(BF)
    for which, out, at in outs:
        acc = jnp.zeros((256, CORE_KV), F32)
        for t, h in enumerate(hs):
            first = p * SHARD + which * 256
            acc = acc + dot_tt(h[:, first : first + 256], gv[t * ROWS : (t + 1) * ROWS, :])
        out[at : at + 256, :] = acc.astype(BF)
        out[at + 256 : at + HALF, :] = middle[which * 64 : (which + 1) * 64]


def value_grad_kernel(dv0, dv1, rdv0, rdv1, gv, gv_keep, gv_send):
    for t in range(4):
        parts = []
        for dv, rdv in ((dv0, rdv0), (dv1, rdv1)):
            a = dv[t * ROWS : (t + 1) * ROWS, :].astype(F32)
            b = rdv[(t ^ 2) * ROWS : ((t ^ 2) + 1) * ROWS, :].astype(F32)
            parts.append(a + b)
        total = jnp.concatenate(parts, axis=1).astype(BF)
        gv[t * ROWS : (t + 1) * ROWS, :] = total
        half = (t // 2) * ROWS
        if t % 2 == 0:
            gv_keep[half : half + ROWS, :] = total
        else:
            gv_send[half : half + ROWS, :] = total


def value_grad(dvs, rdvs):
    return pl.pallas_call(
        value_grad_kernel,
        out_shape=(sds((4 * ROWS, CORE_KV)),) + (sds((2 * ROWS, CORE_KV)),) * 2,
        in_specs=[VM] * 4,
        out_specs=(VM,) * 3,
        compiler_params=params(),
        cost_estimate=cost(0, 1e6),
    )(*dvs, *rdvs)


def weight_grad_far_kernel(which, gv, h0, h1, h2, h3, out):
    for place, p in enumerate((2, 3)):
        weight_grad_pair(p, (h0, h1, h2, h3), gv, (which, out, place * HALF))


def weight_grad_far(which, gv, hs):
    return pl.pallas_call(
        functools.partial(weight_grad_far_kernel, which),
        out_shape=sds((2 * HALF, CORE_KV)),
        in_specs=[VM] * 5,
        out_specs=VM,
        compiler_params=params(),
        cost_estimate=cost(256 * WIDE * 256, 2e6),
    )(gv, *hs)


def weight_grad_near_kernel(gv, h0, h1, h2, h3, send, own):
    for p, out in ((1, send), (0, own)):
        weight_grad_pair(p, (h0, h1, h2, h3), gv, (0, out, 0), (1, out, HALF))


def weight_grad_near(gv, hs):
    return pl.pallas_call(
        weight_grad_near_kernel,
        out_shape=(sds((2 * HALF, CORE_KV)),) * 2,
        in_specs=[VM] * 5,
        out_specs=(VM,) * 2,
        compiler_params=params(),
        cost_estimate=cost(512 * WIDE * 256, 4e6),
    )(gv, *hs)


def hidden_grad_kernel(gv, gvs, wp, wps, dk2, swapped, gh0, send_a, send_b):
    full = dot_nt(gv[...], wp[...]) + dot_nt(gvs[...], wps[...])
    full = full.astype(BF)
    gh0[...] = full[:ROWS]
    far = full[ROWS:]
    send_a[...] = far[:, : CUT]
    send_b[:, : WIDE - CUT] = far[:, CUT :]
    c = lax.axis_index("seq") % 2
    at = WIDE - CUT
    send_b[:, pl.ds(pl.multiple_of(at + c * CORE_KV, CORE_KV), CORE_KV)] = dk2[...]
    send_b[:, pl.ds(pl.multiple_of(at + (1 - c) * CORE_KV, CORE_KV), CORE_KV)] = swapped[
        :, 2 * CORE_Q + CORE_KV :
    ]


def hidden_grad(gv, gvs, wp, wps, dk2, swapped):
    return pl.pallas_call(
        hidden_grad_kernel,
        out_shape=(sds((ROWS, WIDE)), sds((ROWS, CUT)), sds((ROWS, WIDE - CUT + 2 * CORE_KV))),
        in_specs=[VM] * 6,
        out_specs=(VM,) * 3,
        compiler_params=params(),
        cost_estimate=cost(2 * 256 * WIDE * 512, 6e6),
    )(gv, gvs, wp, wps, dk2, swapped)


def hidden_join_kernel(own_ref, far_a, far_b, dk0, swapped, o_ref, dk_ref, far_ref):
    far_ref[:, 0:CUT] = far_a[...]
    far_ref[:, CUT:] = far_b[:, : WIDE - CUT]
    s = lax.axis_index("seq")
    y, c = s // 2, s % 2
    r = lax.axis_index("dp")
    low = first_half()
    for p in range(N_DP // 2):
        for i in range(2):
            base = (r ^ (2 * p + i)) * SHARD
            src = slice(p * SHARD + i * 256, p * SHARD + (i + 1) * 256)
            o_ref[:, pl.ds(pl.multiple_of(base + y * 384, 128), 256)] = own_ref[:, src]
            o_ref[:, pl.ds(pl.multiple_of(base + (1 - y) * 384, 128), 256)] = far_ref[:, src]
        own = own_ref[:, p * SHARD + 512 : (p + 1) * SHARD]
        far = far_ref[:, p * SHARD + 512 : (p + 1) * SHARD]
        part0 = jnp.where(y == 0, own, far)
        part1 = jnp.where(y == 0, far, own)
        at0 = pl.multiple_of((r ^ (2 * p)) * SHARD + 256, 128)
        at1 = pl.multiple_of((r ^ (2 * p + 1)) * SHARD + 256, 128)
        o_ref[:, pl.ds(at0, CHUNK)] = jnp.where(low, part0, turn(part1))
        o_ref[:, pl.ds(at1, CHUNK)] = jnp.where(low, turn(part0), part1)
    for place, near in ((c, dk0[...]), (1 - c, swapped[:, 2 * CORE_Q : 2 * CORE_Q + CORE_KV])):
        far = far_b[:, pl.ds(pl.multiple_of(WIDE - CUT + place * CORE_KV, CORE_KV), CORE_KV)]
        dk_ref[:, pl.ds(pl.multiple_of(place * CORE_KV, CORE_KV), CORE_KV)] = (
            near.astype(F32) + far.astype(F32)
        ).astype(BF)


def hidden_join(own, fars, dk0, swapped):
    return pl.pallas_call(
        hidden_join_kernel,
        out_shape=(sds((ROWS, N_DP * SHARD)), sds((ROWS, 2 * CORE_KV))),
        in_specs=[VM] * 5,
        out_specs=(VM, VM),
        scratch_shapes=[pltpu.VMEM((ROWS, WIDE), BF)],
        compiler_params=params(),
        cost_estimate=cost(0, 3e6),
    )(own, *fars, dk0, swapped)


def heads_join_kernel(o0, dq0, swapped, o_ref, dq_ref):
    c = lax.axis_index("seq") % 2
    near = pl.ds(pl.multiple_of(c * CORE_Q, CORE_Q), CORE_Q)
    far = pl.ds(pl.multiple_of((1 - c) * CORE_Q, CORE_Q), CORE_Q)
    o_ref[:, near] = o0[...]
    o_ref[:, far] = swapped[:, 0:CORE_Q]
    dq_ref[:, near] = dq0[...]
    dq_ref[:, far] = swapped[:, CORE_Q : 2 * CORE_Q]


def heads_join(o0, dq0, swapped):
    return pl.pallas_call(
        heads_join_kernel,
        out_shape=(sds((ROWS, 2 * CORE_Q)),) * 2,
        in_specs=[VM] * 3,
        out_specs=(VM,) * 2,
        compiler_params=params(),
        cost_estimate=cost(0, 4e6),
    )(o0, dq0, swapped)


def add_pair_kernel(a, b, o0, o1):
    total = (a[...].astype(F32) + b[...].astype(F32)).astype(BF)
    o0[...] = total[:HALF]
    o1[...] = total[HALF:]


def add_pair(a, b):
    return pl.pallas_call(
        add_pair_kernel,
        out_shape=(sds((HALF, CORE_KV)),) * 2,
        in_specs=[VM] * 2,
        out_specs=(VM,) * 2,
        compiler_params=params(),
        cost_estimate=cost(0, 1e6),
    )(a, b)


def add_two_kernel(a, b, o):
    o[...] = a[...].astype(F32) + b[...].astype(F32)


def add_two(a, b):
    return pl.pallas_call(
        add_two_kernel,
        out_shape=sds((HALF, CORE_KV), F32),
        in_specs=[VM] * 2,
        out_specs=VM,
        compiler_params=params(),
        cost_estimate=cost(0, 1e6),
    )(a, b)


def add_three_kernel(a, b, c, o):
    o[...] = (a[...] + (b[...].astype(F32) + c[...].astype(F32))).astype(BF)


def add_three(a, b, c):
    return pl.pallas_call(
        add_three_kernel,
        out_shape=sds((HALF, CORE_KV)),
        in_specs=[VM] * 3,
        out_specs=VM,
        compiler_params=params(),
        cost_estimate=cost(0, 1e6),
    )(a, b, c)


def weight_join_kernel(p0, p1, p2, p3, o_ref):
    s = lax.axis_index("seq")
    for t, p in enumerate((p0, p1, p2, p3)):
        y, c = (s ^ t) // 2, (s ^ t) % 2
        cols = pl.ds(pl.multiple_of(c * CORE_KV, CORE_KV), CORE_KV)
        o_ref[pl.ds(pl.multiple_of(y * 384, 128), 256), cols] = p[0:256, :].astype(F32)
        o_ref[pl.ds(pl.multiple_of(256 + y * 64, 64), 64), cols] = p[256:HALF, :].astype(F32)


def weight_join(ps):
    return pl.pallas_call(
        weight_join_kernel,
        out_shape=sds((SHARD, 2 * CORE_KV), F32),
        in_specs=[VM] * 4,
        out_specs=VM,
        compiler_params=params(),
        cost_estimate=cost(0, 2e6),
    )(*ps)


def paired_body(hidden, queries, keys, value_weight, doc_ids, cotangent):
    q, g = queries[0], cotangent[0]
    send, p0, w0 = pack(hidden[0], keys[0], doc_ids, value_weight, q, g)
    p2 = swap(send, "seq", 2)
    w6, w4 = swap(w0, "dp", 6), swap(w0, "dp", 4)
    p1 = swap(p0, "seq", 1)
    later = after(w0, p1)
    w1, w2 = swap(later, "dp", 1), swap(later, "dp", 2)
    w3 = swap(w1, "dp", 2)
    own, w0 = relay(after(p0, p1), w0)
    w7, w5 = swap(after(w6, own), "dp", 1), swap(after(w4, w2), "dp", 1)
    p3 = swap(after(p2, w1, w3, w5, w7), "seq", 1)
    ps = (own, p1, p2, p3)
    vp3, wp = partial_values((own, p1, p2), (w0, w1, w2, w3, w4, w5, w6, w7))
    vp0, vp1 = last_values(vp3, p3, wp)
    rv0, rv1 = swap(vp0, "seq", 2), swap(vp1, "seq", 2)
    e, inv = scores(after(q, vp0), ps)
    wps = swap(wp, "seq", 1)
    first, first_dk, dv0 = attention_first(e, inv, q, g, *ps, vp0, rv0)
    rdv0 = swap(dv0, "seq", 2)
    o0, dq0, dk0, dk2, swap_out, dv1 = attention_second(e, inv, q, g, *ps, vp1, rv1, first, first_dk)
    rdv1 = swap(dv1, "seq", 2)
    gv, gv_keep, gv_send = value_grad((dv0, dv1), (rdv0, rdv1))
    send_a = weight_grad_far(1, gv, ps)
    far_a = swap(send_a, "dp", 1)
    own_a = weight_grad_far(0, after(gv, send_a), ps)
    gvs = swap(gv_send, "seq", 1)
    swapped = swap(after(swap_out, gv), "seq", 1)
    gh0, gh_a, gh_b = hidden_grad(gv_keep, gvs, wp, wps, dk2, swapped)
    send_b, own_b = weight_grad_near(after(gv, gh0), ps)
    far_b = swap(send_b, "dp", 2)
    s4, s6 = add_pair(own_a, far_a)
    t6, t4 = swap(s6, "dp", 6), swap(s4, "dp", 4)
    t46 = add_two(t4, t6)
    s0, s1 = add_pair(own_b, far_b)
    gh_far = swap(gh_a, "seq", 2), swap(gh_b, "seq", 2)
    attn_out, grad_queries = heads_join(o0, dq0, swapped)
    s1, attn_out, grad_queries = lax.optimization_barrier((s1, attn_out, grad_queries))
    t1 = swap(s1, "dp", 1)
    d0 = add_three(t46, s0, t1)
    d2 = swap(d0, "seq", 2)
    d1 = swap(d0, "seq", 1)
    grad_hidden, grad_keys = hidden_join(gh0, gh_far, dk0, swapped)
    d2, grad_hidden, grad_keys = lax.optimization_barrier((d2, grad_hidden, grad_keys))
    d3 = swap(d2, "seq", 1)
    grad_weight = weight_join((d0, d1, d2, d3))
    return attn_out[None], grad_queries[None], grad_keys[None], grad_hidden[None], grad_weight


def solution(mesh):
    in_specs = (
        P("dp", "seq", None),
        P("dp", "seq", None),
        P("dp", "seq", None),
        P("dp", None),
        P("dp", "seq"),
        P("dp", "seq", None),
    )
    out_specs = (
        P("dp", "seq", None),
        P("dp", "seq", None),
        P("dp", "seq", None),
        P("dp", "seq", None),
        P("dp", None),
    )
    paired = mesh.shape["dp"] == N_DP and mesh.shape["seq"] == 4
    return jax.shard_map(
        paired_body if paired else body, mesh=mesh, in_specs=in_specs, out_specs=out_specs, check_vma=False
    )
```

```python
import functools

import jax
import jax.numpy as jnp
from jax import lax
from jax.experimental import pallas as pl
from jax.experimental.pallas import tpu as pltpu
from jax.sharding import PartitionSpec as P

QUERY_HEADS = 20
KEY_VALUE_HEADS = 4
HEAD_SIZE = 128
QUERY_PER_KV = 5

BF = jnp.bfloat16
F32 = jnp.float32
VM = pl.BlockSpec(memory_space=pltpu.VMEM)
ANY = pl.BlockSpec(memory_space=pl.ANY)


def body(hidden, queries, keys, value_weight, doc_ids, cotangent):
    tokens = hidden[0]
    row_count = tokens.shape[0]
    width = value_weight.shape[1]
    scale = HEAD_SIZE ** (-0.5)
    shard_list = lax.axis_size("seq")
    my_index = lax.axis_index("seq")
    full_weight = lax.all_gather(value_weight, "dp", axis=0, tiled=True)
    values_sum = jnp.dot(tokens, full_weight, preferred_element_type=jnp.float32)
    values = values_sum.astype(jnp.bfloat16)
    every_key, every_value, all_docs = (
        lax.all_gather(keys[0], "seq", axis=0, tiled=True),
        lax.all_gather(values, "seq", axis=0, tiled=True),
        lax.all_gather(doc_ids[0], "seq", axis=0, tiled=True),
    )
    query_head_rows = queries[0].reshape(row_count, KEY_VALUE_HEADS, QUERY_PER_KV, HEAD_SIZE)
    gradient_heads = cotangent[0].reshape(row_count, KEY_VALUE_HEADS, QUERY_PER_KV, HEAD_SIZE)
    query_docs = doc_ids[0]
    query_pos = my_index * row_count + jnp.arange(row_count, dtype=jnp.int32)
    local_pos = jnp.arange(row_count, dtype=jnp.int32)

    def block_scores(shard):
        start_offset = shard * row_count
        key_tile = lax.dynamic_slice_in_dim(every_key, start_offset, row_count, 0).reshape(
            row_count, KEY_VALUE_HEADS, HEAD_SIZE
        )
        value_tile = lax.dynamic_slice_in_dim(every_value, start_offset, row_count, 0).reshape(
            row_count, KEY_VALUE_HEADS, HEAD_SIZE
        )
        doc_block = lax.dynamic_slice_in_dim(all_docs, start_offset, row_count, 0)
        scores = (
            jnp.einsum(
                "qhgd,khd->hgqk", query_head_rows, key_tile, preferred_element_type=jnp.float32
            )
            * scale
        )
        allow = ((start_offset + local_pos)[None, :] <= query_pos[:, None]) & (
            doc_block[None, :] == query_docs[:, None]
        )
        return (jnp.where(allow, scores, -1e30), allow, key_tile, value_tile)

    def forward_step(shard, carry):
        peak, total, out_acc = carry
        masked, allow, key_tile, value_tile = block_scores(shard)
        new_peak = jnp.maximum(peak, jnp.max(masked, axis=-1))
        expd = jnp.where(allow, jnp.exp(masked - new_peak[..., None]), 0.0)
        factor = jnp.exp(peak - new_peak)
        total = total * factor + jnp.sum(expd, axis=-1)
        out_acc = out_acc * factor[..., None] + jnp.einsum(
            "hgqk,khd->hgqd",
            expd.astype(jnp.bfloat16),
            value_tile,
            preferred_element_type=jnp.float32,
        )
        return (new_peak, total, out_acc)

    head_layout = (KEY_VALUE_HEADS, QUERY_PER_KV, row_count)
    start_state = (
        jnp.full(head_layout, -1e30, jnp.float32),
        jnp.zeros(head_layout, jnp.float32),
        jnp.zeros((KEY_VALUE_HEADS, QUERY_PER_KV, row_count, HEAD_SIZE), jnp.float32),
    )
    peak, total, out_acc = lax.fori_loop(0, shard_list, forward_step, start_state)
    attn_b = (out_acc / total[..., None]).astype(jnp.bfloat16).transpose(2, 0, 1, 3)
    delta = jnp.sum(
        gradient_heads.astype(jnp.float32) * attn_b.astype(jnp.float32), axis=-1
    ).transpose(1, 2, 0)

    def gradient_update(shard, carry):
        dq_acc, grad_buf = carry
        masked, allow, key_tile, value_tile = block_scores(shard)
        probs = jnp.where(allow, jnp.exp(masked - peak[..., None]), 0.0) / total[..., None]
        probs_b = probs.astype(jnp.bfloat16)
        dprob = jnp.einsum(
            "qhgd,khd->hgqk", gradient_heads, value_tile, preferred_element_type=jnp.float32
        )
        dscore = (probs * (dprob - delta[..., None])).astype(jnp.bfloat16)
        dq_acc = dq_acc + jnp.einsum(
            "hgqk,khd->qhgd", dscore, key_tile, preferred_element_type=jnp.float32
        )
        dk_block = (
            jnp.einsum(
                "hgqk,qhgd->khd", dscore, query_head_rows, preferred_element_type=jnp.float32
            )
            * scale
        ).astype(jnp.bfloat16)
        dv_block = jnp.einsum(
            "hgqk,qhgd->khd", probs_b, gradient_heads, preferred_element_type=jnp.float32
        ).astype(jnp.bfloat16)
        paired = jnp.concatenate(
            (dk_block.reshape(row_count, width), dv_block.reshape(row_count, width)), axis=1
        )
        grad_buf = lax.dynamic_update_slice_in_dim(grad_buf, paired, shard * row_count, 0)
        return (dq_acc, grad_buf)

    blank_buffer = jnp.zeros((row_count * shard_list, 2 * width), jnp.bfloat16)
    dq_acc, grad_buf = lax.fori_loop(
        0,
        shard_list,
        gradient_update,
        (
            jnp.zeros((row_count, KEY_VALUE_HEADS, QUERY_PER_KV, HEAD_SIZE), jnp.float32),
            blank_buffer,
        ),
    )
    grad_queries = (dq_acc * scale).astype(jnp.bfloat16).reshape(row_count, QUERY_HEADS * HEAD_SIZE)
    summed = lax.psum_scatter(
        grad_buf.astype(jnp.float32).astype(jnp.bfloat16), "seq", scatter_dimension=0, tiled=True
    ).astype(jnp.float32)
    grad_keys = summed[:, :width].astype(jnp.bfloat16)
    grad_values = summed[:, width:].astype(jnp.bfloat16)
    grad_hidden = jnp.einsum(
        "kc,dc->kd", grad_values, full_weight, preferred_element_type=jnp.float32
    ).astype(jnp.bfloat16)
    partial_rows = lax.psum_scatter(
        jnp.einsum("kd,kc->dc", tokens, grad_values, preferred_element_type=jnp.float32).astype(
            jnp.bfloat16
        ),
        "dp",
        scatter_dimension=0,
        tiled=True,
    )
    grad_weight = lax.psum(partial_rows, "seq").astype(jnp.float32)
    return (
        attn_b.reshape(row_count, QUERY_HEADS * HEAD_SIZE)[None],
        grad_queries[None],
        grad_keys[None],
        grad_hidden[None],
        grad_weight,
    )


N_DP = 8
ROWS = 128
SHARD = 640
HALF = SHARD // 2
CHUNK = 128
WIDE = N_DP * HALF
CORE_KV = 256
SPARE = 16
CORE_Q = 1280
KEY_AT = WIDE
DOC_AT = KEY_AT + 512
QUERY_AT = DOC_AT + ROWS
COT_AT = QUERY_AT + CORE_Q
PACK = COT_AT + CORE_Q


def params(mib=32):
    return pltpu.CompilerParams(vmem_limit_bytes=mib * 1024 * 1024)


def cost(flops, nbytes):
    return pl.CostEstimate(flops=int(flops), bytes_accessed=int(nbytes), transcendentals=0)


def sds(shape, dtype=BF):
    return jax.ShapeDtypeStruct(shape, dtype)


def swap(x, axis, k):
    size = lax.axis_size(axis)
    return lax.ppermute(x, axis, [(i, i ^ k) for i in range(size)])


def after(x, *others):
    return lax.optimization_barrier((x, *others))[0]


def dot_tt(a, b):
    return lax.dot_general(a, b, (((0,), (0,)), ((), ())), preferred_element_type=F32)


def dot_nt(a, b):
    return lax.dot_general(a, b, (((1,), (1,)), ((), ())), preferred_element_type=F32)


def turn(x):
    return pltpu.roll(x.astype(F32), CHUNK // 2, 1).astype(x.dtype)


def first_half():
    return lax.broadcasted_iota(jnp.int32, (ROWS, CHUNK), 1) < CHUNK // 2


def pack_kernel(h, k, doc, w, q, g, send, keep, w0, h_in, k_in, doc_in, w_in, send_out, keep_out, sems):
    s = lax.axis_index("seq")
    r = lax.axis_index("dp")
    y, c = s // 2, s % 2
    cols = pl.ds(pl.multiple_of(c * CORE_KV, CORE_KV), CORE_KV)
    other = pl.ds(pl.multiple_of((1 - c) * CORE_Q, CORE_Q), CORE_Q)

    def copy(i, src, dst):
        made = pltpu.make_async_copy(src, dst, sems.at[i])
        made.start()
        return made

    w_copies = (
        copy(0, w.at[pl.ds(pl.multiple_of(y * 384, 128), 256), cols], w_in.at[pl.ds(0, 256)]),
        copy(1, w.at[pl.ds(pl.multiple_of(256 + y * 64, 64), 64), cols], w_in.at[pl.ds(256, 64)]),
    )
    blocks = [
        copy(10 + j, h.at[:, pl.ds(pl.multiple_of((r ^ j) * SHARD, 128), SHARD)], h_in.at[:, pl.ds(j * SHARD, SHARD)])
        for j in range(N_DP)
    ]
    small = copy(3, k, k_in), copy(4, doc, doc_in)
    heads = (
        copy(5, q.at[:, other], keep_out.at[:, pl.ds(QUERY_AT, CORE_Q)]),
        copy(6, g.at[:, other], keep_out.at[:, pl.ds(COT_AT, CORE_Q)]),
    )
    for made in w_copies:
        made.wait()
    outs = [copy(7, w_in, w0)]
    low = first_half()
    for p in range(N_DP // 2):
        blocks[2 * p].wait()
        blocks[2 * p + 1].wait()
        for which, (out, dst, part) in enumerate(((send_out, send, 1 - y), (keep_out, keep, y))):
            mids = []
            for i in range(2):
                base = (2 * p + i) * SHARD
                start = pl.multiple_of(base + part * 384, 128)
                out[:, p * SHARD + i * 256 : p * SHARD + (i + 1) * 256] = h_in[:, pl.ds(start, 256)]
                mid = h_in[:, base + 256 : base + 384]
                mids.append(jnp.where(part == i, mid, turn(mid)))
            out[:, p * SHARD + 512 : (p + 1) * SHARD] = jnp.where(low, mids[0], mids[1])
            span = pl.ds(p * SHARD, SHARD)
            outs.append(copy(18 + 4 * which + p, out.at[:, span], dst.at[:, span]))
    for made in small:
        made.wait()
    for out in (send_out, keep_out):
        out[:, KEY_AT:DOC_AT] = k_in[...]
        out[:, DOC_AT:QUERY_AT] = jnp.broadcast_to(doc_in[...].astype(F32), (ROWS, ROWS)).astype(BF)
    rest = pl.ds(KEY_AT, QUERY_AT - KEY_AT)
    outs.append(copy(8, send_out.at[:, rest], send.at[:, rest]))
    for made in heads:
        made.wait()
    rest = pl.ds(KEY_AT, PACK - KEY_AT)
    outs.append(copy(9, keep_out.at[:, rest], keep.at[:, rest]))
    for made in outs:
        made.wait()


def pack(h, k, doc, w, q, g):
    return pl.pallas_call(
        pack_kernel,
        out_shape=(sds((ROWS, QUERY_AT)), sds((ROWS, PACK)), sds((HALF, CORE_KV))),
        in_specs=[ANY] * 6,
        out_specs=(ANY,) * 3,
        scratch_shapes=[
            pltpu.VMEM((ROWS, N_DP * SHARD), BF),
            pltpu.VMEM((ROWS, 2 * CORE_KV), BF),
            pltpu.VMEM((1, ROWS), jnp.int32),
            pltpu.VMEM((HALF, CORE_KV), BF),
            pltpu.VMEM((ROWS, QUERY_AT), BF),
            pltpu.VMEM((ROWS, PACK), BF),
            pltpu.SemaphoreType.DMA((26,)),
        ],
        compiler_params=params(62),
        cost_estimate=cost(0, 3e6),
    )(h, k, doc, w, q, g)


def relay_kernel(p, w, own, ow):
    own[...] = p[:, 0:QUERY_AT]
    ow[...] = w[...]


def relay(p, w):
    return pl.pallas_call(
        relay_kernel,
        out_shape=(sds((ROWS, QUERY_AT)), sds((HALF, CORE_KV))),
        in_specs=[VM] * 2,
        out_specs=(VM,) * 2,
        compiler_params=params(),
        cost_estimate=cost(0, 4e6),
    )(p, w)


def values_kernel(h0, h1, h2, w0, w1, w2, w3, w4, w5, w6, w7, vp_ref, wp_ref):
    ws = (w0, w1, w2, w3, w4, w5, w6, w7)
    for p in range(N_DP // 2):
        a, b = ws[2 * p], ws[2 * p + 1]
        base = p * SHARD
        wp_ref[base : base + 256, :] = a[0:256, :]
        wp_ref[base + 256 : base + 512, :] = b[0:256, :]
        wp_ref[base + 512 : base + 576, :] = a[256:HALF, :]
        wp_ref[base + 576 : base + 640, :] = b[256:HALF, :]
    for t, h in enumerate((h0, h1, h2)):
        vp_ref[t * ROWS : (t + 1) * ROWS, :] = jnp.dot(
            h[:, 0:WIDE], wp_ref[...], preferred_element_type=F32
        ).astype(BF)


def partial_values(hs, ws):
    return pl.pallas_call(
        values_kernel,
        out_shape=(sds((3 * ROWS, CORE_KV)), sds((WIDE, CORE_KV))),
        in_specs=[VM] * 11,
        out_specs=(VM, VM),
        compiler_params=params(),
        cost_estimate=cost(2 * 384 * WIDE * 256, 6e6),
    )(*hs, *ws)


def last_values_kernel(vp, h3, wp, o0, o1):
    last = jnp.dot(h3[:, 0:WIDE], wp[...], preferred_element_type=F32).astype(BF)
    for i, o in enumerate((o0, o1)):
        cols = slice(i * HEAD_SIZE, (i + 1) * HEAD_SIZE)
        o[0 : 3 * ROWS, :] = vp[:, cols]
        o[3 * ROWS :, :] = last[:, cols]


def last_values(vp, h3, wp):
    return pl.pallas_call(
        last_values_kernel,
        out_shape=(sds((4 * ROWS, HEAD_SIZE)),) * 2,
        in_specs=[VM] * 3,
        out_specs=(VM,) * 2,
        compiler_params=params(),
        cost_estimate=cost(2 * 128 * WIDE * 256, 2e6),
    )(vp, h3, wp)


def scores_kernel(q0, p0, p1, p2, p3, e_ref, inv_ref, bias):
    s = lax.axis_index("seq")
    c = s % 2
    factor = HEAD_SIZE ** (-0.5)
    log2e = 1.4426950408889634
    ps = (p0, p1, p2, p3)
    rows = [p[0:16, DOC_AT:QUERY_AT][0:1, :].astype(F32) for p in ps]
    for t in range(4):
        key_doc = jnp.transpose(jnp.broadcast_to(rows[t], (ROWS, ROWS)))
        key_pos = (s ^ t) * ROWS + lax.broadcasted_iota(jnp.int32, (ROWS, ROWS), 0)
        for u in range(2):
            query_pos = (s ^ u) * ROWS + lax.broadcasted_iota(jnp.int32, (ROWS, ROWS), 1)
            allow = (key_pos <= query_pos) & (key_doc == jnp.broadcast_to(rows[u], (ROWS, ROWS)))
            bias[t * ROWS : (t + 1) * ROWS, u * ROWS : (u + 1) * ROWS] = jnp.where(allow, 0.0, -1e30)
    for kvh in range(2):
        cols = pl.ds(pl.multiple_of(KEY_AT + c * CORE_KV + kvh * HEAD_SIZE, HEAD_SIZE), HEAD_SIZE)
        key = jnp.concatenate([p[:, cols] for p in ps], axis=0)
        for i in range(QUERY_PER_KV):
            head = kvh * QUERY_PER_KV + i
            qcols = pl.ds(pl.multiple_of(c * CORE_Q + head * HEAD_SIZE, HEAD_SIZE), HEAD_SIZE)
            far = p1[:, QUERY_AT + head * HEAD_SIZE : QUERY_AT + (head + 1) * HEAD_SIZE]
            query = jnp.concatenate([q0[:, qcols], far], axis=0)
            st = dot_nt(key, query) * (factor * log2e) + bias[...]
            e = jnp.exp2(st - jnp.max(st, axis=0, keepdims=True))
            inv_ref[head * 8 : head * 8 + 8, :] = jnp.broadcast_to(
                1.0 / jnp.sum(e, axis=0, keepdims=True), (8, 2 * ROWS)
            )
            e_ref[head] = e.astype(BF)


def scores(q, ps):
    return pl.pallas_call(
        scores_kernel,
        out_shape=(sds((10, 4 * ROWS, 2 * ROWS)), sds((80, 2 * ROWS), F32)),
        in_specs=[VM] * 5,
        out_specs=(VM,) * 2,
        scratch_shapes=[pltpu.VMEM((4 * ROWS, 2 * ROWS), F32)],
        compiler_params=params(),
        cost_estimate=cost(2 * 10 * 256 * 512 * 128 * 8, 6e6),
    )(q, *ps)


def attend_head(kvh, e_ref, inv_ref, q0, g0, ps, vp, rv):
    c = lax.axis_index("seq") % 2
    factor = HEAD_SIZE ** (-0.5)
    p1 = ps[1]
    cols = pl.ds(pl.multiple_of(KEY_AT + c * CORE_KV + kvh * HEAD_SIZE, HEAD_SIZE), HEAD_SIZE)
    key = jnp.concatenate([p[:, cols] for p in ps], axis=0)
    far = rv[...].astype(F32)
    far = jnp.concatenate([far[2 * ROWS :], far[: 2 * ROWS]], axis=0)
    value = (vp[...].astype(F32) + far).astype(BF)
    dk = jnp.zeros((4 * ROWS, HEAD_SIZE), F32)
    dv = jnp.zeros((4 * ROWS, HEAD_SIZE), F32)
    outs = []
    for i in range(QUERY_PER_KV):
        head = kvh * QUERY_PER_KV + i
        qcols = pl.ds(pl.multiple_of(c * CORE_Q + head * HEAD_SIZE, HEAD_SIZE), HEAD_SIZE)
        low, high = head * HEAD_SIZE, (head + 1) * HEAD_SIZE
        query = jnp.concatenate([q0[:, qcols], p1[:, QUERY_AT + low : QUERY_AT + high]], axis=0)
        cot = jnp.concatenate([g0[:, qcols], p1[:, COT_AT + low : COT_AT + high]], axis=0)
        e = e_ref[head]
        inv = inv_ref[head * 8 : head * 8 + 8, :][0:1, :]
        out = jnp.transpose(dot_tt(value, e) * inv).astype(BF)
        probs = e.astype(F32) * inv
        term = probs * dot_nt(value, cot)
        delta = jnp.sum(term, axis=0, keepdims=True)
        ds = (term - probs * delta).astype(BF)
        dq = jnp.transpose(dot_tt(key, ds) * factor).astype(BF)
        outs.append((out, dq))
        dk = dk + jnp.dot(ds, query, preferred_element_type=F32)
        dv = dv + jnp.dot(probs.astype(BF), cot, preferred_element_type=F32)
    return outs, (dk * factor).astype(BF), dv.astype(BF)


def attention_first_kernel(e_ref, inv_ref, q0, g0, p0, p1, p2, p3, vp, rv, out, dk_ref, dv_ref):
    outs, dk, dv = attend_head(0, e_ref, inv_ref, q0, g0, (p0, p1, p2, p3), vp, rv)
    for i, (o, dq) in enumerate(outs):
        cols = slice(i * HEAD_SIZE, (i + 1) * HEAD_SIZE)
        out[0 : 2 * ROWS, cols] = o
        out[2 * ROWS :, cols] = dq
    dk_ref[...] = dk
    dv_ref[0 : 4 * ROWS, :] = dv
    dv_ref[4 * ROWS :, :] = jnp.zeros((SPARE, HEAD_SIZE), BF)


def attention_second_kernel(
    e_ref, inv_ref, q0, g0, p0, p1, p2, p3, vp, rv, first, first_dk,
    o0, dq0, dk0, dk2, swap_ref, dv_ref,
):
    outs, dk, dv = attend_head(1, e_ref, inv_ref, q0, g0, (p0, p1, p2, p3), vp, rv)
    half = QUERY_PER_KV * HEAD_SIZE
    o0[:, 0:half] = first[0:ROWS, :]
    swap_ref[:, 0:half] = first[ROWS : 2 * ROWS, :]
    dq0[:, 0:half] = first[2 * ROWS : 3 * ROWS, :]
    swap_ref[:, CORE_Q : CORE_Q + half] = first[3 * ROWS :, :]
    for i, (o, dq) in enumerate(outs):
        low, high = half + i * HEAD_SIZE, half + (i + 1) * HEAD_SIZE
        o0[:, low:high] = o[:ROWS]
        swap_ref[:, low:high] = o[ROWS:]
        dq0[:, low:high] = dq[:ROWS]
        swap_ref[:, CORE_Q + low : CORE_Q + high] = dq[ROWS:]
    for kvh, d in enumerate((first_dk[...], dk)):
        mine = slice(kvh * HEAD_SIZE, (kvh + 1) * HEAD_SIZE)
        dk0[:, mine] = d[:ROWS]
        dk2[:, mine] = d[2 * ROWS : 3 * ROWS]
        at = 2 * CORE_Q + kvh * HEAD_SIZE
        swap_ref[:, at : at + HEAD_SIZE] = d[ROWS : 2 * ROWS]
        swap_ref[:, at + CORE_KV : at + CORE_KV + HEAD_SIZE] = d[3 * ROWS :]
    dv_ref[...] = dv


def attention_first(*args):
    return pl.pallas_call(
        attention_first_kernel,
        out_shape=(
            sds((4 * ROWS, QUERY_PER_KV * HEAD_SIZE)), sds((4 * ROWS, HEAD_SIZE)),
            sds((4 * ROWS + SPARE, HEAD_SIZE)),
        ),
        in_specs=[VM] * 10,
        out_specs=(VM,) * 3,
        compiler_params=params(),
        cost_estimate=cost(5 * 10 * 256 * 512 * 128 * 4, 3e6),
    )(*args)


def attention_second(*args):
    return pl.pallas_call(
        attention_second_kernel,
        out_shape=(sds((ROWS, CORE_Q)),) * 2
        + (sds((ROWS, CORE_KV)),) * 2
        + (sds((ROWS, 2 * CORE_Q + 2 * CORE_KV)), sds((4 * ROWS, HEAD_SIZE))),
        in_specs=[VM] * 12,
        out_specs=(VM,) * 6,
        compiler_params=params(),
        cost_estimate=cost(5 * 10 * 256 * 512 * 128 * 4, 3e6),
    )(*args)


def weight_grad_pair(p, hs, gv, *outs):
    acc = jnp.zeros((CHUNK, CORE_KV), F32)
    for t, h in enumerate(hs):
        acc = acc + dot_tt(h[:, p * SHARD + 512 : (p + 1) * SHARD], gv[t * ROWS : (t + 1) * ROWS, :])
    middle = acc.astype(BF)
    for which, out, at in outs:
        acc = jnp.zeros((256, CORE_KV), F32)
        for t, h in enumerate(hs):
            first = p * SHARD + which * 256
            acc = acc + dot_tt(h[:, first : first + 256], gv[t * ROWS : (t + 1) * ROWS, :])
        out[at : at + 256, :] = acc.astype(BF)
        out[at + 256 : at + HALF, :] = middle[which * 64 : (which + 1) * 64]


def value_grad_kernel(dv0, dv1, rdv0, rdv1, gv, gv_keep, gv_send):
    for t in range(4):
        parts = []
        for dv, rdv in ((dv0, rdv0), (dv1, rdv1)):
            a = dv[t * ROWS : (t + 1) * ROWS, :].astype(F32)
            b = rdv[(t ^ 2) * ROWS : ((t ^ 2) + 1) * ROWS, :].astype(F32)
            parts.append(a + b)
        total = jnp.concatenate(parts, axis=1).astype(BF)
        gv[t * ROWS : (t + 1) * ROWS, :] = total
        half = (t // 2) * ROWS
        if t % 2 == 0:
            gv_keep[half : half + ROWS, :] = total
        else:
            gv_send[half : half + ROWS, :] = total


def value_grad(dvs, rdvs):
    return pl.pallas_call(
        value_grad_kernel,
        out_shape=(sds((4 * ROWS, CORE_KV)),) + (sds((2 * ROWS, CORE_KV)),) * 2,
        in_specs=[VM] * 4,
        out_specs=(VM,) * 3,
        compiler_params=params(),
        cost_estimate=cost(0, 1e6),
    )(*dvs, *rdvs)


def weight_grad_sent_kernel(gv, h0, h1, h2, h3, first, second):
    weight_grad_pair(2, (h0, h1, h2, h3), gv, (1, first, 0))
    first[HALF:, :] = jnp.zeros((SPARE, CORE_KV), BF)
    weight_grad_pair(3, (h0, h1, h2, h3), gv, (1, second, 0))


def weight_grad_sent(gv, hs):
    return pl.pallas_call(
        weight_grad_sent_kernel,
        out_shape=(sds((HALF + SPARE, CORE_KV)), sds((HALF, CORE_KV))),
        in_specs=[VM] * 5,
        out_specs=(VM,) * 2,
        compiler_params=params(),
        cost_estimate=cost(256 * WIDE * 256, 2e6),
    )(gv, *hs)


def weight_grad_kept_kernel(gv, h0, h1, h2, h3, first, second):
    weight_grad_pair(2, (h0, h1, h2, h3), gv, (0, first, 0))
    weight_grad_pair(3, (h0, h1, h2, h3), gv, (0, second, 0))


def weight_grad_kept(gv, hs):
    return pl.pallas_call(
        weight_grad_kept_kernel,
        out_shape=(sds((HALF, CORE_KV)),) * 2,
        in_specs=[VM] * 5,
        out_specs=(VM,) * 2,
        compiler_params=params(),
        cost_estimate=cost(256 * WIDE * 256, 2e6),
    )(gv, *hs)


def weight_grad_near_kernel(gv, h0, h1, h2, h3, send, own):
    for p, out in ((1, send), (0, own)):
        weight_grad_pair(p, (h0, h1, h2, h3), gv, (0, out, 0), (1, out, HALF))


def weight_grad_near(gv, hs):
    return pl.pallas_call(
        weight_grad_near_kernel,
        out_shape=(sds((2 * HALF, CORE_KV)),) * 2,
        in_specs=[VM] * 5,
        out_specs=(VM,) * 2,
        compiler_params=params(),
        cost_estimate=cost(512 * WIDE * 256, 4e6),
    )(gv, *hs)


def hidden_grad_kernel(gv, gvs, wp, wps, dk2, swapped, gh0, send_b):
    full = dot_nt(gv[...], wp[...]) + dot_nt(gvs[...], wps[...])
    full = full.astype(BF)
    gh0[...] = full[:ROWS]
    far = full[ROWS:]
    send_b[:, :WIDE] = far
    c = lax.axis_index("seq") % 2
    at = WIDE
    send_b[:, pl.ds(pl.multiple_of(at + c * CORE_KV, CORE_KV), CORE_KV)] = dk2[...]
    send_b[:, pl.ds(pl.multiple_of(at + (1 - c) * CORE_KV, CORE_KV), CORE_KV)] = swapped[
        :, 2 * CORE_Q + CORE_KV :
    ]


def hidden_grad(gv, gvs, wp, wps, dk2, swapped):
    return pl.pallas_call(
        hidden_grad_kernel,
        out_shape=(sds((ROWS, WIDE)), sds((ROWS, WIDE + 2 * CORE_KV))),
        in_specs=[VM] * 6,
        out_specs=(VM,) * 2,
        compiler_params=params(),
        cost_estimate=cost(2 * 256 * WIDE * 512, 6e6),
    )(gv, gvs, wp, wps, dk2, swapped)


def hidden_join_kernel(own_ref, far_ref, dk0, swapped, o_ref, dk_ref):
    s = lax.axis_index("seq")
    y, c = s // 2, s % 2
    r = lax.axis_index("dp")
    low = first_half()
    for p in range(N_DP // 2):
        for i in range(2):
            base = (r ^ (2 * p + i)) * SHARD
            src = slice(p * SHARD + i * 256, p * SHARD + (i + 1) * 256)
            o_ref[:, pl.ds(pl.multiple_of(base + y * 384, 128), 256)] = own_ref[:, src]
            o_ref[:, pl.ds(pl.multiple_of(base + (1 - y) * 384, 128), 256)] = far_ref[:, src]
        own = own_ref[:, p * SHARD + 512 : (p + 1) * SHARD]
        far = far_ref[:, p * SHARD + 512 : (p + 1) * SHARD]
        part0 = jnp.where(y == 0, own, far)
        part1 = jnp.where(y == 0, far, own)
        at0 = pl.multiple_of((r ^ (2 * p)) * SHARD + 256, 128)
        at1 = pl.multiple_of((r ^ (2 * p + 1)) * SHARD + 256, 128)
        o_ref[:, pl.ds(at0, CHUNK)] = jnp.where(low, part0, turn(part1))
        o_ref[:, pl.ds(at1, CHUNK)] = jnp.where(low, turn(part0), part1)
    for place, near in ((c, dk0[...]), (1 - c, swapped[:, 2 * CORE_Q : 2 * CORE_Q + CORE_KV])):
        far = far_ref[:, pl.ds(pl.multiple_of(WIDE + place * CORE_KV, CORE_KV), CORE_KV)]
        dk_ref[:, pl.ds(pl.multiple_of(place * CORE_KV, CORE_KV), CORE_KV)] = (
            near.astype(F32) + far.astype(F32)
        ).astype(BF)


def hidden_join(own, far, dk0, swapped):
    return pl.pallas_call(
        hidden_join_kernel,
        out_shape=(sds((ROWS, N_DP * SHARD)), sds((ROWS, 2 * CORE_KV))),
        in_specs=[VM] * 4,
        out_specs=(VM, VM),
        compiler_params=params(),
        cost_estimate=cost(0, 3e6),
    )(own, far, dk0, swapped)


def heads_join_kernel(o0, dq0, swapped, o_ref, dq_ref):
    c = lax.axis_index("seq") % 2
    near = pl.ds(pl.multiple_of(c * CORE_Q, CORE_Q), CORE_Q)
    far = pl.ds(pl.multiple_of((1 - c) * CORE_Q, CORE_Q), CORE_Q)
    o_ref[:, near] = o0[...]
    o_ref[:, far] = swapped[:, 0:CORE_Q]
    dq_ref[:, near] = dq0[...]
    dq_ref[:, far] = swapped[:, CORE_Q : 2 * CORE_Q]


def heads_join(o0, dq0, swapped):
    return pl.pallas_call(
        heads_join_kernel,
        out_shape=(sds((ROWS, 2 * CORE_Q)),) * 2,
        in_specs=[VM] * 3,
        out_specs=(VM,) * 2,
        compiler_params=params(),
        cost_estimate=cost(0, 4e6),
    )(o0, dq0, swapped)


def add_pair_kernel(a, b, o0, o1):
    total = (a[...].astype(F32) + b[...].astype(F32)).astype(BF)
    o0[...] = total[:HALF]
    o1[...] = total[HALF:]


def add_pair(a, b):
    return pl.pallas_call(
        add_pair_kernel,
        out_shape=(sds((HALF, CORE_KV)),) * 2,
        in_specs=[VM] * 2,
        out_specs=(VM,) * 2,
        compiler_params=params(),
        cost_estimate=cost(0, 1e6),
    )(a, b)


def add_one_kernel(a, b, o):
    o[0:HALF, :] = (a[...].astype(F32) + b[0:HALF, :].astype(F32)).astype(BF)
    if o.shape[0] > HALF:
        o[HALF:, :] = jnp.zeros((o.shape[0] - HALF, CORE_KV), BF)


def add_one(a, b, spare):
    return pl.pallas_call(
        add_one_kernel,
        out_shape=sds((HALF + spare, CORE_KV)),
        in_specs=[VM] * 2,
        out_specs=VM,
        compiler_params=params(),
        cost_estimate=cost(0 if spare else 1e9, 1e3),
    )(a, b)


def add_two_kernel(a, b, o):
    o[...] = a[0:HALF, :].astype(F32) + b[...].astype(F32)


def add_two(a, b):
    return pl.pallas_call(
        add_two_kernel,
        out_shape=sds((HALF, CORE_KV), F32),
        in_specs=[VM] * 2,
        out_specs=VM,
        compiler_params=params(),
        cost_estimate=cost(3e9, 1e6),
    )(a, b)


def add_three_kernel(a, b, c, o):
    o[...] = (a[...] + (b[...].astype(F32) + c[...].astype(F32))).astype(BF)


def add_three(a, b, c):
    return pl.pallas_call(
        add_three_kernel,
        out_shape=sds((HALF, CORE_KV)),
        in_specs=[VM] * 3,
        out_specs=VM,
        compiler_params=params(),
        cost_estimate=cost(0, 1e6),
    )(a, b, c)


def weight_join_kernel(p0, p1, p2, p3, o_ref):
    s = lax.axis_index("seq")
    for t, p in enumerate((p0, p1, p2, p3)):
        y, c = (s ^ t) // 2, (s ^ t) % 2
        cols = pl.ds(pl.multiple_of(c * CORE_KV, CORE_KV), CORE_KV)
        o_ref[pl.ds(pl.multiple_of(y * 384, 128), 256), cols] = p[0:256, :].astype(F32)
        o_ref[pl.ds(pl.multiple_of(256 + y * 64, 64), 64), cols] = p[256:HALF, :].astype(F32)


def weight_join(ps):
    return pl.pallas_call(
        weight_join_kernel,
        out_shape=sds((SHARD, 2 * CORE_KV), F32),
        in_specs=[VM] * 4,
        out_specs=VM,
        compiler_params=params(),
        cost_estimate=cost(0, 2e6),
    )(*ps)


def paired_body(hidden, queries, keys, value_weight, doc_ids, cotangent):
    q, g = queries[0], cotangent[0]
    send, p0, w0 = pack(hidden[0], keys[0], doc_ids, value_weight, q, g)
    p2 = swap(send, "seq", 2)
    w6, w4 = swap(w0, "dp", 6), swap(w0, "dp", 4)
    p1 = swap(p0, "seq", 1)
    later = after(w0, p1)
    w1, w2 = swap(later, "dp", 1), swap(later, "dp", 2)
    w3 = swap(w1, "dp", 2)
    own, w0 = relay(after(p0, p1), w0)
    w7, w5 = swap(after(w6, own), "dp", 1), swap(after(w4, w2), "dp", 1)
    p3 = swap(after(p2, w1, w3, w5, w7), "seq", 1)
    ps = (own, p1, p2, p3)
    vp3, wp = partial_values((own, p1, p2), (w0, w1, w2, w3, w4, w5, w6, w7))
    vp0, vp1 = last_values(vp3, p3, wp)
    rv0, rv1 = swap(vp0, "seq", 2), swap(vp1, "seq", 2)
    e, inv = scores(after(q, vp0), ps)
    wps = swap(wp, "seq", 1)
    first, first_dk, dv0 = attention_first(e, inv, q, g, *ps, vp0, rv0)
    rdv0 = swap(dv0, "seq", 2)
    o0, dq0, dk0, dk2, swap_out, dv1 = attention_second(e, inv, q, g, *ps, vp1, rv1, first, first_dk)
    rdv1 = swap(dv1, "seq", 2)
    gv, gv_keep, gv_send = value_grad((dv0, dv1), (rdv0, rdv1))
    send5, send7 = weight_grad_sent(gv, ps)
    far5, far7 = swap(send5, "dp", 1), swap(send7, "dp", 1)
    own4, own6 = weight_grad_kept(after(gv, send5), ps)
    gvs = swap(gv_send, "seq", 1)
    swapped = swap(after(swap_out, gv), "seq", 1)
    gh0, gh_send = hidden_grad(gv_keep, gvs, wp, wps, dk2, swapped)
    send_b, own_b = weight_grad_near(after(gv, gh0), ps)
    far_b = swap(send_b, "dp", 2)
    s4 = add_one(own4, far5, SPARE)
    t4 = swap(s4, "dp", 4)
    s6 = add_one(own6, after(far7, s4), 0)
    t6 = swap(s6, "dp", 6)
    t46 = add_two(t4, t6)
    s0, s1 = add_pair(own_b, far_b)
    gh_far = swap(gh_send, "seq", 2)
    attn_out, grad_queries = heads_join(o0, dq0, swapped)
    s1, attn_out, grad_queries = lax.optimization_barrier((s1, attn_out, grad_queries))
    t1 = swap(s1, "dp", 1)
    d0 = add_three(t46, s0, t1)
    d2 = swap(d0, "seq", 2)
    d1 = swap(d0, "seq", 1)
    grad_hidden, grad_keys = hidden_join(gh0, gh_far, dk0, swapped)
    d2, grad_hidden, grad_keys = lax.optimization_barrier((d2, grad_hidden, grad_keys))
    d3 = swap(d2, "seq", 1)
    grad_weight = weight_join((d0, d1, d2, d3))
    return attn_out[None], grad_queries[None], grad_keys[None], grad_hidden[None], grad_weight


def solution(mesh):
    in_specs = (
        P("dp", "seq", None),
        P("dp", "seq", None),
        P("dp", "seq", None),
        P("dp", None),
        P("dp", "seq"),
        P("dp", "seq", None),
    )
    out_specs = (
        P("dp", "seq", None),
        P("dp", "seq", None),
        P("dp", "seq", None),
        P("dp", "seq", None),
        P("dp", None),
    )
    paired = mesh.shape["dp"] == N_DP and mesh.shape["seq"] == 4
    return jax.shard_map(
        paired_body if paired else body, mesh=mesh, in_specs=in_specs, out_specs=out_specs, check_vma=False
    )
```

```python
import functools

import jax
import jax.numpy as jnp
from jax import lax
from jax.experimental import pallas as pl
from jax.experimental.pallas import tpu as pltpu
from jax.sharding import PartitionSpec as P

QUERY_HEADS = 20
KEY_VALUE_HEADS = 4
HEAD_SIZE = 128
QUERY_PER_KV = 5

BF = jnp.bfloat16
F32 = jnp.float32
VM = pl.BlockSpec(memory_space=pltpu.VMEM)
ANY = pl.BlockSpec(memory_space=pl.ANY)


def body(hidden, queries, keys, value_weight, doc_ids, cotangent):
    tokens = hidden[0]
    row_count = tokens.shape[0]
    width = value_weight.shape[1]
    scale = HEAD_SIZE ** (-0.5)
    shard_list = lax.axis_size("seq")
    my_index = lax.axis_index("seq")
    full_weight = lax.all_gather(value_weight, "dp", axis=0, tiled=True)
    values_sum = jnp.dot(tokens, full_weight, preferred_element_type=jnp.float32)
    values = values_sum.astype(jnp.bfloat16)
    every_key, every_value, all_docs = (
        lax.all_gather(keys[0], "seq", axis=0, tiled=True),
        lax.all_gather(values, "seq", axis=0, tiled=True),
        lax.all_gather(doc_ids[0], "seq", axis=0, tiled=True),
    )
    query_head_rows = queries[0].reshape(row_count, KEY_VALUE_HEADS, QUERY_PER_KV, HEAD_SIZE)
    gradient_heads = cotangent[0].reshape(row_count, KEY_VALUE_HEADS, QUERY_PER_KV, HEAD_SIZE)
    query_docs = doc_ids[0]
    query_pos = my_index * row_count + jnp.arange(row_count, dtype=jnp.int32)
    local_pos = jnp.arange(row_count, dtype=jnp.int32)

    def block_scores(shard):
        start_offset = shard * row_count
        key_tile = lax.dynamic_slice_in_dim(every_key, start_offset, row_count, 0).reshape(
            row_count, KEY_VALUE_HEADS, HEAD_SIZE
        )
        value_tile = lax.dynamic_slice_in_dim(every_value, start_offset, row_count, 0).reshape(
            row_count, KEY_VALUE_HEADS, HEAD_SIZE
        )
        doc_block = lax.dynamic_slice_in_dim(all_docs, start_offset, row_count, 0)
        scores = (
            jnp.einsum(
                "qhgd,khd->hgqk", query_head_rows, key_tile, preferred_element_type=jnp.float32
            )
            * scale
        )
        allow = ((start_offset + local_pos)[None, :] <= query_pos[:, None]) & (
            doc_block[None, :] == query_docs[:, None]
        )
        return (jnp.where(allow, scores, -1e30), allow, key_tile, value_tile)

    def forward_step(shard, carry):
        peak, total, out_acc = carry
        masked, allow, key_tile, value_tile = block_scores(shard)
        new_peak = jnp.maximum(peak, jnp.max(masked, axis=-1))
        expd = jnp.where(allow, jnp.exp(masked - new_peak[..., None]), 0.0)
        factor = jnp.exp(peak - new_peak)
        total = total * factor + jnp.sum(expd, axis=-1)
        out_acc = out_acc * factor[..., None] + jnp.einsum(
            "hgqk,khd->hgqd",
            expd.astype(jnp.bfloat16),
            value_tile,
            preferred_element_type=jnp.float32,
        )
        return (new_peak, total, out_acc)

    head_layout = (KEY_VALUE_HEADS, QUERY_PER_KV, row_count)
    start_state = (
        jnp.full(head_layout, -1e30, jnp.float32),
        jnp.zeros(head_layout, jnp.float32),
        jnp.zeros((KEY_VALUE_HEADS, QUERY_PER_KV, row_count, HEAD_SIZE), jnp.float32),
    )
    peak, total, out_acc = lax.fori_loop(0, shard_list, forward_step, start_state)
    attn_b = (out_acc / total[..., None]).astype(jnp.bfloat16).transpose(2, 0, 1, 3)
    delta = jnp.sum(
        gradient_heads.astype(jnp.float32) * attn_b.astype(jnp.float32), axis=-1
    ).transpose(1, 2, 0)

    def gradient_update(shard, carry):
        dq_acc, grad_buf = carry
        masked, allow, key_tile, value_tile = block_scores(shard)
        probs = jnp.where(allow, jnp.exp(masked - peak[..., None]), 0.0) / total[..., None]
        probs_b = probs.astype(jnp.bfloat16)
        dprob = jnp.einsum(
            "qhgd,khd->hgqk", gradient_heads, value_tile, preferred_element_type=jnp.float32
        )
        dscore = (probs * (dprob - delta[..., None])).astype(jnp.bfloat16)
        dq_acc = dq_acc + jnp.einsum(
            "hgqk,khd->qhgd", dscore, key_tile, preferred_element_type=jnp.float32
        )
        dk_block = (
            jnp.einsum(
                "hgqk,qhgd->khd", dscore, query_head_rows, preferred_element_type=jnp.float32
            )
            * scale
        ).astype(jnp.bfloat16)
        dv_block = jnp.einsum(
            "hgqk,qhgd->khd", probs_b, gradient_heads, preferred_element_type=jnp.float32
        ).astype(jnp.bfloat16)
        paired = jnp.concatenate(
            (dk_block.reshape(row_count, width), dv_block.reshape(row_count, width)), axis=1
        )
        grad_buf = lax.dynamic_update_slice_in_dim(grad_buf, paired, shard * row_count, 0)
        return (dq_acc, grad_buf)

    blank_buffer = jnp.zeros((row_count * shard_list, 2 * width), jnp.bfloat16)
    dq_acc, grad_buf = lax.fori_loop(
        0,
        shard_list,
        gradient_update,
        (
            jnp.zeros((row_count, KEY_VALUE_HEADS, QUERY_PER_KV, HEAD_SIZE), jnp.float32),
            blank_buffer,
        ),
    )
    grad_queries = (dq_acc * scale).astype(jnp.bfloat16).reshape(row_count, QUERY_HEADS * HEAD_SIZE)
    summed = lax.psum_scatter(
        grad_buf.astype(jnp.float32).astype(jnp.bfloat16), "seq", scatter_dimension=0, tiled=True
    ).astype(jnp.float32)
    grad_keys = summed[:, :width].astype(jnp.bfloat16)
    grad_values = summed[:, width:].astype(jnp.bfloat16)
    grad_hidden = jnp.einsum(
        "kc,dc->kd", grad_values, full_weight, preferred_element_type=jnp.float32
    ).astype(jnp.bfloat16)
    partial_rows = lax.psum_scatter(
        jnp.einsum("kd,kc->dc", tokens, grad_values, preferred_element_type=jnp.float32).astype(
            jnp.bfloat16
        ),
        "dp",
        scatter_dimension=0,
        tiled=True,
    )
    grad_weight = lax.psum(partial_rows, "seq").astype(jnp.float32)
    return (
        attn_b.reshape(row_count, QUERY_HEADS * HEAD_SIZE)[None],
        grad_queries[None],
        grad_keys[None],
        grad_hidden[None],
        grad_weight,
    )


N_DP = 8
ROWS = 128
SHARD = 640
HALF = SHARD // 2
CHUNK = 128
WIDE = N_DP * HALF
CORE_KV = 256
SPARE = 16
CORE_Q = 1280
KEY_AT = WIDE
DOC_AT = KEY_AT + 512
QUERY_AT = DOC_AT + ROWS
COT_AT = QUERY_AT + CORE_Q
PACK = COT_AT + CORE_Q


def params(mib=32):
    return pltpu.CompilerParams(vmem_limit_bytes=mib * 1024 * 1024)


def cost(flops, nbytes):
    return pl.CostEstimate(flops=int(flops), bytes_accessed=int(nbytes), transcendentals=0)


def sds(shape, dtype=BF):
    return jax.ShapeDtypeStruct(shape, dtype)


def swap(x, axis, k):
    size = lax.axis_size(axis)
    return lax.ppermute(x, axis, [(i, i ^ k) for i in range(size)])


def after(x, *others):
    return lax.optimization_barrier((x, *others))[0]


def dot_tt(a, b):
    return lax.dot_general(a, b, (((0,), (0,)), ((), ())), preferred_element_type=F32)


def dot_nt(a, b):
    return lax.dot_general(a, b, (((1,), (1,)), ((), ())), preferred_element_type=F32)


def turn(x):
    return pltpu.roll(x.astype(F32), CHUNK // 2, 1).astype(x.dtype)


def first_half():
    return lax.broadcasted_iota(jnp.int32, (ROWS, CHUNK), 1) < CHUNK // 2


def pack_kernel(h, k, doc, w, q, g, send, keep, w0, h_in, k_in, doc_in, w_in, send_out, keep_out, sems):
    s = lax.axis_index("seq")
    r = lax.axis_index("dp")
    y, c = s // 2, s % 2
    cols = pl.ds(pl.multiple_of(c * CORE_KV, CORE_KV), CORE_KV)
    other = pl.ds(pl.multiple_of((1 - c) * CORE_Q, CORE_Q), CORE_Q)

    def copy(i, src, dst):
        made = pltpu.make_async_copy(src, dst, sems.at[i])
        made.start()
        return made

    w_copies = (
        copy(0, w.at[pl.ds(pl.multiple_of(y * 384, 128), 256), cols], w_in.at[pl.ds(0, 256)]),
        copy(1, w.at[pl.ds(pl.multiple_of(256 + y * 64, 64), 64), cols], w_in.at[pl.ds(256, 64)]),
    )
    blocks = [
        copy(10 + j, h.at[:, pl.ds(pl.multiple_of((r ^ j) * SHARD, 128), SHARD)], h_in.at[:, pl.ds(j * SHARD, SHARD)])
        for j in range(N_DP)
    ]
    small = copy(3, k, k_in), copy(4, doc, doc_in)
    heads = (
        copy(5, q.at[:, other], keep_out.at[:, pl.ds(QUERY_AT, CORE_Q)]),
        copy(6, g.at[:, other], keep_out.at[:, pl.ds(COT_AT, CORE_Q)]),
    )
    for made in w_copies:
        made.wait()
    outs = [copy(7, w_in, w0)]
    low = first_half()
    for p in range(N_DP // 2):
        blocks[2 * p].wait()
        blocks[2 * p + 1].wait()
        for which, (out, dst, part) in enumerate(((send_out, send, 1 - y), (keep_out, keep, y))):
            mids = []
            for i in range(2):
                base = (2 * p + i) * SHARD
                start = pl.multiple_of(base + part * 384, 128)
                out[:, p * SHARD + i * 256 : p * SHARD + (i + 1) * 256] = h_in[:, pl.ds(start, 256)]
                mid = h_in[:, base + 256 : base + 384]
                mids.append(jnp.where(part == i, mid, turn(mid)))
            out[:, p * SHARD + 512 : (p + 1) * SHARD] = jnp.where(low, mids[0], mids[1])
            span = pl.ds(p * SHARD, SHARD)
            outs.append(copy(18 + 4 * which + p, out.at[:, span], dst.at[:, span]))
    for made in small:
        made.wait()
    for out in (send_out, keep_out):
        out[:, KEY_AT:DOC_AT] = k_in[...]
        out[:, DOC_AT:QUERY_AT] = jnp.broadcast_to(doc_in[...].astype(F32), (ROWS, ROWS)).astype(BF)
    rest = pl.ds(KEY_AT, QUERY_AT - KEY_AT)
    outs.append(copy(8, send_out.at[:, rest], send.at[:, rest]))
    for made in heads:
        made.wait()
    rest = pl.ds(KEY_AT, PACK - KEY_AT)
    outs.append(copy(9, keep_out.at[:, rest], keep.at[:, rest]))
    for made in outs:
        made.wait()


def pack(h, k, doc, w, q, g):
    return pl.pallas_call(
        pack_kernel,
        out_shape=(sds((ROWS, QUERY_AT)), sds((ROWS, PACK)), sds((HALF, CORE_KV))),
        in_specs=[ANY] * 6,
        out_specs=(ANY,) * 3,
        scratch_shapes=[
            pltpu.VMEM((ROWS, N_DP * SHARD), BF),
            pltpu.VMEM((ROWS, 2 * CORE_KV), BF),
            pltpu.VMEM((1, ROWS), jnp.int32),
            pltpu.VMEM((HALF, CORE_KV), BF),
            pltpu.VMEM((ROWS, QUERY_AT), BF),
            pltpu.VMEM((ROWS, PACK), BF),
            pltpu.SemaphoreType.DMA((26,)),
        ],
        compiler_params=params(62),
        cost_estimate=cost(0, 3e6),
    )(h, k, doc, w, q, g)


def relay_kernel(p, w, own, ow):
    own[...] = p[:, 0:QUERY_AT]
    ow[...] = w[...]


def relay(p, w):
    return pl.pallas_call(
        relay_kernel,
        out_shape=(sds((ROWS, QUERY_AT)), sds((HALF, CORE_KV))),
        in_specs=[VM] * 2,
        out_specs=(VM,) * 2,
        compiler_params=params(),
        cost_estimate=cost(0, 4e6),
    )(p, w)


def values_kernel(h0, h1, h2, w0, w1, w2, w3, w4, w5, w6, w7, vp_ref, wp_ref):
    ws = (w0, w1, w2, w3, w4, w5, w6, w7)
    for p in range(N_DP // 2):
        a, b = ws[2 * p], ws[2 * p + 1]
        base = p * SHARD
        wp_ref[base : base + 256, :] = a[0:256, :]
        wp_ref[base + 256 : base + 512, :] = b[0:256, :]
        wp_ref[base + 512 : base + 576, :] = a[256:HALF, :]
        wp_ref[base + 576 : base + 640, :] = b[256:HALF, :]
    for t, h in enumerate((h0, h1, h2)):
        vp_ref[t * ROWS : (t + 1) * ROWS, :] = jnp.dot(
            h[:, 0:WIDE], wp_ref[...], preferred_element_type=F32
        ).astype(BF)


def partial_values(hs, ws):
    return pl.pallas_call(
        values_kernel,
        out_shape=(sds((3 * ROWS, CORE_KV)), sds((WIDE, CORE_KV))),
        in_specs=[VM] * 11,
        out_specs=(VM, VM),
        compiler_params=params(),
        cost_estimate=cost(2 * 384 * WIDE * 256, 6e6),
    )(*hs, *ws)


def last_values_kernel(vp, h3, wp, o0, o1):
    last = jnp.dot(h3[:, 0:WIDE], wp[...], preferred_element_type=F32).astype(BF)
    for i, o in enumerate((o0, o1)):
        cols = slice(i * HEAD_SIZE, (i + 1) * HEAD_SIZE)
        o[0 : 3 * ROWS, :] = vp[:, cols]
        o[3 * ROWS :, :] = last[:, cols]


def last_values(vp, h3, wp):
    return pl.pallas_call(
        last_values_kernel,
        out_shape=(sds((4 * ROWS, HEAD_SIZE)),) * 2,
        in_specs=[VM] * 3,
        out_specs=(VM,) * 2,
        compiler_params=params(),
        cost_estimate=cost(2 * 128 * WIDE * 256, 2e6),
    )(vp, h3, wp)


def scores_kernel(q0, p0, p1, p2, p3, e_ref, inv_ref, bias):
    s = lax.axis_index("seq")
    c = s % 2
    factor = HEAD_SIZE ** (-0.5)
    log2e = 1.4426950408889634
    ps = (p0, p1, p2, p3)
    rows = [p[0:16, DOC_AT:QUERY_AT][0:1, :].astype(F32) for p in ps]
    for t in range(4):
        key_doc = jnp.transpose(jnp.broadcast_to(rows[t], (ROWS, ROWS)))
        key_pos = (s ^ t) * ROWS + lax.broadcasted_iota(jnp.int32, (ROWS, ROWS), 0)
        for u in range(2):
            query_pos = (s ^ u) * ROWS + lax.broadcasted_iota(jnp.int32, (ROWS, ROWS), 1)
            allow = (key_pos <= query_pos) & (key_doc == jnp.broadcast_to(rows[u], (ROWS, ROWS)))
            bias[t * ROWS : (t + 1) * ROWS, u * ROWS : (u + 1) * ROWS] = jnp.where(allow, 0.0, -1e30)
    for kvh in range(2):
        cols = pl.ds(pl.multiple_of(KEY_AT + c * CORE_KV + kvh * HEAD_SIZE, HEAD_SIZE), HEAD_SIZE)
        key = jnp.concatenate([p[:, cols] for p in ps], axis=0)
        for i in range(QUERY_PER_KV):
            head = kvh * QUERY_PER_KV + i
            qcols = pl.ds(pl.multiple_of(c * CORE_Q + head * HEAD_SIZE, HEAD_SIZE), HEAD_SIZE)
            far = p1[:, QUERY_AT + head * HEAD_SIZE : QUERY_AT + (head + 1) * HEAD_SIZE]
            query = jnp.concatenate([q0[:, qcols], far], axis=0)
            st = dot_nt(key, query) * (factor * log2e) + bias[...]
            e = jnp.exp2(st - jnp.max(st, axis=0, keepdims=True))
            inv_ref[head * 8 : head * 8 + 8, :] = jnp.broadcast_to(
                1.0 / jnp.sum(e, axis=0, keepdims=True), (8, 2 * ROWS)
            )
            e_ref[head] = e.astype(BF)


def scores(q, ps):
    return pl.pallas_call(
        scores_kernel,
        out_shape=(sds((10, 4 * ROWS, 2 * ROWS)), sds((80, 2 * ROWS), F32)),
        in_specs=[VM] * 5,
        out_specs=(VM,) * 2,
        scratch_shapes=[pltpu.VMEM((4 * ROWS, 2 * ROWS), F32)],
        compiler_params=params(),
        cost_estimate=cost(2 * 10 * 256 * 512 * 128 * 8, 6e6),
    )(q, *ps)


def attend_head(kvh, e_ref, inv_ref, q0, g0, ps, vp, rv):
    c = lax.axis_index("seq") % 2
    factor = HEAD_SIZE ** (-0.5)
    p1 = ps[1]
    cols = pl.ds(pl.multiple_of(KEY_AT + c * CORE_KV + kvh * HEAD_SIZE, HEAD_SIZE), HEAD_SIZE)
    key = jnp.concatenate([p[:, cols] for p in ps], axis=0)
    far = rv[...].astype(F32)
    far = jnp.concatenate([far[2 * ROWS :], far[: 2 * ROWS]], axis=0)
    value = (vp[...].astype(F32) + far).astype(BF)
    dk = jnp.zeros((4 * ROWS, HEAD_SIZE), F32)
    dv = jnp.zeros((4 * ROWS, HEAD_SIZE), F32)
    outs = []
    for i in range(QUERY_PER_KV):
        head = kvh * QUERY_PER_KV + i
        qcols = pl.ds(pl.multiple_of(c * CORE_Q + head * HEAD_SIZE, HEAD_SIZE), HEAD_SIZE)
        low, high = head * HEAD_SIZE, (head + 1) * HEAD_SIZE
        query = jnp.concatenate([q0[:, qcols], p1[:, QUERY_AT + low : QUERY_AT + high]], axis=0)
        cot = jnp.concatenate([g0[:, qcols], p1[:, COT_AT + low : COT_AT + high]], axis=0)
        e = e_ref[head]
        inv = inv_ref[head * 8 : head * 8 + 8, :][0:1, :]
        out = jnp.transpose(dot_tt(value, e) * inv).astype(BF)
        probs = e.astype(F32) * inv
        term = probs * dot_nt(value, cot)
        delta = jnp.sum(term, axis=0, keepdims=True)
        ds = (term - probs * delta).astype(BF)
        dq = jnp.transpose(dot_tt(key, ds) * factor).astype(BF)
        outs.append((out, dq))
        dk = dk + jnp.dot(ds, query, preferred_element_type=F32)
        dv = dv + jnp.dot(probs.astype(BF), cot, preferred_element_type=F32)
    return outs, (dk * factor).astype(BF), dv.astype(BF)


def attention_first_kernel(e_ref, inv_ref, q0, g0, p0, p1, p2, p3, vp, rv, out, dk_ref, dv_ref):
    outs, dk, dv = attend_head(0, e_ref, inv_ref, q0, g0, (p0, p1, p2, p3), vp, rv)
    for i, (o, dq) in enumerate(outs):
        cols = slice(i * HEAD_SIZE, (i + 1) * HEAD_SIZE)
        out[0 : 2 * ROWS, cols] = o
        out[2 * ROWS :, cols] = dq
    dk_ref[...] = dk
    dv_ref[0 : 4 * ROWS, :] = dv
    dv_ref[4 * ROWS :, :] = jnp.zeros((SPARE, HEAD_SIZE), BF)


def attention_second_kernel(
    e_ref, inv_ref, q0, g0, p0, p1, p2, p3, vp, rv, first, first_dk,
    o0, dq0, dk0, dk2, swap_ref, dv_ref,
):
    outs, dk, dv = attend_head(1, e_ref, inv_ref, q0, g0, (p0, p1, p2, p3), vp, rv)
    half = QUERY_PER_KV * HEAD_SIZE
    o0[:, 0:half] = first[0:ROWS, :]
    swap_ref[:, 0:half] = first[ROWS : 2 * ROWS, :]
    dq0[:, 0:half] = first[2 * ROWS : 3 * ROWS, :]
    swap_ref[:, CORE_Q : CORE_Q + half] = first[3 * ROWS :, :]
    for i, (o, dq) in enumerate(outs):
        low, high = half + i * HEAD_SIZE, half + (i + 1) * HEAD_SIZE
        o0[:, low:high] = o[:ROWS]
        swap_ref[:, low:high] = o[ROWS:]
        dq0[:, low:high] = dq[:ROWS]
        swap_ref[:, CORE_Q + low : CORE_Q + high] = dq[ROWS:]
    for kvh, d in enumerate((first_dk[...], dk)):
        mine = slice(kvh * HEAD_SIZE, (kvh + 1) * HEAD_SIZE)
        dk0[:, mine] = d[:ROWS]
        dk2[:, mine] = d[2 * ROWS : 3 * ROWS]
        at = 2 * CORE_Q + kvh * HEAD_SIZE
        swap_ref[:, at : at + HEAD_SIZE] = d[ROWS : 2 * ROWS]
        swap_ref[:, at + CORE_KV : at + CORE_KV + HEAD_SIZE] = d[3 * ROWS :]
    dv_ref[...] = dv


def attention_first(*args):
    return pl.pallas_call(
        attention_first_kernel,
        out_shape=(
            sds((4 * ROWS, QUERY_PER_KV * HEAD_SIZE)), sds((4 * ROWS, HEAD_SIZE)),
            sds((4 * ROWS + SPARE, HEAD_SIZE)),
        ),
        in_specs=[VM] * 10,
        out_specs=(VM,) * 3,
        compiler_params=params(),
        cost_estimate=cost(5 * 10 * 256 * 512 * 128 * 4, 3e6),
    )(*args)


def attention_second(*args):
    return pl.pallas_call(
        attention_second_kernel,
        out_shape=(sds((ROWS, CORE_Q)),) * 2
        + (sds((ROWS, CORE_KV)),) * 2
        + (sds((ROWS, 2 * CORE_Q + 2 * CORE_KV)), sds((4 * ROWS, HEAD_SIZE))),
        in_specs=[VM] * 12,
        out_specs=(VM,) * 6,
        compiler_params=params(),
        cost_estimate=cost(5 * 10 * 256 * 512 * 128 * 4, 3e6),
    )(*args)


def weight_grad_pair(p, hs, gv, *outs):
    acc = jnp.zeros((CHUNK, CORE_KV), F32)
    for t, h in enumerate(hs):
        acc = acc + dot_tt(h[:, p * SHARD + 512 : (p + 1) * SHARD], gv[t * ROWS : (t + 1) * ROWS, :])
    middle = acc.astype(BF)
    for which, out, at in outs:
        acc = jnp.zeros((256, CORE_KV), F32)
        for t, h in enumerate(hs):
            first = p * SHARD + which * 256
            acc = acc + dot_tt(h[:, first : first + 256], gv[t * ROWS : (t + 1) * ROWS, :])
        out[at : at + 256, :] = acc.astype(BF)
        out[at + 256 : at + HALF, :] = middle[which * 64 : (which + 1) * 64]


def value_grad_kernel(dv0, dv1, rdv0, rdv1, gv, gv_keep, gv_send):
    for t in range(4):
        parts = []
        for dv, rdv in ((dv0, rdv0), (dv1, rdv1)):
            a = dv[t * ROWS : (t + 1) * ROWS, :].astype(F32)
            b = rdv[(t ^ 2) * ROWS : ((t ^ 2) + 1) * ROWS, :].astype(F32)
            parts.append(a + b)
        total = jnp.concatenate(parts, axis=1).astype(BF)
        gv[t * ROWS : (t + 1) * ROWS, :] = total
        half = (t // 2) * ROWS
        if t % 2 == 0:
            gv_keep[half : half + ROWS, :] = total
        else:
            gv_send[half : half + ROWS, :] = total


def value_grad(dvs, rdvs):
    return pl.pallas_call(
        value_grad_kernel,
        out_shape=(sds((4 * ROWS, CORE_KV)),) + (sds((2 * ROWS, CORE_KV)),) * 2,
        in_specs=[VM] * 4,
        out_specs=(VM,) * 3,
        compiler_params=params(),
        cost_estimate=cost(0, 1e6),
    )(*dvs, *rdvs)


def weight_grad_sent_kernel(gv, h0, h1, h2, h3, first, second):
    weight_grad_pair(2, (h0, h1, h2, h3), gv, (1, first, 0))
    first[HALF:, :] = jnp.zeros((SPARE, CORE_KV), BF)
    weight_grad_pair(3, (h0, h1, h2, h3), gv, (1, second, 0))


def weight_grad_sent(gv, hs):
    return pl.pallas_call(
        weight_grad_sent_kernel,
        out_shape=(sds((HALF + SPARE, CORE_KV)), sds((HALF, CORE_KV))),
        in_specs=[VM] * 5,
        out_specs=(VM,) * 2,
        compiler_params=params(),
        cost_estimate=cost(256 * WIDE * 256, 2e6),
    )(gv, *hs)


def weight_grad_kept_kernel(gv, h0, h1, h2, h3, first, second):
    weight_grad_pair(2, (h0, h1, h2, h3), gv, (0, first, 0))
    weight_grad_pair(3, (h0, h1, h2, h3), gv, (0, second, 0))


def weight_grad_kept(gv, hs):
    return pl.pallas_call(
        weight_grad_kept_kernel,
        out_shape=(sds((HALF, CORE_KV)),) * 2,
        in_specs=[VM] * 5,
        out_specs=(VM,) * 2,
        compiler_params=params(),
        cost_estimate=cost(256 * WIDE * 256, 2e6),
    )(gv, *hs)


def weight_grad_near_kernel(gv, h0, h1, h2, h3, send, own):
    for p, out in ((1, send), (0, own)):
        weight_grad_pair(p, (h0, h1, h2, h3), gv, (0, out, 0), (1, out, HALF))


def weight_grad_near(gv, hs):
    return pl.pallas_call(
        weight_grad_near_kernel,
        out_shape=(sds((2 * HALF, CORE_KV)),) * 2,
        in_specs=[VM] * 5,
        out_specs=(VM,) * 2,
        compiler_params=params(),
        cost_estimate=cost(512 * WIDE * 256, 4e6),
    )(gv, *hs)


def hidden_grad_kernel(gv, gvs, wp, wps, dk2, swapped, gh0, send_b):
    full = dot_nt(gv[...], wp[...]) + dot_nt(gvs[...], wps[...])
    full = full.astype(BF)
    gh0[...] = full[:ROWS]
    far = full[ROWS:]
    send_b[:, :WIDE] = far
    c = lax.axis_index("seq") % 2
    at = WIDE
    send_b[:, pl.ds(pl.multiple_of(at + c * CORE_KV, CORE_KV), CORE_KV)] = dk2[...]
    send_b[:, pl.ds(pl.multiple_of(at + (1 - c) * CORE_KV, CORE_KV), CORE_KV)] = swapped[
        :, 2 * CORE_Q + CORE_KV :
    ]


def hidden_grad(gv, gvs, wp, wps, dk2, swapped):
    return pl.pallas_call(
        hidden_grad_kernel,
        out_shape=(sds((ROWS, WIDE)), sds((ROWS, WIDE + 2 * CORE_KV))),
        in_specs=[VM] * 6,
        out_specs=(VM,) * 2,
        compiler_params=params(),
        cost_estimate=cost(2 * 256 * WIDE * 512, 6e6),
    )(gv, gvs, wp, wps, dk2, swapped)


def hidden_join_kernel(own_ref, far_ref, dk0, swapped, o_ref, dk_ref):
    s = lax.axis_index("seq")
    y, c = s // 2, s % 2
    r = lax.axis_index("dp")
    low = first_half()
    for p in range(N_DP // 2):
        for i in range(2):
            base = (r ^ (2 * p + i)) * SHARD
            src = slice(p * SHARD + i * 256, p * SHARD + (i + 1) * 256)
            o_ref[:, pl.ds(pl.multiple_of(base + y * 384, 128), 256)] = own_ref[:, src]
            o_ref[:, pl.ds(pl.multiple_of(base + (1 - y) * 384, 128), 256)] = far_ref[:, src]
        own = own_ref[:, p * SHARD + 512 : (p + 1) * SHARD]
        far = far_ref[:, p * SHARD + 512 : (p + 1) * SHARD]
        part0 = jnp.where(y == 0, own, far)
        part1 = jnp.where(y == 0, far, own)
        at0 = pl.multiple_of((r ^ (2 * p)) * SHARD + 256, 128)
        at1 = pl.multiple_of((r ^ (2 * p + 1)) * SHARD + 256, 128)
        o_ref[:, pl.ds(at0, CHUNK)] = jnp.where(low, part0, turn(part1))
        o_ref[:, pl.ds(at1, CHUNK)] = jnp.where(low, turn(part0), part1)
    for place, near in ((c, dk0[...]), (1 - c, swapped[:, 2 * CORE_Q : 2 * CORE_Q + CORE_KV])):
        far = far_ref[:, pl.ds(pl.multiple_of(WIDE + place * CORE_KV, CORE_KV), CORE_KV)]
        dk_ref[:, pl.ds(pl.multiple_of(place * CORE_KV, CORE_KV), CORE_KV)] = (
            near.astype(F32) + far.astype(F32)
        ).astype(BF)


def hidden_join(own, far, dk0, swapped):
    return pl.pallas_call(
        hidden_join_kernel,
        out_shape=(sds((ROWS, N_DP * SHARD)), sds((ROWS, 2 * CORE_KV))),
        in_specs=[VM] * 4,
        out_specs=(VM, VM),
        compiler_params=params(),
        cost_estimate=cost(0, 3e6),
    )(own, far, dk0, swapped)


def heads_join_kernel(o0, dq0, swapped, o_ref, dq_ref):
    c = lax.axis_index("seq") % 2
    near = pl.ds(pl.multiple_of(c * CORE_Q, CORE_Q), CORE_Q)
    far = pl.ds(pl.multiple_of((1 - c) * CORE_Q, CORE_Q), CORE_Q)
    o_ref[:, near] = o0[...]
    o_ref[:, far] = swapped[:, 0:CORE_Q]
    dq_ref[:, near] = dq0[...]
    dq_ref[:, far] = swapped[:, CORE_Q : 2 * CORE_Q]


def heads_join(o0, dq0, swapped):
    return pl.pallas_call(
        heads_join_kernel,
        out_shape=(sds((ROWS, 2 * CORE_Q)),) * 2,
        in_specs=[VM] * 3,
        out_specs=(VM,) * 2,
        compiler_params=params(),
        cost_estimate=cost(0, 4e6),
    )(o0, dq0, swapped)


def add_pair_kernel(a, b, o0, o1):
    total = (a[...].astype(F32) + b[...].astype(F32)).astype(BF)
    o0[...] = total[:HALF]
    o1[...] = total[HALF:]


def add_pair(a, b):
    return pl.pallas_call(
        add_pair_kernel,
        out_shape=(sds((HALF, CORE_KV)),) * 2,
        in_specs=[VM] * 2,
        out_specs=(VM,) * 2,
        compiler_params=params(),
        cost_estimate=cost(0, 1e6),
    )(a, b)


def add_one_kernel(a, b, o):
    o[0:HALF, :] = (a[...].astype(F32) + b[0:HALF, :].astype(F32)).astype(BF)
    if o.shape[0] > HALF:
        o[HALF:, :] = jnp.zeros((o.shape[0] - HALF, CORE_KV), BF)


def add_one(a, b, spare):
    return pl.pallas_call(
        add_one_kernel,
        out_shape=sds((HALF + spare, CORE_KV)),
        in_specs=[VM] * 2,
        out_specs=VM,
        compiler_params=params(),
        cost_estimate=cost(1e9, 1e3),
    )(a, b)


def add_two_kernel(a, b, o):
    o[...] = a[...].astype(F32) + b[...].astype(F32)


def add_two(a, b):
    return pl.pallas_call(
        add_two_kernel,
        out_shape=sds((HALF, CORE_KV), F32),
        in_specs=[VM] * 2,
        out_specs=VM,
        compiler_params=params(),
        cost_estimate=cost(3e9, 1e6),
    )(a, b)


def add_three_kernel(a, b, c, o):
    o[...] = (a[...] + (b[...].astype(F32) + c[...].astype(F32))).astype(BF)


def add_three(a, b, c):
    return pl.pallas_call(
        add_three_kernel,
        out_shape=sds((HALF, CORE_KV)),
        in_specs=[VM] * 3,
        out_specs=VM,
        compiler_params=params(),
        cost_estimate=cost(0, 1e6),
    )(a, b, c)


def weight_join_kernel(p0, p1, p2, p3, o_ref):
    s = lax.axis_index("seq")
    for t, p in enumerate((p0, p1, p2, p3)):
        y, c = (s ^ t) // 2, (s ^ t) % 2
        cols = pl.ds(pl.multiple_of(c * CORE_KV, CORE_KV), CORE_KV)
        o_ref[pl.ds(pl.multiple_of(y * 384, 128), 256), cols] = p[0:256, :].astype(F32)
        o_ref[pl.ds(pl.multiple_of(256 + y * 64, 64), 64), cols] = p[256:HALF, :].astype(F32)


def weight_join(ps):
    return pl.pallas_call(
        weight_join_kernel,
        out_shape=sds((SHARD, 2 * CORE_KV), F32),
        in_specs=[VM] * 4,
        out_specs=VM,
        compiler_params=params(),
        cost_estimate=cost(0, 2e6),
    )(*ps)


def paired_body(hidden, queries, keys, value_weight, doc_ids, cotangent):
    q, g = queries[0], cotangent[0]
    send, p0, w0 = pack(hidden[0], keys[0], doc_ids, value_weight, q, g)
    p2 = swap(send, "seq", 2)
    w6, w4 = swap(w0, "dp", 6), swap(w0, "dp", 4)
    p1 = swap(p0, "seq", 1)
    later = after(w0, p1)
    w1, w2 = swap(later, "dp", 1), swap(later, "dp", 2)
    w3 = swap(w1, "dp", 2)
    own, w0 = relay(after(p0, p1), w0)
    w7, w5 = swap(after(w6, own), "dp", 1), swap(after(w4, w2), "dp", 1)
    p3 = swap(after(p2, w1, w3, w5, w7), "seq", 1)
    ps = (own, p1, p2, p3)
    vp3, wp = partial_values((own, p1, p2), (w0, w1, w2, w3, w4, w5, w6, w7))
    vp0, vp1 = last_values(vp3, p3, wp)
    rv0, rv1 = swap(vp0, "seq", 2), swap(vp1, "seq", 2)
    e, inv = scores(after(q, vp0), ps)
    wps = swap(wp, "seq", 1)
    first, first_dk, dv0 = attention_first(e, inv, q, g, *ps, vp0, rv0)
    rdv0 = swap(dv0, "seq", 2)
    o0, dq0, dk0, dk2, swap_out, dv1 = attention_second(e, inv, q, g, *ps, vp1, rv1, first, first_dk)
    rdv1 = swap(dv1, "seq", 2)
    gv, gv_keep, gv_send = value_grad((dv0, dv1), (rdv0, rdv1))
    send5, send7 = weight_grad_sent(gv, ps)
    far5, far7 = swap(send5, "dp", 1), swap(send7, "dp", 1)
    own4, own6 = weight_grad_kept(after(gv, send5), ps)
    gvs = swap(gv_send, "seq", 1)
    swapped = swap(after(swap_out, gv), "seq", 1)
    gh0, gh_send = hidden_grad(gv_keep, gvs, wp, wps, dk2, swapped)
    send_b, own_b = weight_grad_near(after(gv, gh0), ps)
    far_b = swap(send_b, "dp", 2)
    s4 = add_one(own4, far5, 0)
    t4 = swap(s4, "dp", 4)
    s6 = add_one(own6, after(far7, s4), 0)
    t6 = swap(s6, "dp", 6)
    t46 = add_two(t4, t6)
    s0, s1 = add_pair(own_b, far_b)
    gh_far = swap(gh_send, "seq", 2)
    attn_out, grad_queries = heads_join(o0, dq0, swapped)
    s1, attn_out, grad_queries = lax.optimization_barrier((s1, attn_out, grad_queries))
    t1 = swap(s1, "dp", 1)
    d0 = add_three(t46, s0, t1)
    d2 = swap(d0, "seq", 2)
    d1 = swap(d0, "seq", 1)
    grad_hidden, grad_keys = hidden_join(gh0, gh_far, dk0, swapped)
    d2, grad_hidden, grad_keys = lax.optimization_barrier((d2, grad_hidden, grad_keys))
    d3 = swap(d2, "seq", 1)
    grad_weight = weight_join((d0, d1, d2, d3))
    return attn_out[None], grad_queries[None], grad_keys[None], grad_hidden[None], grad_weight


def solution(mesh):
    in_specs = (
        P("dp", "seq", None),
        P("dp", "seq", None),
        P("dp", "seq", None),
        P("dp", None),
        P("dp", "seq"),
        P("dp", "seq", None),
    )
    out_specs = (
        P("dp", "seq", None),
        P("dp", "seq", None),
        P("dp", "seq", None),
        P("dp", "seq", None),
        P("dp", None),
    )
    paired = mesh.shape["dp"] == N_DP and mesh.shape["seq"] == 4
    return jax.shard_map(
        paired_body if paired else body, mesh=mesh, in_specs=in_specs, out_specs=out_specs, check_vma=False
    )
```

```python
import functools

import jax
import jax.numpy as jnp
from jax import lax
from jax.experimental import pallas as pl
from jax.experimental.pallas import tpu as pltpu
from jax.sharding import PartitionSpec as P

QUERY_HEADS = 20
KEY_VALUE_HEADS = 4
HEAD_SIZE = 128
QUERY_PER_KV = 5

BF = jnp.bfloat16
F32 = jnp.float32
VM = pl.BlockSpec(memory_space=pltpu.VMEM)
ANY = pl.BlockSpec(memory_space=pl.ANY)


def body(hidden, queries, keys, value_weight, doc_ids, cotangent):
    tokens = hidden[0]
    row_count = tokens.shape[0]
    width = value_weight.shape[1]
    scale = HEAD_SIZE ** (-0.5)
    shard_list = lax.axis_size("seq")
    my_index = lax.axis_index("seq")
    full_weight = lax.all_gather(value_weight, "dp", axis=0, tiled=True)
    values_sum = jnp.dot(tokens, full_weight, preferred_element_type=jnp.float32)
    values = values_sum.astype(jnp.bfloat16)
    every_key, every_value, all_docs = (
        lax.all_gather(keys[0], "seq", axis=0, tiled=True),
        lax.all_gather(values, "seq", axis=0, tiled=True),
        lax.all_gather(doc_ids[0], "seq", axis=0, tiled=True),
    )
    query_head_rows = queries[0].reshape(row_count, KEY_VALUE_HEADS, QUERY_PER_KV, HEAD_SIZE)
    gradient_heads = cotangent[0].reshape(row_count, KEY_VALUE_HEADS, QUERY_PER_KV, HEAD_SIZE)
    query_docs = doc_ids[0]
    query_pos = my_index * row_count + jnp.arange(row_count, dtype=jnp.int32)
    local_pos = jnp.arange(row_count, dtype=jnp.int32)

    def block_scores(shard):
        start_offset = shard * row_count
        key_tile = lax.dynamic_slice_in_dim(every_key, start_offset, row_count, 0).reshape(
            row_count, KEY_VALUE_HEADS, HEAD_SIZE
        )
        value_tile = lax.dynamic_slice_in_dim(every_value, start_offset, row_count, 0).reshape(
            row_count, KEY_VALUE_HEADS, HEAD_SIZE
        )
        doc_block = lax.dynamic_slice_in_dim(all_docs, start_offset, row_count, 0)
        scores = (
            jnp.einsum(
                "qhgd,khd->hgqk", query_head_rows, key_tile, preferred_element_type=jnp.float32
            )
            * scale
        )
        allow = ((start_offset + local_pos)[None, :] <= query_pos[:, None]) & (
            doc_block[None, :] == query_docs[:, None]
        )
        return (jnp.where(allow, scores, -1e30), allow, key_tile, value_tile)

    def forward_step(shard, carry):
        peak, total, out_acc = carry
        masked, allow, key_tile, value_tile = block_scores(shard)
        new_peak = jnp.maximum(peak, jnp.max(masked, axis=-1))
        expd = jnp.where(allow, jnp.exp(masked - new_peak[..., None]), 0.0)
        factor = jnp.exp(peak - new_peak)
        total = total * factor + jnp.sum(expd, axis=-1)
        out_acc = out_acc * factor[..., None] + jnp.einsum(
            "hgqk,khd->hgqd",
            expd.astype(jnp.bfloat16),
            value_tile,
            preferred_element_type=jnp.float32,
        )
        return (new_peak, total, out_acc)

    head_layout = (KEY_VALUE_HEADS, QUERY_PER_KV, row_count)
    start_state = (
        jnp.full(head_layout, -1e30, jnp.float32),
        jnp.zeros(head_layout, jnp.float32),
        jnp.zeros((KEY_VALUE_HEADS, QUERY_PER_KV, row_count, HEAD_SIZE), jnp.float32),
    )
    peak, total, out_acc = lax.fori_loop(0, shard_list, forward_step, start_state)
    attn_b = (out_acc / total[..., None]).astype(jnp.bfloat16).transpose(2, 0, 1, 3)
    delta = jnp.sum(
        gradient_heads.astype(jnp.float32) * attn_b.astype(jnp.float32), axis=-1
    ).transpose(1, 2, 0)

    def gradient_update(shard, carry):
        dq_acc, grad_buf = carry
        masked, allow, key_tile, value_tile = block_scores(shard)
        probs = jnp.where(allow, jnp.exp(masked - peak[..., None]), 0.0) / total[..., None]
        probs_b = probs.astype(jnp.bfloat16)
        dprob = jnp.einsum(
            "qhgd,khd->hgqk", gradient_heads, value_tile, preferred_element_type=jnp.float32
        )
        dscore = (probs * (dprob - delta[..., None])).astype(jnp.bfloat16)
        dq_acc = dq_acc + jnp.einsum(
            "hgqk,khd->qhgd", dscore, key_tile, preferred_element_type=jnp.float32
        )
        dk_block = (
            jnp.einsum(
                "hgqk,qhgd->khd", dscore, query_head_rows, preferred_element_type=jnp.float32
            )
            * scale
        ).astype(jnp.bfloat16)
        dv_block = jnp.einsum(
            "hgqk,qhgd->khd", probs_b, gradient_heads, preferred_element_type=jnp.float32
        ).astype(jnp.bfloat16)
        paired = jnp.concatenate(
            (dk_block.reshape(row_count, width), dv_block.reshape(row_count, width)), axis=1
        )
        grad_buf = lax.dynamic_update_slice_in_dim(grad_buf, paired, shard * row_count, 0)
        return (dq_acc, grad_buf)

    blank_buffer = jnp.zeros((row_count * shard_list, 2 * width), jnp.bfloat16)
    dq_acc, grad_buf = lax.fori_loop(
        0,
        shard_list,
        gradient_update,
        (
            jnp.zeros((row_count, KEY_VALUE_HEADS, QUERY_PER_KV, HEAD_SIZE), jnp.float32),
            blank_buffer,
        ),
    )
    grad_queries = (dq_acc * scale).astype(jnp.bfloat16).reshape(row_count, QUERY_HEADS * HEAD_SIZE)
    summed = lax.psum_scatter(
        grad_buf.astype(jnp.float32).astype(jnp.bfloat16), "seq", scatter_dimension=0, tiled=True
    ).astype(jnp.float32)
    grad_keys = summed[:, :width].astype(jnp.bfloat16)
    grad_values = summed[:, width:].astype(jnp.bfloat16)
    grad_hidden = jnp.einsum(
        "kc,dc->kd", grad_values, full_weight, preferred_element_type=jnp.float32
    ).astype(jnp.bfloat16)
    partial_rows = lax.psum_scatter(
        jnp.einsum("kd,kc->dc", tokens, grad_values, preferred_element_type=jnp.float32).astype(
            jnp.bfloat16
        ),
        "dp",
        scatter_dimension=0,
        tiled=True,
    )
    grad_weight = lax.psum(partial_rows, "seq").astype(jnp.float32)
    return (
        attn_b.reshape(row_count, QUERY_HEADS * HEAD_SIZE)[None],
        grad_queries[None],
        grad_keys[None],
        grad_hidden[None],
        grad_weight,
    )


N_DP = 8
ROWS = 128
SHARD = 640
HALF = SHARD // 2
CHUNK = 128
WIDE = N_DP * HALF
CORE_KV = 256
SPARE = 16
CORE_Q = 1280
KEY_AT = WIDE
DOC_AT = KEY_AT + 512
QUERY_AT = DOC_AT + ROWS
COT_AT = QUERY_AT + CORE_Q
PACK = COT_AT + CORE_Q


def params(mib=32):
    return pltpu.CompilerParams(vmem_limit_bytes=mib * 1024 * 1024)


def cost(flops, nbytes):
    return pl.CostEstimate(flops=int(flops), bytes_accessed=int(nbytes), transcendentals=0)


def sds(shape, dtype=BF):
    return jax.ShapeDtypeStruct(shape, dtype)


def swap(x, axis, k):
    size = lax.axis_size(axis)
    return lax.ppermute(x, axis, [(i, i ^ k) for i in range(size)])


def after(x, *others):
    return lax.optimization_barrier((x, *others))[0]


def dot_tt(a, b):
    return lax.dot_general(a, b, (((0,), (0,)), ((), ())), preferred_element_type=F32)


def dot_nt(a, b):
    return lax.dot_general(a, b, (((1,), (1,)), ((), ())), preferred_element_type=F32)


def turn(x):
    return pltpu.roll(x.astype(F32), CHUNK // 2, 1).astype(x.dtype)


def first_half():
    return lax.broadcasted_iota(jnp.int32, (ROWS, CHUNK), 1) < CHUNK // 2


def pack_kernel(h, k, doc, w, q, g, send, keep, w0, h_in, k_in, doc_in, w_in, send_out, keep_out, sems):
    s = lax.axis_index("seq")
    r = lax.axis_index("dp")
    y, c = s // 2, s % 2
    cols = pl.ds(pl.multiple_of(c * CORE_KV, CORE_KV), CORE_KV)
    other = pl.ds(pl.multiple_of((1 - c) * CORE_Q, CORE_Q), CORE_Q)

    def copy(i, src, dst):
        made = pltpu.make_async_copy(src, dst, sems.at[i])
        made.start()
        return made

    w_copies = (
        copy(0, w.at[pl.ds(pl.multiple_of(y * 384, 128), 256), cols], w_in.at[pl.ds(0, 256)]),
        copy(1, w.at[pl.ds(pl.multiple_of(256 + y * 64, 64), 64), cols], w_in.at[pl.ds(256, 64)]),
    )
    blocks = [
        copy(10 + j, h.at[:, pl.ds(pl.multiple_of((r ^ j) * SHARD, 128), SHARD)], h_in.at[:, pl.ds(j * SHARD, SHARD)])
        for j in range(N_DP)
    ]
    small = copy(3, k, k_in), copy(4, doc, doc_in)
    heads = (
        copy(5, q.at[:, other], keep_out.at[:, pl.ds(QUERY_AT, CORE_Q)]),
        copy(6, g.at[:, other], keep_out.at[:, pl.ds(COT_AT, CORE_Q)]),
    )
    for made in w_copies:
        made.wait()
    outs = [copy(7, w_in, w0)]
    low = first_half()
    for p in range(N_DP // 2):
        blocks[2 * p].wait()
        blocks[2 * p + 1].wait()
        for which, (out, dst, part) in enumerate(((send_out, send, 1 - y), (keep_out, keep, y))):
            mids = []
            for i in range(2):
                base = (2 * p + i) * SHARD
                start = pl.multiple_of(base + part * 384, 128)
                out[:, p * SHARD + i * 256 : p * SHARD + (i + 1) * 256] = h_in[:, pl.ds(start, 256)]
                mid = h_in[:, base + 256 : base + 384]
                mids.append(jnp.where(part == i, mid, turn(mid)))
            out[:, p * SHARD + 512 : (p + 1) * SHARD] = jnp.where(low, mids[0], mids[1])
            span = pl.ds(p * SHARD, SHARD)
            outs.append(copy(18 + 4 * which + p, out.at[:, span], dst.at[:, span]))
    for made in small:
        made.wait()
    for out in (send_out, keep_out):
        out[:, KEY_AT:DOC_AT] = k_in[...]
        out[:, DOC_AT:QUERY_AT] = jnp.broadcast_to(doc_in[...].astype(F32), (ROWS, ROWS)).astype(BF)
    rest = pl.ds(KEY_AT, QUERY_AT - KEY_AT)
    outs.append(copy(8, send_out.at[:, rest], send.at[:, rest]))
    for made in heads:
        made.wait()
    rest = pl.ds(KEY_AT, PACK - KEY_AT)
    outs.append(copy(9, keep_out.at[:, rest], keep.at[:, rest]))
    for made in outs:
        made.wait()


def pack(h, k, doc, w, q, g):
    return pl.pallas_call(
        pack_kernel,
        out_shape=(sds((ROWS, QUERY_AT)), sds((ROWS, PACK)), sds((HALF, CORE_KV))),
        in_specs=[ANY] * 6,
        out_specs=(ANY,) * 3,
        scratch_shapes=[
            pltpu.VMEM((ROWS, N_DP * SHARD), BF),
            pltpu.VMEM((ROWS, 2 * CORE_KV), BF),
            pltpu.VMEM((1, ROWS), jnp.int32),
            pltpu.VMEM((HALF, CORE_KV), BF),
            pltpu.VMEM((ROWS, QUERY_AT), BF),
            pltpu.VMEM((ROWS, PACK), BF),
            pltpu.SemaphoreType.DMA((26,)),
        ],
        compiler_params=params(62),
        cost_estimate=cost(0, 3e6),
    )(h, k, doc, w, q, g)


def relay_kernel(p, w, own, ow):
    own[...] = p[:, 0:QUERY_AT]
    ow[...] = w[...]


def relay(p, w):
    return pl.pallas_call(
        relay_kernel,
        out_shape=(sds((ROWS, QUERY_AT)), sds((HALF, CORE_KV))),
        in_specs=[VM] * 2,
        out_specs=(VM,) * 2,
        compiler_params=params(),
        cost_estimate=cost(0, 4e6),
    )(p, w)


def values_kernel(h0, h1, h2, w0, w1, w2, w3, w4, w5, w6, w7, vp_ref, wp_ref):
    ws = (w0, w1, w2, w3, w4, w5, w6, w7)
    for p in range(N_DP // 2):
        a, b = ws[2 * p], ws[2 * p + 1]
        base = p * SHARD
        wp_ref[base : base + 256, :] = a[0:256, :]
        wp_ref[base + 256 : base + 512, :] = b[0:256, :]
        wp_ref[base + 512 : base + 576, :] = a[256:HALF, :]
        wp_ref[base + 576 : base + 640, :] = b[256:HALF, :]
    for t, h in enumerate((h0, h1, h2)):
        vp_ref[t * ROWS : (t + 1) * ROWS, :] = jnp.dot(
            h[:, 0:WIDE], wp_ref[...], preferred_element_type=F32
        ).astype(BF)


def partial_values(hs, ws):
    return pl.pallas_call(
        values_kernel,
        out_shape=(sds((3 * ROWS, CORE_KV)), sds((WIDE, CORE_KV))),
        in_specs=[VM] * 11,
        out_specs=(VM, VM),
        compiler_params=params(),
        cost_estimate=cost(2 * 384 * WIDE * 256, 6e6),
    )(*hs, *ws)


def last_values_kernel(vp, h3, wp, o0, o1):
    last = jnp.dot(h3[:, 0:WIDE], wp[...], preferred_element_type=F32).astype(BF)
    for i, o in enumerate((o0, o1)):
        cols = slice(i * HEAD_SIZE, (i + 1) * HEAD_SIZE)
        o[0 : 3 * ROWS, :] = vp[:, cols]
        o[3 * ROWS :, :] = last[:, cols]


def last_values(vp, h3, wp):
    return pl.pallas_call(
        last_values_kernel,
        out_shape=(sds((4 * ROWS, HEAD_SIZE)),) * 2,
        in_specs=[VM] * 3,
        out_specs=(VM,) * 2,
        compiler_params=params(),
        cost_estimate=cost(2 * 128 * WIDE * 256, 2e6),
    )(vp, h3, wp)


def scores_kernel(q0, p0, p1, p2, p3, e_ref, inv_ref, bias):
    s = lax.axis_index("seq")
    c = s % 2
    factor = HEAD_SIZE ** (-0.5)
    log2e = 1.4426950408889634
    ps = (p0, p1, p2, p3)
    rows = [p[0:16, DOC_AT:QUERY_AT][0:1, :].astype(F32) for p in ps]
    for t in range(4):
        key_doc = jnp.transpose(jnp.broadcast_to(rows[t], (ROWS, ROWS)))
        key_pos = (s ^ t) * ROWS + lax.broadcasted_iota(jnp.int32, (ROWS, ROWS), 0)
        for u in range(2):
            query_pos = (s ^ u) * ROWS + lax.broadcasted_iota(jnp.int32, (ROWS, ROWS), 1)
            allow = (key_pos <= query_pos) & (key_doc == jnp.broadcast_to(rows[u], (ROWS, ROWS)))
            bias[t * ROWS : (t + 1) * ROWS, u * ROWS : (u + 1) * ROWS] = jnp.where(allow, 0.0, -1e30)
    for kvh in range(2):
        cols = pl.ds(pl.multiple_of(KEY_AT + c * CORE_KV + kvh * HEAD_SIZE, HEAD_SIZE), HEAD_SIZE)
        key = jnp.concatenate([p[:, cols] for p in ps], axis=0)
        for i in range(QUERY_PER_KV):
            head = kvh * QUERY_PER_KV + i
            qcols = pl.ds(pl.multiple_of(c * CORE_Q + head * HEAD_SIZE, HEAD_SIZE), HEAD_SIZE)
            far = p1[:, QUERY_AT + head * HEAD_SIZE : QUERY_AT + (head + 1) * HEAD_SIZE]
            query = jnp.concatenate([q0[:, qcols], far], axis=0)
            st = dot_nt(key, query) * (factor * log2e) + bias[...]
            e = jnp.exp2(st - jnp.max(st, axis=0, keepdims=True))
            inv_ref[head * 8 : head * 8 + 8, :] = jnp.broadcast_to(
                1.0 / jnp.sum(e, axis=0, keepdims=True), (8, 2 * ROWS)
            )
            e_ref[head] = e.astype(BF)


def scores(q, ps):
    return pl.pallas_call(
        scores_kernel,
        out_shape=(sds((10, 4 * ROWS, 2 * ROWS)), sds((80, 2 * ROWS), F32)),
        in_specs=[VM] * 5,
        out_specs=(VM,) * 2,
        scratch_shapes=[pltpu.VMEM((4 * ROWS, 2 * ROWS), F32)],
        compiler_params=params(),
        cost_estimate=cost(2 * 10 * 256 * 512 * 128 * 8, 6e6),
    )(q, *ps)


def attend_head(kvh, e_ref, inv_ref, q0, g0, ps, vp, rv):
    c = lax.axis_index("seq") % 2
    factor = HEAD_SIZE ** (-0.5)
    p1 = ps[1]
    cols = pl.ds(pl.multiple_of(KEY_AT + c * CORE_KV + kvh * HEAD_SIZE, HEAD_SIZE), HEAD_SIZE)
    key = jnp.concatenate([p[:, cols] for p in ps], axis=0)
    far = rv[...].astype(F32)
    far = jnp.concatenate([far[2 * ROWS :], far[: 2 * ROWS]], axis=0)
    value = (vp[...].astype(F32) + far).astype(BF)
    dk = jnp.zeros((4 * ROWS, HEAD_SIZE), F32)
    dv = jnp.zeros((4 * ROWS, HEAD_SIZE), F32)
    outs = []
    for i in range(QUERY_PER_KV):
        head = kvh * QUERY_PER_KV + i
        qcols = pl.ds(pl.multiple_of(c * CORE_Q + head * HEAD_SIZE, HEAD_SIZE), HEAD_SIZE)
        low, high = head * HEAD_SIZE, (head + 1) * HEAD_SIZE
        query = jnp.concatenate([q0[:, qcols], p1[:, QUERY_AT + low : QUERY_AT + high]], axis=0)
        cot = jnp.concatenate([g0[:, qcols], p1[:, COT_AT + low : COT_AT + high]], axis=0)
        e = e_ref[head]
        inv = inv_ref[head * 8 : head * 8 + 8, :][0:1, :]
        out = jnp.transpose(dot_tt(value, e) * inv).astype(BF)
        probs = e.astype(F32) * inv
        term = probs * dot_nt(value, cot)
        delta = jnp.sum(term, axis=0, keepdims=True)
        ds = (term - probs * delta).astype(BF)
        dq = jnp.transpose(dot_tt(key, ds) * factor).astype(BF)
        outs.append((out, dq))
        dk = dk + jnp.dot(ds, query, preferred_element_type=F32)
        dv = dv + jnp.dot(probs.astype(BF), cot, preferred_element_type=F32)
    return outs, (dk * factor).astype(BF), dv.astype(BF)


def attention_first_kernel(e_ref, inv_ref, q0, g0, p0, p1, p2, p3, vp, rv, out, dk_ref, dv_ref):
    outs, dk, dv = attend_head(0, e_ref, inv_ref, q0, g0, (p0, p1, p2, p3), vp, rv)
    for i, (o, dq) in enumerate(outs):
        cols = slice(i * HEAD_SIZE, (i + 1) * HEAD_SIZE)
        out[0 : 2 * ROWS, cols] = o
        out[2 * ROWS :, cols] = dq
    dk_ref[...] = dk
    dv_ref[0 : 4 * ROWS, :] = dv
    dv_ref[4 * ROWS :, :] = jnp.zeros((SPARE, HEAD_SIZE), BF)


def attention_second_kernel(
    e_ref, inv_ref, q0, g0, p0, p1, p2, p3, vp, rv, first, first_dk,
    o0, dq0, dk0, dk2, swap_ref, dv_ref,
):
    outs, dk, dv = attend_head(1, e_ref, inv_ref, q0, g0, (p0, p1, p2, p3), vp, rv)
    half = QUERY_PER_KV * HEAD_SIZE
    o0[:, 0:half] = first[0:ROWS, :]
    swap_ref[:, 0:half] = first[ROWS : 2 * ROWS, :]
    dq0[:, 0:half] = first[2 * ROWS : 3 * ROWS, :]
    swap_ref[:, CORE_Q : CORE_Q + half] = first[3 * ROWS :, :]
    for i, (o, dq) in enumerate(outs):
        low, high = half + i * HEAD_SIZE, half + (i + 1) * HEAD_SIZE
        o0[:, low:high] = o[:ROWS]
        swap_ref[:, low:high] = o[ROWS:]
        dq0[:, low:high] = dq[:ROWS]
        swap_ref[:, CORE_Q + low : CORE_Q + high] = dq[ROWS:]
    for kvh, d in enumerate((first_dk[...], dk)):
        mine = slice(kvh * HEAD_SIZE, (kvh + 1) * HEAD_SIZE)
        dk0[:, mine] = d[:ROWS]
        dk2[:, mine] = d[2 * ROWS : 3 * ROWS]
        at = 2 * CORE_Q + kvh * HEAD_SIZE
        swap_ref[:, at : at + HEAD_SIZE] = d[ROWS : 2 * ROWS]
        swap_ref[:, at + CORE_KV : at + CORE_KV + HEAD_SIZE] = d[3 * ROWS :]
    dv_ref[...] = dv


def attention_first(*args):
    return pl.pallas_call(
        attention_first_kernel,
        out_shape=(
            sds((4 * ROWS, QUERY_PER_KV * HEAD_SIZE)), sds((4 * ROWS, HEAD_SIZE)),
            sds((4 * ROWS + SPARE, HEAD_SIZE)),
        ),
        in_specs=[VM] * 10,
        out_specs=(VM,) * 3,
        compiler_params=params(),
        cost_estimate=cost(5 * 10 * 256 * 512 * 128 * 4, 3e6),
    )(*args)


def attention_second(*args):
    return pl.pallas_call(
        attention_second_kernel,
        out_shape=(sds((ROWS, CORE_Q)),) * 2
        + (sds((ROWS, CORE_KV)),) * 2
        + (sds((ROWS, 2 * CORE_Q + 2 * CORE_KV)), sds((4 * ROWS, HEAD_SIZE))),
        in_specs=[VM] * 12,
        out_specs=(VM,) * 6,
        compiler_params=params(),
        cost_estimate=cost(5 * 10 * 256 * 512 * 128 * 4, 3e6),
    )(*args)


def weight_grad_pair(p, hs, gv, *outs):
    acc = jnp.zeros((CHUNK, CORE_KV), F32)
    for t, h in enumerate(hs):
        acc = acc + dot_tt(h[:, p * SHARD + 512 : (p + 1) * SHARD], gv[t * ROWS : (t + 1) * ROWS, :])
    middle = acc.astype(BF)
    for which, out, at in outs:
        acc = jnp.zeros((256, CORE_KV), F32)
        for t, h in enumerate(hs):
            first = p * SHARD + which * 256
            acc = acc + dot_tt(h[:, first : first + 256], gv[t * ROWS : (t + 1) * ROWS, :])
        out[at : at + 256, :] = acc.astype(BF)
        out[at + 256 : at + HALF, :] = middle[which * 64 : (which + 1) * 64]


def value_grad_kernel(dv0, dv1, rdv0, rdv1, gv, gv_keep, gv_send):
    for t in range(4):
        parts = []
        for dv, rdv in ((dv0, rdv0), (dv1, rdv1)):
            a = dv[t * ROWS : (t + 1) * ROWS, :].astype(F32)
            b = rdv[(t ^ 2) * ROWS : ((t ^ 2) + 1) * ROWS, :].astype(F32)
            parts.append(a + b)
        total = jnp.concatenate(parts, axis=1).astype(BF)
        gv[t * ROWS : (t + 1) * ROWS, :] = total
        half = (t // 2) * ROWS
        if t % 2 == 0:
            gv_keep[half : half + ROWS, :] = total
        else:
            gv_send[half : half + ROWS, :] = total


def value_grad(dvs, rdvs):
    return pl.pallas_call(
        value_grad_kernel,
        out_shape=(sds((4 * ROWS, CORE_KV)),) + (sds((2 * ROWS, CORE_KV)),) * 2,
        in_specs=[VM] * 4,
        out_specs=(VM,) * 3,
        compiler_params=params(),
        cost_estimate=cost(0, 1e6),
    )(*dvs, *rdvs)


def weight_grad_sent_kernel(gv, h0, h1, h2, h3, first, second):
    weight_grad_pair(2, (h0, h1, h2, h3), gv, (1, first, 0))
    first[HALF:, :] = jnp.zeros((SPARE, CORE_KV), BF)
    weight_grad_pair(3, (h0, h1, h2, h3), gv, (1, second, 0))


def weight_grad_sent(gv, hs):
    return pl.pallas_call(
        weight_grad_sent_kernel,
        out_shape=(sds((HALF + SPARE, CORE_KV)), sds((HALF, CORE_KV))),
        in_specs=[VM] * 5,
        out_specs=(VM,) * 2,
        compiler_params=params(),
        cost_estimate=cost(256 * WIDE * 256, 2e6),
    )(gv, *hs)


def weight_grad_kept_kernel(gv, h0, h1, h2, h3, first, second):
    weight_grad_pair(2, (h0, h1, h2, h3), gv, (0, first, 0))
    weight_grad_pair(3, (h0, h1, h2, h3), gv, (0, second, 0))


def weight_grad_kept(gv, hs):
    return pl.pallas_call(
        weight_grad_kept_kernel,
        out_shape=(sds((HALF, CORE_KV)),) * 2,
        in_specs=[VM] * 5,
        out_specs=(VM,) * 2,
        compiler_params=params(),
        cost_estimate=cost(256 * WIDE * 256, 2e6),
    )(gv, *hs)


def weight_grad_near_kernel(gv, h0, h1, h2, h3, send, own):
    for p, out in ((1, send), (0, own)):
        weight_grad_pair(p, (h0, h1, h2, h3), gv, (0, out, 0), (1, out, HALF))


def weight_grad_near(gv, hs):
    return pl.pallas_call(
        weight_grad_near_kernel,
        out_shape=(sds((2 * HALF, CORE_KV)),) * 2,
        in_specs=[VM] * 5,
        out_specs=(VM,) * 2,
        compiler_params=params(),
        cost_estimate=cost(512 * WIDE * 256, 4e6),
    )(gv, *hs)


def hidden_grad_kernel(gv, gvs, wp, wps, dk2, swapped, gh0, send_b):
    full = dot_nt(gv[...], wp[...]) + dot_nt(gvs[...], wps[...])
    full = full.astype(BF)
    gh0[...] = full[:ROWS]
    far = full[ROWS:]
    send_b[:, :WIDE] = far
    c = lax.axis_index("seq") % 2
    at = WIDE
    send_b[:, pl.ds(pl.multiple_of(at + c * CORE_KV, CORE_KV), CORE_KV)] = dk2[...]
    send_b[:, pl.ds(pl.multiple_of(at + (1 - c) * CORE_KV, CORE_KV), CORE_KV)] = swapped[
        :, 2 * CORE_Q + CORE_KV :
    ]


def hidden_grad(gv, gvs, wp, wps, dk2, swapped):
    return pl.pallas_call(
        hidden_grad_kernel,
        out_shape=(sds((ROWS, WIDE)), sds((ROWS, WIDE + 2 * CORE_KV))),
        in_specs=[VM] * 6,
        out_specs=(VM,) * 2,
        compiler_params=params(),
        cost_estimate=cost(2 * 256 * WIDE * 512, 6e6),
    )(gv, gvs, wp, wps, dk2, swapped)


def hidden_join_kernel(own_ref, far_ref, dk0, swapped, o_ref, dk_ref):
    s = lax.axis_index("seq")
    y, c = s // 2, s % 2
    r = lax.axis_index("dp")
    low = first_half()
    for p in range(N_DP // 2):
        for i in range(2):
            base = (r ^ (2 * p + i)) * SHARD
            src = slice(p * SHARD + i * 256, p * SHARD + (i + 1) * 256)
            o_ref[:, pl.ds(pl.multiple_of(base + y * 384, 128), 256)] = own_ref[:, src]
            o_ref[:, pl.ds(pl.multiple_of(base + (1 - y) * 384, 128), 256)] = far_ref[:, src]
        own = own_ref[:, p * SHARD + 512 : (p + 1) * SHARD]
        far = far_ref[:, p * SHARD + 512 : (p + 1) * SHARD]
        part0 = jnp.where(y == 0, own, far)
        part1 = jnp.where(y == 0, far, own)
        at0 = pl.multiple_of((r ^ (2 * p)) * SHARD + 256, 128)
        at1 = pl.multiple_of((r ^ (2 * p + 1)) * SHARD + 256, 128)
        o_ref[:, pl.ds(at0, CHUNK)] = jnp.where(low, part0, turn(part1))
        o_ref[:, pl.ds(at1, CHUNK)] = jnp.where(low, turn(part0), part1)
    for place, near in ((c, dk0[...]), (1 - c, swapped[:, 2 * CORE_Q : 2 * CORE_Q + CORE_KV])):
        far = far_ref[:, pl.ds(pl.multiple_of(WIDE + place * CORE_KV, CORE_KV), CORE_KV)]
        dk_ref[:, pl.ds(pl.multiple_of(place * CORE_KV, CORE_KV), CORE_KV)] = (
            near.astype(F32) + far.astype(F32)
        ).astype(BF)


def hidden_join(own, far, dk0, swapped):
    return pl.pallas_call(
        hidden_join_kernel,
        out_shape=(sds((ROWS, N_DP * SHARD)), sds((ROWS, 2 * CORE_KV))),
        in_specs=[VM] * 4,
        out_specs=(VM, VM),
        compiler_params=params(),
        cost_estimate=cost(0, 3e6),
    )(own, far, dk0, swapped)


def heads_join_kernel(o0, dq0, swapped, o_ref, dq_ref):
    c = lax.axis_index("seq") % 2
    near = pl.ds(pl.multiple_of(c * CORE_Q, CORE_Q), CORE_Q)
    far = pl.ds(pl.multiple_of((1 - c) * CORE_Q, CORE_Q), CORE_Q)
    o_ref[:, near] = o0[...]
    o_ref[:, far] = swapped[:, 0:CORE_Q]
    dq_ref[:, near] = dq0[...]
    dq_ref[:, far] = swapped[:, CORE_Q : 2 * CORE_Q]


def heads_join(o0, dq0, swapped):
    return pl.pallas_call(
        heads_join_kernel,
        out_shape=(sds((ROWS, 2 * CORE_Q)),) * 2,
        in_specs=[VM] * 3,
        out_specs=(VM,) * 2,
        compiler_params=params(),
        cost_estimate=cost(0, 4e6),
    )(o0, dq0, swapped)


def add_pair_kernel(a, b, o0, o1):
    total = (a[...].astype(F32) + b[...].astype(F32)).astype(BF)
    o0[...] = total[:HALF]
    o1[...] = total[HALF:]


def add_pair(a, b):
    return pl.pallas_call(
        add_pair_kernel,
        out_shape=(sds((HALF, CORE_KV)),) * 2,
        in_specs=[VM] * 2,
        out_specs=(VM,) * 2,
        compiler_params=params(),
        cost_estimate=cost(0, 1e6),
    )(a, b)


def add_one_kernel(a, b, o):
    o[0:HALF, :] = (a[...].astype(F32) + b[0:HALF, :].astype(F32)).astype(BF)
    if o.shape[0] > HALF:
        o[HALF:, :] = jnp.zeros((o.shape[0] - HALF, CORE_KV), BF)


def add_one(a, b, spare):
    return pl.pallas_call(
        add_one_kernel,
        out_shape=sds((HALF + spare, CORE_KV)),
        in_specs=[VM] * 2,
        out_specs=VM,
        compiler_params=params(),
        cost_estimate=cost(1e9, 1e3),
    )(a, b)


def add_two_kernel(a, b, o):
    o[...] = a[...].astype(F32) + b[...].astype(F32)


def add_two(a, b):
    return pl.pallas_call(
        add_two_kernel,
        out_shape=sds((HALF, CORE_KV), F32),
        in_specs=[VM] * 2,
        out_specs=VM,
        compiler_params=params(),
        cost_estimate=cost(3e9, 1e6),
    )(a, b)


def add_three_kernel(a, b, c, o):
    o[...] = (a[...] + (b[...].astype(F32) + c[...].astype(F32))).astype(BF)


def add_three(a, b, c):
    return pl.pallas_call(
        add_three_kernel,
        out_shape=sds((HALF, CORE_KV)),
        in_specs=[VM] * 3,
        out_specs=VM,
        compiler_params=params(),
        cost_estimate=cost(0, 1e6),
    )(a, b, c)


def weight_join_kernel(p0, p1, p2, p3, o_ref):
    s = lax.axis_index("seq")
    for t, p in enumerate((p0, p1, p2, p3)):
        y, c = (s ^ t) // 2, (s ^ t) % 2
        cols = pl.ds(pl.multiple_of(c * CORE_KV, CORE_KV), CORE_KV)
        o_ref[pl.ds(pl.multiple_of(y * 384, 128), 256), cols] = p[0:256, :].astype(F32)
        o_ref[pl.ds(pl.multiple_of(256 + y * 64, 64), 64), cols] = p[256:HALF, :].astype(F32)


def weight_join(ps):
    return pl.pallas_call(
        weight_join_kernel,
        out_shape=sds((SHARD, 2 * CORE_KV), F32),
        in_specs=[VM] * 4,
        out_specs=VM,
        compiler_params=params(),
        cost_estimate=cost(0, 2e6),
    )(*ps)


def paired_body(hidden, queries, keys, value_weight, doc_ids, cotangent):
    q, g = queries[0], cotangent[0]
    send, p0, w0 = pack(hidden[0], keys[0], doc_ids, value_weight, q, g)
    p2 = swap(send, "seq", 2)
    w6, w4 = swap(w0, "dp", 6), swap(w0, "dp", 4)
    p1 = swap(p0, "seq", 1)
    later = after(w0, p1)
    w1, w2 = swap(later, "dp", 1), swap(later, "dp", 2)
    w3 = swap(w1, "dp", 2)
    own, w0 = relay(after(p0, p1), w0)
    w7, w5 = swap(after(w6, own), "dp", 1), swap(after(w4, w2), "dp", 1)
    p3 = swap(after(p2, w1, w3, w5, w7), "seq", 1)
    ps = (own, p1, p2, p3)
    vp3, wp = partial_values((own, p1, p2), (w0, w1, w2, w3, w4, w5, w6, w7))
    vp0, vp1 = last_values(vp3, p3, wp)
    rv0, rv1 = swap(vp0, "seq", 2), swap(vp1, "seq", 2)
    e, inv = scores(after(q, vp0), ps)
    wps = swap(wp, "seq", 1)
    first, first_dk, dv0 = attention_first(e, inv, q, g, *ps, vp0, rv0)
    rdv0 = swap(dv0, "seq", 2)
    o0, dq0, dk0, dk2, swap_out, dv1 = attention_second(e, inv, q, g, *ps, vp1, rv1, first, first_dk)
    rdv1 = swap(dv1, "seq", 2)
    gv, gv_keep, gv_send = value_grad((dv0, dv1), (rdv0, rdv1))
    send5, send7 = weight_grad_sent(gv, ps)
    far5, far7 = swap(send5, "dp", 1), swap(send7, "dp", 1)
    own4, own6 = weight_grad_kept(after(gv, send5), ps)
    gvs = swap(after(gv_send, send5), "seq", 1)
    swapped = swap(after(swap_out, send5), "seq", 1)
    gh0, gh_send = hidden_grad(gv_keep, gvs, wp, wps, dk2, swapped)
    send_b, own_b = weight_grad_near(after(gv, gh0), ps)
    far_b = swap(send_b, "dp", 2)
    s4 = add_one(own4, far5, 0)
    t4 = swap(s4, "dp", 4)
    s6 = add_one(own6, after(far7, s4), 0)
    t6 = swap(s6, "dp", 6)
    t46 = add_two(t4, t6)
    s0, s1 = add_pair(own_b, far_b)
    gh_far = swap(gh_send, "seq", 2)
    attn_out, grad_queries = heads_join(o0, dq0, swapped)
    s1, attn_out, grad_queries = lax.optimization_barrier((s1, attn_out, grad_queries))
    t1 = swap(s1, "dp", 1)
    d0 = add_three(t46, s0, t1)
    d2 = swap(d0, "seq", 2)
    d1 = swap(d0, "seq", 1)
    grad_hidden, grad_keys = hidden_join(gh0, gh_far, dk0, swapped)
    d2, grad_hidden, grad_keys = lax.optimization_barrier((d2, grad_hidden, grad_keys))
    d3 = swap(d2, "seq", 1)
    grad_weight = weight_join((d0, d1, d2, d3))
    return attn_out[None], grad_queries[None], grad_keys[None], grad_hidden[None], grad_weight


def solution(mesh):
    in_specs = (
        P("dp", "seq", None),
        P("dp", "seq", None),
        P("dp", "seq", None),
        P("dp", None),
        P("dp", "seq"),
        P("dp", "seq", None),
    )
    out_specs = (
        P("dp", "seq", None),
        P("dp", "seq", None),
        P("dp", "seq", None),
        P("dp", "seq", None),
        P("dp", None),
    )
    paired = mesh.shape["dp"] == N_DP and mesh.shape["seq"] == 4
    return jax.shard_map(
        paired_body if paired else body, mesh=mesh, in_specs=in_specs, out_specs=out_specs, check_vma=False
    )
```
